32 devices in a mesh: groups: 2 (over x), expert: 16 (over z, y, core).
Axes of the slice: x: 2, y: 2, z: 4, core: 2. Of those that a mesh axis runs over, the one named last changes fastest.
Arguments:
- tokens_in: bfloat16 [4096, 1024], P(('groups', 'expert')), parts along dimension 0, may hold values from -6 to 6
- grad_out: bfloat16 [4096, 1024], P(('groups', 'expert')), parts along dimension 0, may hold values from -6 to 6
- gates: bfloat16 [4096, 8], P(('groups', 'expert')), parts along dimension 0, may hold values from 0.049804688 to 0.5
- expert_ids: int32 [4096, 8], P(('groups', 'expert')), parts along dimension 0, may hold values from 0 to 15, as said below
- replica_table: int32 [32], P('groups'), parts along dimension 0, may hold values from 0 to 15, as said below
- w_gate: bfloat16 [16, 1024, 384], P('expert'), may hold values from -0.1875 to 0.1875
- w_up: bfloat16 [16, 1024, 384], P('expert'), may hold values from -0.1875 to 0.1875
- w_down: bfloat16 [16, 384, 1024], P('expert'), may hold values from -0.3125 to 0.3125
Outputs:
- grad_tokens: bfloat16 [4096, 1024], P(('groups', 'expert')), parts along dimension 0
- grad_gates: bfloat16 [4096, 8], P(('groups', 'expert')), parts along dimension 0
- grad_w_gate: bfloat16 [32, 1024, 384], P(('groups', 'expert')), parts along dimension 0
- grad_w_up: bfloat16 [32, 1024, 384], P(('groups', 'expert')), parts along dimension 0
- grad_w_down: bfloat16 [32, 384, 1024], P(('groups', 'expert')), parts along dimension 0
The draws below stay inside these ranges and needn't reach their ends.
There are 2 independent parts, one for each index of `groups`. The reference program is written for one: setup_inputs(seed, part) draws one part's arguments, and reference() takes and returns one part's arrays. A program takes and returns all parts, laid end to end along the dimension named above; an argument that names none is the same for every part. Nothing has to cross between parts.
Inputs may be any that keep to these rules, and one draw needn't show every extreme that they name: `expert_ids`: each row names 8 different experts. `replica_table`: entry d is the expert whose weights device d holds in its replica slot.
All inputs are finite; a program needn't handle non-finite values.
Results may differ from the reference program's by a relative error of at most 0.0057.
Values may be sent and summed in bfloat16 or wider, within the bound.
No kernel may reach another device: no remote copies, remote signals or barrier semaphores. Data moves between devices by JAX's collectives and lax.ppermute only.
A program may use at most 128 MiB of HBM per device.

```python
import math
import jax
import jax.numpy as jnp
from jax import lax

D = 1024
FF = 384
TOP = 8
TOK_DEV = 128
HOME_CAP = 80
REP_CAP = 32
SPECIALIST_COUNT = 16
TOKENS = 2048
N_EXPERT = 16


def routing_draw(key):
    order_key = jax.random.fold_in(key, 7001)
    score_key = jax.random.fold_in(key, 7002)
    table_key = jax.random.fold_in(key, 7003)
    uplift_seed_handle = jax.random.fold_in(key, 7004)
    popular = jax.random.permutation(order_key, SPECIALIST_COUNT).astype(jnp.int32)
    specialist_sorted_order = jnp.argsort(popular, stable=True).astype(jnp.int32)
    heaviest_loaded_specialist = max(SPECIALIST_COUNT // 8, 2)
    duplicate_uplift = jax.random.randint(uplift_seed_handle, (SPECIALIST_COUNT,), 0, 16384, dtype=jnp.int32)
    logit_increment = jnp.where(specialist_sorted_order < heaviest_loaded_specialist, 147456, 0).astype(jnp.int32) + duplicate_uplift
    drawn_router_logits = jax.random.randint(score_key, (TOKENS, SPECIALIST_COUNT), 0, 1048576, dtype=jnp.int32)
    specialist_logits = (drawn_router_logits + logit_increment[None, :]) * SPECIALIST_COUNT + jnp.arange(SPECIALIST_COUNT, dtype=jnp.int32)[None, :]
    chosen_ids = lax.top_k(specialist_logits, TOP)[1].astype(jnp.int32)
    shuffled = jax.random.permutation(table_key, SPECIALIST_COUNT).astype(jnp.int32) % heaviest_loaded_specialist
    placement = jnp.take(popular, shuffled).astype(jnp.int32)
    return (chosen_ids, placement)


def draw_expert_ids(key, part):
    return routing_draw(key)[0]


def draw_replica_table(key, part):
    return routing_draw(key)[1]


def level_of(stream_key, shape, split, low, top_value):
    loudness = 1.0
    for axis_at, shards_of in split:
        draws = jax.random.uniform(jax.random.fold_in(jax.random.fold_in(stream_key, 6), axis_at), (shards_of,), jnp.float32, low / len(split), top_value / len(split))
        loudness = loudness * jnp.repeat(jnp.exp(draws), shape[axis_at] // shards_of).reshape((-1,) + (1,) * (len(shape) - 1 - axis_at))
    return loudness


def bell_draw(key, extent, width, limit, shards=(), held_as=jnp.bfloat16):
    level = level_of(key, extent, shards, -0.22, 0.18) if shards else 1.0
    entries = jax.random.normal(key, extent, jnp.float32) * width * level
    return jnp.minimum(jnp.maximum(entries, -limit), limit).astype(held_as)


def setup_inputs(seed: int = 0, part: int = 0) -> dict:
    key_of = jax.random.split(jax.random.key(seed), 9)
    part_splits = jax.random.split(jax.random.fold_in(key_of[8], part), 9)
    tokens_in = bell_draw(part_splits[0], (TOKENS, D), 1.0, 6.0, ((0, 16),))
    grad_out = bell_draw(part_splits[1], (TOKENS, D), 1.0, 6.0, ((0, 16),))
    gates = jnp.clip(jnp.exp(math.log(0.5) - 2.306499 * jax.random.uniform(part_splits[2], (TOKENS, TOP), jnp.float32) ** level_of(part_splits[2], (TOKENS, TOP), ((0, 16),), -0.2, 0.2)), 0.049804688, 0.5).astype(jnp.bfloat16)
    expert_ids = draw_expert_ids(jax.random.fold_in(jax.random.fold_in(key_of[8], part), 71), part)
    replica_table = draw_replica_table(jax.random.fold_in(jax.random.fold_in(key_of[8], part), 71), part)
    w_gate = bell_draw(key_of[5], (SPECIALIST_COUNT, D, FF), D ** -0.5, 0.1875, ((0, 16),))
    w_up = bell_draw(key_of[6], (SPECIALIST_COUNT, D, FF), D ** -0.5, 0.1875, ((0, 16),))
    w_down = bell_draw(key_of[7], (SPECIALIST_COUNT, FF, D), FF ** -0.5, 0.3125, ((0, 16),))
    return {"tokens_in": tokens_in, "grad_out": grad_out, "gates": gates, "expert_ids": expert_ids, "replica_table": replica_table, "w_gate": w_gate, "w_up": w_up, "w_down": w_down}


contract_rows = (((0,), (0,)), ((), ()))
contract_cols = (((1,), (1,)), ((), ()))


def plan_routes(row_ids, replica_table, source, devices, home_cap, rep_cap):
    flat_ids = row_ids.reshape(-1).astype(jnp.int32)
    expert_axis = jnp.arange(devices, dtype=jnp.int32)
    hosted = (replica_table[None, :] == expert_axis[:, None]).astype(jnp.int32)
    copies = 1 + jnp.sum(hosted, axis=1)
    replica_order = jnp.cumsum(hosted, axis=1) - hosted
    chosen = (flat_ids[:, None] == expert_axis[None, :]).astype(jnp.int32)
    row_rank = jnp.sum((jnp.cumsum(chosen, axis=0) - chosen) * chosen, axis=1)
    row_copies = jnp.take(copies, flat_ids, axis=0)
    copy_index = (row_rank + source) % row_copies
    at_home = copy_index == 0
    matched = (jnp.take(hosted, flat_ids, axis=0) == 1) & (jnp.take(replica_order, flat_ids, axis=0) == (copy_index - 1)[:, None])
    replica_device = jnp.sum(jnp.where(matched, expert_axis[None, :], 0), axis=1)
    target = jnp.where(at_home, flat_ids, replica_device)
    bucket = target * 2 + jnp.where(at_home, 0, 1)
    bucket_hot = (bucket[:, None] == jnp.arange(2 * devices, dtype=jnp.int32)[None, :]).astype(jnp.int32)
    position = jnp.sum((jnp.cumsum(bucket_hot, axis=0) - bucket_hot) * bucket_hot, axis=1)
    slot_width = home_cap + rep_cap
    kept_rows = jnp.where(at_home, position < home_cap, position < rep_cap)
    slot_index = target * slot_width + jnp.where(at_home, position, home_cap + position)
    slot_index = jnp.where(kept_rows, slot_index, devices * slot_width)
    return slot_index.astype(jnp.int32), kept_rows


def expert_grads(rows_x, rows_dy, rows_gate, gate_w, up_w, down_w):
    pre_gate = jnp.dot(rows_x, gate_w, preferred_element_type=jnp.float32)
    pre_up = jnp.dot(rows_x, up_w, preferred_element_type=jnp.float32)
    sigmoid_gate = jax.nn.sigmoid(pre_gate)
    activated = pre_gate * sigmoid_gate
    product = activated * pre_up
    hidden = product.astype(jnp.bfloat16)
    back_hidden = lax.dot_general(rows_dy, down_w, contract_cols, preferred_element_type=jnp.float32)
    gate_grad = jnp.sum(lax.optimization_barrier(hidden).astype(jnp.float32) * back_hidden, axis=1).astype(jnp.bfloat16)
    gate_value = rows_gate.astype(jnp.float32)[:, None]
    weighted = (gate_value * product).astype(jnp.bfloat16)
    down_grad = lax.dot_general(weighted, rows_dy, contract_rows, preferred_element_type=jnp.float32)
    scaled = gate_value * back_hidden
    grad_pre_gate = (scaled * pre_up * sigmoid_gate * (1.0 + pre_gate * (1.0 - sigmoid_gate))).astype(jnp.bfloat16)
    grad_pre_up = (scaled * activated).astype(jnp.bfloat16)
    gate_w_grad = lax.dot_general(rows_x, grad_pre_gate, contract_rows, preferred_element_type=jnp.float32)
    up_w_grad = lax.dot_general(rows_x, grad_pre_up, contract_rows, preferred_element_type=jnp.float32)
    input_grad = lax.dot_general(grad_pre_gate, gate_w, contract_cols, preferred_element_type=jnp.float32)
    input_grad = input_grad + lax.dot_general(grad_pre_up, up_w, contract_cols, preferred_element_type=jnp.float32)
    return input_grad.astype(jnp.bfloat16), gate_grad, gate_w_grad, up_w_grad, down_grad


def reference(tokens_in, grad_out, gates, expert_ids, replica_table, w_gate, w_up, w_down):
    devices = N_EXPERT
    slot_width = HOME_CAP + REP_CAP
    model_width = D
    hidden_units = FF
    routed = TOK_DEV * TOP
    per_source = expert_ids.reshape(devices, routed)
    sources = jnp.arange(devices, dtype=jnp.int32)
    slot_index, kept_rows = jax.vmap(lambda row_ids, src_index: plan_routes(row_ids, replica_table, src_index, devices, HOME_CAP, REP_CAP))(per_source, sources)

    def fill_slots(slot_rows):
        empty = jnp.full((devices * slot_width + 1,), -1, jnp.int32)
        return empty.at[slot_rows].set(jnp.arange(routed, dtype=jnp.int32))[:-1]

    slot_fill = jax.vmap(fill_slots)(slot_index)
    zero_bf = jnp.zeros((), jnp.bfloat16)

    def visit(state_carry, target):
        acc_tokens, acc_gates, replica_gate, replica_up, replica_down = state_carry
        taken_slots = lax.dynamic_slice_in_dim(slot_fill, (target * slot_width).astype(jnp.int32), slot_width, 1)
        filled = taken_slots >= 0
        clipped = jnp.maximum(taken_slots, 0)
        token_row = (sources[:, None] * TOK_DEV + clipped // TOP).astype(jnp.int32)
        top_index = (clipped % TOP).astype(jnp.int32)
        rows_x = jnp.where(filled[..., None], tokens_in[token_row], zero_bf)
        rows_dy = jnp.where(filled[..., None], grad_out[token_row], zero_bf)
        rows_gate = jnp.where(filled, gates[token_row, top_index], zero_bf)
        hosted = replica_table[target]
        home_grads = expert_grads(rows_x[:, :HOME_CAP].reshape(-1, model_width), rows_dy[:, :HOME_CAP].reshape(-1, model_width),
                                  rows_gate[:, :HOME_CAP].reshape(-1), w_gate[target], w_up[target], w_down[target])
        extra_grads = expert_grads(rows_x[:, HOME_CAP:].reshape(-1, model_width), rows_dy[:, HOME_CAP:].reshape(-1, model_width),
                                   rows_gate[:, HOME_CAP:].reshape(-1), w_gate[hosted], w_up[hosted], w_down[hosted])
        back_x = jnp.concatenate([home_grads[0].reshape(devices, HOME_CAP, model_width),
                                  extra_grads[0].reshape(devices, REP_CAP, model_width)], axis=1)
        back_gate = jnp.concatenate([home_grads[1].reshape(devices, HOME_CAP), extra_grads[1].reshape(devices, REP_CAP)], axis=1)
        masked_x = jnp.where(filled[..., None], back_x.astype(jnp.float32), jnp.float32(0.0))
        acc_tokens = acc_tokens.at[token_row.reshape(-1)].add(masked_x.reshape(-1, model_width))
        masked_gate = jnp.where(filled, back_gate.astype(jnp.float32), jnp.float32(0.0))
        acc_gates = acc_gates.at[token_row.reshape(-1), top_index.reshape(-1)].add(masked_gate.reshape(-1))
        replica_gate = replica_gate.at[hosted].add(lax.optimization_barrier(extra_grads[2].astype(jnp.bfloat16)).astype(jnp.float32))
        replica_up = replica_up.at[hosted].add(lax.optimization_barrier(extra_grads[3].astype(jnp.bfloat16)).astype(jnp.float32))
        replica_down = replica_down.at[hosted].add(lax.optimization_barrier(extra_grads[4].astype(jnp.bfloat16)).astype(jnp.float32))
        return (acc_tokens, acc_gates, replica_gate, replica_up, replica_down), (home_grads[2], home_grads[3], home_grads[4])

    initial = (jnp.zeros((TOKENS, model_width), jnp.float32), jnp.zeros((TOKENS, TOP), jnp.float32),
               jnp.zeros((devices, model_width, hidden_units), jnp.float32),
               jnp.zeros((devices, model_width, hidden_units), jnp.float32),
               jnp.zeros((devices, hidden_units, model_width), jnp.float32))
    final_state, home_parts = lax.scan(visit, initial, sources)
    acc_tokens, acc_gates, replica_gate, replica_up, replica_down = final_state
    grad_tokens = acc_tokens.astype(jnp.bfloat16)
    grad_gates = acc_gates.astype(jnp.bfloat16)
    grad_w_gate = (home_parts[0] + lax.optimization_barrier(replica_gate.astype(jnp.bfloat16)).astype(jnp.float32)).astype(jnp.bfloat16)
    grad_w_up = (home_parts[1] + lax.optimization_barrier(replica_up.astype(jnp.bfloat16)).astype(jnp.float32)).astype(jnp.bfloat16)
    grad_w_down = (home_parts[2] + lax.optimization_barrier(replica_down.astype(jnp.bfloat16)).astype(jnp.float32)).astype(jnp.bfloat16)
    return (grad_tokens, grad_gates, grad_w_gate, grad_w_up, grad_w_down)
```

```python
import functools
import math

import jax
import jax.numpy as jnp
from jax import lax
from jax.experimental import pallas as pl
from jax.experimental.pallas import tpu as pltpu
from jax.sharding import PartitionSpec as P

TOP = 8
CORES = 2
LANES = 128
ROW_BLOCK = 256
W_ROWS = 1024

f32 = jnp.float32
bf16 = jnp.bfloat16
nt = (((1,), (1,)), ((), ()))
tn = (((0,), (0,)), ((), ()))
VMEM = pl.BlockSpec(memory_space=pltpu.VMEM)
SMEM = pl.BlockSpec(memory_space=pltpu.SMEM)
ANY = pl.BlockSpec(memory_space=pl.ANY)


def params(mib):
    return pltpu.CompilerParams(vmem_limit_bytes=mib * 1024 * 1024)


def lane_iota(rows, lanes):
    return lax.broadcasted_iota(jnp.int32, (rows, lanes), 1)


def plan_kernel(devices, home_cap, rep_cap, table, ids, gates, dy, dyg, kept_out):
    tokens, width = dy.shape
    lanes = dyg.shape[1] - width
    dyg[:, :width] = dy[...]
    lane = lane_iota(tokens, lanes)
    lane_row = lane_iota(8, lanes)

    def count(d, total):
        return total + jnp.where(lane_row == table[d], 1.0, 0.0)

    copies = lax.fori_loop(0, devices, count, jnp.ones((8, lanes), f32))[:1]
    named = jnp.zeros((tokens, lanes), f32)
    weight = jnp.zeros((tokens, lanes), f32)
    for k in range(TOP):
        hit = lane == ids[:, k : k + 1]
        named = jnp.where(hit, 1.0, named)
        weight = jnp.where(hit, gates[:, k : k + 1].astype(f32), weight)
    below = lax.broadcasted_iota(jnp.int32, (tokens, tokens), 0) > lane_iota(tokens, tokens)
    rank = jnp.dot(
        jnp.where(below, 1.0, 0.0).astype(bf16), named.astype(bf16), preferred_element_type=f32
    )
    turn = rank + lax.axis_index("expert").astype(f32)
    at_home = turn == copies * jnp.floor(turn / copies + 0.5)
    cap = jnp.where(at_home, float(home_cap), float(rep_cap))
    kept = jnp.where((named > 0.0) & (rank < cap * copies), 1.0, 0.0)
    dyg[:, width:] = (weight * kept).astype(bf16)
    kept_out[...] = kept


def plan(table, ids, gates, dy, devices, lanes):
    tokens, width = dy.shape
    home_cap = max(2, 5 * tokens * TOP // (4 * devices))
    rep_cap = max(2, tokens * TOP // (2 * devices))
    return pl.pallas_call(
        functools.partial(plan_kernel, devices, home_cap, rep_cap),
        out_shape=(
            jax.ShapeDtypeStruct((tokens, width + lanes), bf16),
            jax.ShapeDtypeStruct((tokens, lanes), f32),
        ),
        in_specs=[SMEM, VMEM, VMEM, VMEM],
        out_specs=(VMEM, VMEM),
        compiler_params=params(16),
        name="plan",
    )(table, ids, gates, dy)


def rows_kernel(slots, *refs):
    x_in, dyg_in = refs[:slots], refs[slots : 2 * slots]
    weights = refs[2 * slots : 2 * slots + 6]
    dxg, act = refs[2 * slots + 6 : 3 * slots + 6], refs[3 * slots + 6]
    x, dyg, w_gu, w_dn, sem = refs[3 * slots + 7 :]
    tokens, width = x_in[0].shape
    hidden = weights[2].shape[0]
    lanes = dyg.shape[1] - width
    copies = []

    def fetch(src, dst):
        copies.append(pltpu.make_async_copy(src, dst, sem.at[len(copies)]))
        copies[-1].start()
        return copies[-1]

    def fetch_weights(j):
        up = [
            fetch(weights[3 * j], w_gu.at[j, :, pl.ds(0, hidden)]),
            fetch(weights[3 * j + 1], w_gu.at[j, :, pl.ds(hidden, hidden)]),
        ]
        return up, [fetch(weights[3 * j + 2], w_dn.at[j])]

    got_x = [fetch(x_in[i], x.at[pl.ds(i * tokens, tokens)]) for i in range(slots)]
    own = fetch_weights(0)
    got_dy = [fetch(dyg_in[i], dyg.at[pl.ds(i * tokens, tokens)]) for i in range(slots)]
    sibling = fetch_weights(1)
    for c in got_x + own[0]:
        c.wait()

    rows = slots * tokens
    block = math.gcd(rows, max(ROW_BLOCK, tokens))
    me = lax.axis_index("expert")
    lane = lane_iota(block, lanes)

    def expert(j, at, after_up):
        here = pl.ds(at, block)
        pre = jnp.dot(x[here, :], w_gu[j], preferred_element_type=f32)
        after_up()
        back = lax.dot_general(dyg[here, :width], w_dn[j], nt, preferred_element_type=f32)
        column = lane == (me if j == 0 else me ^ 1)
        gate = jnp.sum(
            jnp.where(column, dyg[here, width:].astype(f32), 0.0), axis=1, keepdims=True
        )
        a, b = pre[:, :hidden], pre[:, hidden:]
        sig = jax.nn.sigmoid(a)
        silu = a * sig
        h = silu * b
        gg = jnp.sum(h.astype(bf16).astype(f32) * back, axis=1, keepdims=True)
        scaled = gate * back
        da = (scaled * b * sig * (1.0 + a * (1.0 - sig))).astype(bf16)
        db = (scaled * silu).astype(bf16)
        grads = jnp.concatenate([da, db], axis=1)
        first = j * 3 * hidden
        act[here, first : first + 2 * hidden] = grads
        act[here, first + 2 * hidden : first + 3 * hidden] = (gate * h).astype(bf16)
        dx = lax.dot_general(grads, w_gu[j], nt, preferred_element_type=f32)
        return dx, jnp.where(column, gg, 0.0)

    def wait_all(group):
        for c in group:
            c.wait()

    for at in range(0, rows, block):
        first = at == 0
        dx0, gg0 = expert(0, at, lambda: wait_all(got_dy + own[1]) if first else None)
        if first:
            wait_all(sibling[0] + sibling[1])
        dx1, gg1 = expert(1, at, lambda: None)
        dx = (dx0 + dx1).astype(bf16)
        gg = (gg0 + gg1).astype(bf16)
        for i in range(block // tokens):
            out = dxg[at // tokens + i]
            part = slice(i * tokens, (i + 1) * tokens)
            out[:, :width] = dx[part]
            out[:, width:] = gg[part]


def rows_grads(xs, dygs, weights):
    slots = len(xs)
    tokens, width = xs[0].shape
    full = dygs[0].shape[1]
    hidden = weights[2].shape[0]
    rows = slots * tokens
    flops = 2 * rows * 2 * 5 * width * hidden
    moved = 4 * rows * (width + full) + 12 * width * hidden + 4 * rows * full + 12 * rows * hidden
    return pl.pallas_call(
        functools.partial(rows_kernel, slots),
        out_shape=tuple(jax.ShapeDtypeStruct((tokens, full), bf16) for _ in xs)
        + (jax.ShapeDtypeStruct((rows, 6 * hidden), bf16),),
        in_specs=[ANY] * (2 * slots + 6),
        out_specs=(VMEM,) * (slots + 1),
        scratch_shapes=[
            pltpu.VMEM((rows, width), bf16),
            pltpu.VMEM((rows, full), bf16),
            pltpu.VMEM((2, width, 2 * hidden), bf16),
            pltpu.VMEM((2, hidden, width), bf16),
            pltpu.SemaphoreType.DMA((2 * slots + 6,)),
        ],
        compiler_params=params(40),
        cost_estimate=pl.CostEstimate(
            flops=flops, bytes_accessed=moved, transcendentals=2 * rows * hidden
        ),
        name="rows_grads",
    )(*xs, *dygs, *weights)


def weights_kernel(j, slots, steps, extra, *refs):
    x_in, dyg_in, act_in = refs[:slots], refs[slots : 2 * slots], refs[2 * slots : 2 * slots + steps]
    refs = refs[2 * slots + steps :]
    more, refs = refs[:extra], refs[extra:]
    gate_out, up_out, down_out = refs[:3]
    x, dy, act, sem = refs[3:]
    tokens, width = x_in[0].shape
    hidden = act.shape[1] // 3
    step_rows = act_in[0].shape[0]
    copies = []

    def fetch(src, dst):
        copies.append(pltpu.make_async_copy(src, dst, sem.at[len(copies)]))
        copies[-1].start()

    for i in range(steps):
        fetch(
            act_in[i].at[:, pl.ds(j * 3 * hidden, 3 * hidden)],
            act.at[pl.ds(i * step_rows, step_rows)],
        )
    for i in range(slots):
        fetch(x_in[i], x.at[pl.ds(i * tokens, tokens)])
    for i in range(slots):
        fetch(dyg_in[i].at[:, pl.ds(0, width)], dy.at[pl.ds(i * tokens, tokens)])
    for c in copies[: steps + slots]:
        c.wait()

    def put(out, here, value, k):
        if extra:
            value = value + more[k][here].astype(f32)
        if len(out.shape) == 3:
            out[0, here[0], here[1]] = value.astype(out.dtype)
        else:
            out[here[0], here[1]] = value.astype(out.dtype)

    part = math.gcd(width, 256)
    everything = slice(None)
    for m in range(0, width, part):
        here = (slice(m, m + part), everything)
        both = lax.dot_general(
            x[:, m : m + part], act[:, : 2 * hidden], tn, preferred_element_type=f32
        )
        put(gate_out, here, both[:, :hidden], 0)
        put(up_out, here, both[:, hidden:], 1)
    for c in copies[steps + slots :]:
        c.wait()
    part = math.gcd(hidden, 128)
    for m in range(0, hidden, part):
        here = (slice(m, m + part), everything)
        value = lax.dot_general(
            act[:, 2 * hidden + m : 2 * hidden + m + part], dy[...], tn, preferred_element_type=f32
        )
        put(down_out, here, value, 2)


def weights_grads(j, xs, dygs, acts, dtype, more=()):
    slots, steps = len(xs), len(acts)
    tokens, width = xs[0].shape
    hidden = acts[0].shape[1] // 6
    rows = slots * tokens
    lead = (1,) if more else ()
    return pl.pallas_call(
        functools.partial(weights_kernel, j, slots, steps, len(more)),
        out_shape=(
            jax.ShapeDtypeStruct(lead + (width, hidden), dtype),
            jax.ShapeDtypeStruct(lead + (width, hidden), dtype),
            jax.ShapeDtypeStruct(lead + (hidden, width), dtype),
        ),
        in_specs=[ANY] * (2 * slots + steps) + [VMEM] * len(more),
        out_specs=(VMEM,) * 3,
        scratch_shapes=[
            pltpu.VMEM((rows, width), bf16),
            pltpu.VMEM((rows, width), bf16),
            pltpu.VMEM((rows, 3 * hidden), bf16),
            pltpu.SemaphoreType.DMA((2 * slots + steps,)),
        ],
        compiler_params=params(40),
        cost_estimate=pl.CostEstimate(
            flops=6 * rows * width * hidden,
            bytes_accessed=rows * (4 * width + 6 * hidden) + 6 * width * hidden,
            transcendentals=0,
        ),
        name="weights_grads",
    )(*xs, *dygs, *acts, *more)


def finish_kernel(parts, ids, kept, *refs):
    pieces, (tokens_out, gates_out) = refs[:parts], refs[parts:]
    tokens, width = tokens_out.shape
    lanes = kept.shape[1]
    total = pieces[0][:, :width].astype(f32)
    gg = pieces[0][:, width:].astype(f32)
    for p in pieces[1:]:
        total = total + p[:, :width].astype(f32)
        gg = gg + p[:, width:].astype(f32)
    tokens_out[...] = total.astype(bf16)
    gg = gg * kept[...]
    lane = lane_iota(tokens, lanes)
    place = lane_iota(tokens, TOP)
    out = jnp.zeros((tokens, TOP), f32)
    for k in range(TOP):
        value = jnp.sum(jnp.where(lane == ids[:, k : k + 1], gg, 0.0), axis=1, keepdims=True)
        out = jnp.where(place == k, value, out)
    gates_out[...] = out.astype(bf16)


def finish(ids, kept, pieces, width):
    tokens = ids.shape[0]
    return pl.pallas_call(
        functools.partial(finish_kernel, len(pieces)),
        out_shape=(
            jax.ShapeDtypeStruct((tokens, width), bf16),
            jax.ShapeDtypeStruct((tokens, TOP), bf16),
        ),
        in_specs=[VMEM] * (2 + len(pieces)),
        out_specs=(VMEM, VMEM),
        compiler_params=params(16),
        name="finish",
    )(ids, kept, *pieces)


def add(*terms):
    total = terms[0].astype(f32)
    for t in terms[1:]:
        total = total + t.astype(f32)
    return total.astype(bf16)


def on_device(tokens_in, grad_out, gates, expert_ids, replica_table, w_gate, w_up, w_down):
    devices = lax.axis_size("expert")
    tokens, width = tokens_in.shape
    lanes = -(-devices // LANES) * LANES
    chips = devices // CORES
    inner = 2 ** (int(math.log2(chips)) // 2)
    outer = chips // inner

    def moved(i, dz, dy):
        core, chip = i % CORES, i // CORES
        z, y = chip // inner, chip % inner
        return (((z + dz) % outer) * inner + (y + dy) % inner) * CORES + core

    def send_z(v):
        return lax.ppermute(v, "expert", [(i, moved(i, 1, 0)) for i in range(devices)])

    def send_y(v):
        return lax.ppermute(v, "expert", [(i, moved(i, 0, 1)) for i in range(devices)])

    def send_core(v):
        return lax.ppermute(v, "expert", [(i, i ^ 1) for i in range(devices)])

    dyg, kept = plan(replica_table, expert_ids, gates, grad_out, devices, lanes)
    own = (w_gate[0], w_up[0], w_down[0])
    weights = own + tuple(send_core(w) for w in own)

    xs = [[tokens_in]]
    dygs = [[dyg]]
    for z in range(outer):
        if z:
            xs.append([send_z(xs[z - 1][0])])
            dygs.append([send_z(dygs[z - 1][0])])
        for y in range(1, inner):
            xs[z].append(send_y(xs[z][y - 1]))
            if z > 0 and z == outer - 1 and y == inner - 1:
                dygs[z].append(send_z(dygs[z - 1][y]))
            else:
                dygs[z].append(send_y(dygs[z][y - 1]))

    per = max(1, W_ROWS // (inner * tokens))
    groups = [range(z, min(outer, z + per)) for z in range(0, outer, per)]
    sums = [None, None]

    def partial(j, group, dtype, more=()):
        return weights_grads(
            j,
            [x for z in group for x in xs[z]],
            [d for z in group for d in dygs[z]],
            [acts[z] for z in group],
            dtype,
            more,
        )

    dxs, acts, across = [], [], []
    for z in range(outer):
        *dx, act = rows_grads(xs[z], dygs[z], weights)
        dxs.append(dx)
        acts.append(act)
        if inner > 1:
            total = dx[1]
            for y in range(2, inner):
                total = add(send_y(total), dx[y])
            across.append([send_y(total)])
        else:
            across.append([])
        if len(groups) > 1 and z == groups[z // per][-1]:
            for j in range(2):
                value = partial(j, groups[z // per], f32)
                sums[j] = value if z < per else [t + v for t, v in zip(sums[j], value)]
            if z + 1 < outer:
                sums, xs[z + 1] = lax.optimization_barrier((sums, xs[z + 1]))

    if len(groups) == 1:
        other = [send_core(v) for v in partial(1, groups[0], bf16)]
        grad_w = partial(0, groups[0], bf16, other)
    else:
        other = [send_core(v.astype(bf16)) for v in sums[1]]
        grad_w = [(v + o.astype(f32)).astype(bf16)[None] for v, o in zip(sums[0], other)]

    pieces = [dxs[0][0], *across[0]]
    if outer > 1:
        total = add(dxs[1][0], *across[1])
        for z in range(2, outer):
            total = add(send_z(total), dxs[z][0], *across[z])
        pieces.append(send_z(total))
    grad_tokens, grad_gates = finish(expert_ids, kept, pieces, width)
    return (grad_tokens, grad_gates, *grad_w)


def solution(mesh):
    both = ("groups", "expert")
    return jax.shard_map(
        on_device,
        mesh=mesh,
        in_specs=(
            P(both, None),
            P(both, None),
            P(both, None),
            P(both, None),
            P("groups"),
            P("expert", None, None),
            P("expert", None, None),
            P("expert", None, None),
        ),
        out_specs=(
            P(both, None),
            P(both, None),
            P(both, None, None),
            P(both, None, None),
            P(both, None, None),
        ),
        check_vma=False,
    )
```

```python
import functools
import math

import jax
import jax.numpy as jnp
from jax import lax
from jax.experimental import pallas as pl
from jax.experimental.pallas import tpu as pltpu
from jax.sharding import PartitionSpec as P

TOP = 8
CORES = 2
LANES = 128
ROW_BLOCK = 256
W_ROWS = 1024

f32 = jnp.float32
bf16 = jnp.bfloat16
nt = (((1,), (1,)), ((), ()))
tn = (((0,), (0,)), ((), ()))
VMEM = pl.BlockSpec(memory_space=pltpu.VMEM)
ANY = pl.BlockSpec(memory_space=pl.ANY)


def params(mib):
    return pltpu.CompilerParams(vmem_limit_bytes=mib * 1024 * 1024)


def row_iota(rows, lanes):
    return lax.broadcasted_iota(jnp.int32, (rows, lanes), 0)


def lane_iota(rows, lanes):
    return lax.broadcasted_iota(jnp.int32, (rows, lanes), 1)


def plan_kernel(home_cap, rep_cap, table, ids, gates, dy, dyg, kept_out):
    tokens, width = dy.shape
    lanes = dyg.shape[1] - width
    devices = table.shape[1]
    dyg[:, :width] = dy[...]
    expert = row_iota(devices, tokens)
    hosts = jnp.where(table[...] == row_iota(devices, devices), 1.0, 0.0)
    copies = 1.0 + jnp.sum(hosts, axis=1, keepdims=True)
    named = jnp.zeros((devices, tokens), f32)
    weight = jnp.zeros((devices, tokens), f32)
    for k in range(TOP):
        hit = expert == ids[k : k + 1]
        named = jnp.where(hit, 1.0, named)
        weight = jnp.where(hit, gates[k : k + 1].astype(f32), weight)
    earlier = row_iota(tokens, tokens) < lane_iota(tokens, tokens)
    rank = jnp.dot(
        named.astype(bf16), jnp.where(earlier, 1.0, 0.0).astype(bf16), preferred_element_type=f32
    )
    turn = rank + lax.axis_index("expert").astype(f32)
    at_home = turn == copies * jnp.floor(turn / copies + 0.5)
    cap = jnp.where(at_home, float(home_cap), float(rep_cap))
    kept = jnp.where((named > 0.0) & (rank < cap * copies), 1.0, 0.0)
    kept_out[...] = kept
    dense = (weight * kept).T
    if lanes > devices:
        dense = jnp.concatenate([dense, jnp.zeros((tokens, lanes - devices), f32)], axis=1)
    dyg[:, width:] = dense.astype(bf16)


def plan(table, ids, gates, dy, devices, lanes):
    tokens, width = dy.shape
    home_cap = max(2, 5 * tokens * TOP // (4 * devices))
    rep_cap = max(2, tokens * TOP // (2 * devices))
    return pl.pallas_call(
        functools.partial(plan_kernel, home_cap, rep_cap),
        out_shape=(
            jax.ShapeDtypeStruct((tokens, width + lanes), bf16),
            jax.ShapeDtypeStruct((devices, tokens), f32),
        ),
        in_specs=[VMEM] * 4,
        out_specs=(VMEM, VMEM),
        compiler_params=params(16),
        name="plan",
    )(table, ids, gates, dy)


def rows_kernel(slots, *refs):
    x_in, dyg_in = refs[:slots], refs[slots : 2 * slots]
    weights = refs[2 * slots : 2 * slots + 6]
    dxg, act = refs[2 * slots + 6 : 3 * slots + 6], refs[3 * slots + 6]
    x, dyg, w_gu, w_dn, sem = refs[3 * slots + 7 :]
    tokens, width = x_in[0].shape
    hidden = weights[2].shape[0]
    lanes = dyg.shape[1] - width
    copies = []

    def fetch(src, dst):
        copies.append(pltpu.make_async_copy(src, dst, sem.at[len(copies)]))
        copies[-1].start()
        return copies[-1]

    def fetch_weights(j):
        up = [
            fetch(weights[3 * j], w_gu.at[j, :, pl.ds(0, hidden)]),
            fetch(weights[3 * j + 1], w_gu.at[j, :, pl.ds(hidden, hidden)]),
        ]
        return up, [fetch(weights[3 * j + 2], w_dn.at[j])]

    got_x = [fetch(x_in[i], x.at[pl.ds(i * tokens, tokens)]) for i in range(slots)]
    own = fetch_weights(0)
    got_dy = [fetch(dyg_in[i], dyg.at[pl.ds(i * tokens, tokens)]) for i in range(slots)]
    sibling = fetch_weights(1)
    for c in got_x + own[0]:
        c.wait()

    rows = slots * tokens
    block = math.gcd(rows, max(ROW_BLOCK, tokens))
    me = lax.axis_index("expert")
    lane = lane_iota(block, lanes)

    def expert(j, at, after_up):
        here = pl.ds(at, block)
        pre = jnp.dot(x[here, :], w_gu[j], preferred_element_type=f32)
        after_up()
        back = lax.dot_general(dyg[here, :width], w_dn[j], nt, preferred_element_type=f32)
        column = lane == (me if j == 0 else me ^ 1)
        gate = jnp.sum(
            jnp.where(column, dyg[here, width:].astype(f32), 0.0), axis=1, keepdims=True
        )
        a, b = pre[:, :hidden], pre[:, hidden:]
        sig = jax.nn.sigmoid(a)
        silu = a * sig
        h = silu * b
        gg = jnp.sum(h.astype(bf16).astype(f32) * back, axis=1, keepdims=True)
        scaled = gate * back
        da = (scaled * b * sig * (1.0 + a * (1.0 - sig))).astype(bf16)
        db = (scaled * silu).astype(bf16)
        grads = jnp.concatenate([da, db], axis=1)
        first = j * 3 * hidden
        act[here, first : first + 2 * hidden] = grads
        act[here, first + 2 * hidden : first + 3 * hidden] = (gate * h).astype(bf16)
        dx = lax.dot_general(grads, w_gu[j], nt, preferred_element_type=f32)
        return dx, jnp.where(column, gg, 0.0)

    def wait_all(group):
        for c in group:
            c.wait()

    for at in range(0, rows, block):
        first = at == 0
        dx0, gg0 = expert(0, at, lambda: wait_all(got_dy + own[1]) if first else None)
        if first:
            wait_all(sibling[0] + sibling[1])
        dx1, gg1 = expert(1, at, lambda: None)
        dx = (dx0 + dx1).astype(bf16)
        gg = (gg0 + gg1).astype(bf16)
        for i in range(block // tokens):
            out = dxg[at // tokens + i]
            part = slice(i * tokens, (i + 1) * tokens)
            out[:, :width] = dx[part]
            out[:, width:] = gg[part]


def rows_grads(xs, dygs, weights):
    slots = len(xs)
    tokens, width = xs[0].shape
    full = dygs[0].shape[1]
    hidden = weights[2].shape[0]
    rows = slots * tokens
    flops = 2 * rows * 2 * 5 * width * hidden
    moved = 4 * rows * (width + full) + 12 * width * hidden + 4 * rows * full + 12 * rows * hidden
    return pl.pallas_call(
        functools.partial(rows_kernel, slots),
        out_shape=tuple(jax.ShapeDtypeStruct((tokens, full), bf16) for _ in xs)
        + (jax.ShapeDtypeStruct((rows, 6 * hidden), bf16),),
        in_specs=[ANY] * (2 * slots + 6),
        out_specs=(VMEM,) * (slots + 1),
        scratch_shapes=[
            pltpu.VMEM((rows, width), bf16),
            pltpu.VMEM((rows, full), bf16),
            pltpu.VMEM((2, width, 2 * hidden), bf16),
            pltpu.VMEM((2, hidden, width), bf16),
            pltpu.SemaphoreType.DMA((2 * slots + 6,)),
        ],
        compiler_params=params(20),
        cost_estimate=pl.CostEstimate(
            flops=flops, bytes_accessed=moved, transcendentals=2 * rows * hidden
        ),
        name="rows_grads",
    )(*xs, *dygs, *weights)


def weights_kernel(j, slots, steps, extra, *refs):
    x_in, dyg_in, act_in = refs[:slots], refs[slots : 2 * slots], refs[2 * slots : 2 * slots + steps]
    refs = refs[2 * slots + steps :]
    more, refs = refs[:extra], refs[extra:]
    gate_out, up_out, down_out = refs[:3]
    x, dy, act, sem = refs[3:]
    tokens, width = x_in[0].shape
    hidden = act.shape[1] // 3
    step_rows = act_in[0].shape[0]
    copies = []

    def fetch(src, dst):
        copies.append(pltpu.make_async_copy(src, dst, sem.at[len(copies)]))
        copies[-1].start()

    for i in range(steps):
        fetch(
            act_in[i].at[:, pl.ds(j * 3 * hidden, 3 * hidden)],
            act.at[pl.ds(i * step_rows, step_rows)],
        )
    for i in range(slots):
        fetch(x_in[i], x.at[pl.ds(i * tokens, tokens)])
    for i in range(slots):
        fetch(dyg_in[i].at[:, pl.ds(0, width)], dy.at[pl.ds(i * tokens, tokens)])
    for c in copies[: steps + slots]:
        c.wait()

    def put(out, here, value, k):
        if extra:
            value = value + more[k][here].astype(f32)
        if len(out.shape) == 3:
            out[0, here[0], here[1]] = value.astype(out.dtype)
        else:
            out[here[0], here[1]] = value.astype(out.dtype)

    part = math.gcd(width, 256)
    everything = slice(None)
    for m in range(0, width, part):
        here = (slice(m, m + part), everything)
        both = lax.dot_general(
            x[:, m : m + part], act[:, : 2 * hidden], tn, preferred_element_type=f32
        )
        put(gate_out, here, both[:, :hidden], 0)
        put(up_out, here, both[:, hidden:], 1)
    for c in copies[steps + slots :]:
        c.wait()
    part = math.gcd(hidden, 128)
    for m in range(0, hidden, part):
        here = (slice(m, m + part), everything)
        value = lax.dot_general(
            act[:, 2 * hidden + m : 2 * hidden + m + part], dy[...], tn, preferred_element_type=f32
        )
        put(down_out, here, value, 2)


def weights_grads(j, xs, dygs, acts, dtype, more=()):
    slots, steps = len(xs), len(acts)
    tokens, width = xs[0].shape
    hidden = acts[0].shape[1] // 6
    rows = slots * tokens
    lead = (1,) if more else ()
    return pl.pallas_call(
        functools.partial(weights_kernel, j, slots, steps, len(more)),
        out_shape=(
            jax.ShapeDtypeStruct(lead + (width, hidden), dtype),
            jax.ShapeDtypeStruct(lead + (width, hidden), dtype),
            jax.ShapeDtypeStruct(lead + (hidden, width), dtype),
        ),
        in_specs=[ANY] * (2 * slots + steps) + [VMEM] * len(more),
        out_specs=(VMEM,) * 3,
        scratch_shapes=[
            pltpu.VMEM((rows, width), bf16),
            pltpu.VMEM((rows, width), bf16),
            pltpu.VMEM((rows, 3 * hidden), bf16),
            pltpu.SemaphoreType.DMA((2 * slots + steps,)),
        ],
        compiler_params=params(20),
        cost_estimate=pl.CostEstimate(
            flops=6 * rows * width * hidden,
            bytes_accessed=rows * (4 * width + 6 * hidden) + 6 * width * hidden,
            transcendentals=0,
        ),
        name="weights_grads",
    )(*xs, *dygs, *acts, *more)


def finish_kernel(parts, ids, kept, *refs):
    pieces, (tokens_out, gates_out) = refs[:parts], refs[parts:]
    tokens, width = tokens_out.shape
    total = pieces[0][:, :width].astype(f32)
    gg = pieces[0][:, width:].astype(f32)
    for p in pieces[1:]:
        total = total + p[:, :width].astype(f32)
        gg = gg + p[:, width:].astype(f32)
    tokens_out[...] = total.astype(bf16)
    devices = kept.shape[0]
    gg = gg.T[:devices] * kept[...]
    expert = row_iota(devices, tokens)
    place = row_iota(TOP, tokens)
    out = jnp.zeros((TOP, tokens), f32)
    for k in range(TOP):
        value = jnp.sum(jnp.where(expert == ids[k : k + 1], gg, 0.0), axis=0, keepdims=True)
        out = jnp.where(place == k, value, out)
    gates_out[...] = out.astype(bf16)


def finish(ids, kept, pieces, width):
    tokens = ids.shape[1]
    return pl.pallas_call(
        functools.partial(finish_kernel, len(pieces)),
        out_shape=(
            jax.ShapeDtypeStruct((tokens, width), bf16),
            jax.ShapeDtypeStruct((TOP, tokens), bf16),
        ),
        in_specs=[VMEM] * (2 + len(pieces)),
        out_specs=(VMEM, VMEM),
        compiler_params=params(16),
        name="finish",
    )(ids, kept, *pieces)


def add(*terms):
    total = terms[0].astype(f32)
    for t in terms[1:]:
        total = total + t.astype(f32)
    return total.astype(bf16)


def on_device(tokens_in, grad_out, gates, expert_ids, replica_table, w_gate, w_up, w_down):
    devices = lax.axis_size("expert")
    tokens, width = tokens_in.shape
    lanes = -(-devices // LANES) * LANES
    chips = devices // CORES
    inner = 2 ** (int(math.log2(chips)) // 2)
    outer = chips // inner

    def moved(i, dz, dy):
        core, chip = i % CORES, i // CORES
        z, y = chip // inner, chip % inner
        return (((z + dz) % outer) * inner + (y + dy) % inner) * CORES + core

    def send_z(v):
        return lax.ppermute(v, "expert", [(i, moved(i, 1, 0)) for i in range(devices)])

    def send_y(v):
        return lax.ppermute(v, "expert", [(i, moved(i, 0, 1)) for i in range(devices)])

    def send_core(v):
        return lax.ppermute(v, "expert", [(i, i ^ 1) for i in range(devices)])

    ids = expert_ids.T
    dyg, kept = plan(replica_table[None], ids, gates.T, grad_out, devices, lanes)
    own = (w_gate[0], w_up[0], w_down[0])
    weights = own + tuple(send_core(w) for w in own)

    def together(*values):
        return lax.optimization_barrier(values)

    xs, dygs = [[tokens_in]], [[dyg]]
    for z in range(1, outer + 1):
        for k, stream in enumerate((xs, dygs)):
            last = stream[z - 1]
            if z < outer:
                ahead = send_z(last[0])
                for y in range(1, inner):
                    last.append(send_y(last[y - 1]))
                if inner > 1:
                    ahead, last[-1] = together(ahead, last[-1])
                stream.append([ahead])
            else:
                for y in range(1, inner):
                    if k and outer > 1 and y == inner - 1:
                        last.append(send_z(stream[z - 2][y]))
                    else:
                        last.append(send_y(last[y - 1]))

    per = max(1, W_ROWS // (inner * tokens))
    groups = [range(z, min(outer, z + per)) for z in range(0, outer, per)]
    sums = [None, None]

    def partial(j, group, dtype, more=()):
        return weights_grads(
            j,
            [x for z in group for x in xs[z]],
            [d for z in group for d in dygs[z]],
            [acts[z] for z in group],
            dtype,
            more,
        )

    dxs, acts, across = [], [], []
    for z in range(outer):
        *dx, act = rows_grads(xs[z], dygs[z], weights)
        dxs.append(dx)
        acts.append(act)
        if inner > 1:
            total = dx[1]
            for y in range(2, inner):
                total = add(send_y(total), dx[y])
            across.append([send_y(total)])
        else:
            across.append([])
        if len(groups) > 1 and z == groups[z // per][-1]:
            for j in range(2):
                value = partial(j, groups[z // per], f32)
                sums[j] = value if z < per else [t + v for t, v in zip(sums[j], value)]
            if z + 1 < outer:
                sums, xs[z + 1] = lax.optimization_barrier((sums, xs[z + 1]))

    single = len(groups) == 1
    if single:
        other = [send_core(v) for v in partial(1, groups[0], bf16)]
    else:
        other = [send_core(v.astype(bf16)) for v in sums[1]]

    pieces = [dxs[0][0], *across[0]]
    if outer > 1:
        total = add(dxs[1][0], *across[1])
        for z in range(2, outer):
            total = add(send_z(total), dxs[z][0], *across[z])
        total, other = together(total, other)
        pieces.append(send_z(total))
    if single:
        grad_w = partial(0, groups[0], bf16, other)
    else:
        grad_w = [(v + o.astype(f32)).astype(bf16)[None] for v, o in zip(sums[0], other)]
    pieces, grad_w = together(pieces, grad_w)
    grad_tokens, grad_gates = finish(ids, kept, pieces, width)
    grad_gates = grad_gates.T
    return (grad_tokens, grad_gates, *grad_w)


def solution(mesh):
    both = ("groups", "expert")
    return jax.shard_map(
        on_device,
        mesh=mesh,
        in_specs=(
            P(both, None),
            P(both, None),
            P(both, None),
            P(both, None),
            P("groups"),
            P("expert", None, None),
            P("expert", None, None),
            P("expert", None, None),
        ),
        out_specs=(
            P(both, None),
            P(both, None),
            P(both, None, None),
            P(both, None, None),
            P(both, None, None),
        ),
        check_vma=False,
    )
```

```python
import functools
import math

import jax
import jax.numpy as jnp
from jax import lax
from jax.experimental import pallas as pl
from jax.experimental.pallas import tpu as pltpu
from jax.sharding import PartitionSpec as P

TOP = 8
CORES = 2
LANES = 128
ROW_BLOCK = 256
W_ROWS = 1024
HOLD = 10**10

f32 = jnp.float32
bf16 = jnp.bfloat16
nt = (((1,), (1,)), ((), ()))
tn = (((0,), (0,)), ((), ()))
VMEM = pl.BlockSpec(memory_space=pltpu.VMEM)
ANY = pl.BlockSpec(memory_space=pl.ANY)


def params(mib):
    return pltpu.CompilerParams(vmem_limit_bytes=mib * 1024 * 1024)


def row_iota(rows, lanes):
    return lax.broadcasted_iota(jnp.int32, (rows, lanes), 0)


def lane_iota(rows, lanes):
    return lax.broadcasted_iota(jnp.int32, (rows, lanes), 1)


def plan_kernel(home_cap, rep_cap, table, ids, gates, dy, dyg, kept_out):
    tokens, width = dy.shape
    lanes = dyg.shape[1] - width
    devices = table.shape[1]
    dyg[:, :width] = dy[...]
    expert = row_iota(devices, tokens)
    hosts = jnp.where(table[...] == row_iota(devices, devices), 1.0, 0.0)
    copies = 1.0 + jnp.sum(hosts, axis=1, keepdims=True)
    named = jnp.zeros((devices, tokens), f32)
    weight = jnp.zeros((devices, tokens), f32)
    for k in range(TOP):
        hit = expert == ids[k : k + 1]
        named = jnp.where(hit, 1.0, named)
        weight = jnp.where(hit, gates[k : k + 1].astype(f32), weight)
    earlier = row_iota(tokens, tokens) < lane_iota(tokens, tokens)
    rank = jnp.dot(
        named.astype(bf16), jnp.where(earlier, 1.0, 0.0).astype(bf16), preferred_element_type=f32
    )
    turn = rank + lax.axis_index("expert").astype(f32)
    at_home = turn == copies * jnp.floor(turn / copies + 0.5)
    cap = jnp.where(at_home, float(home_cap), float(rep_cap))
    kept = jnp.where((named > 0.0) & (rank < cap * copies), 1.0, 0.0)
    kept_out[...] = kept
    dense = (weight * kept).T
    if lanes > devices:
        dense = jnp.concatenate([dense, jnp.zeros((tokens, lanes - devices), f32)], axis=1)
    dyg[:, width:] = dense.astype(bf16)


def plan(table, ids, gates, dy, devices, lanes):
    tokens, width = dy.shape
    home_cap = max(2, 5 * tokens * TOP // (4 * devices))
    rep_cap = max(2, tokens * TOP // (2 * devices))
    return pl.pallas_call(
        functools.partial(plan_kernel, home_cap, rep_cap),
        out_shape=(
            jax.ShapeDtypeStruct((tokens, width + lanes), bf16),
            jax.ShapeDtypeStruct((devices, tokens), f32),
        ),
        in_specs=[VMEM] * 4,
        out_specs=(VMEM, VMEM),
        compiler_params=params(16),
        name="plan",
    )(table, ids, gates, dy)


def hold_kernel(source, out):
    out[...] = source[...]


def hold(value, flops):
    return pl.pallas_call(
        hold_kernel,
        out_shape=jax.ShapeDtypeStruct(value.shape, value.dtype),
        in_specs=[VMEM],
        out_specs=VMEM,
        cost_estimate=pl.CostEstimate(flops=flops, bytes_accessed=1000, transcendentals=0),
        name="hold",
    )(value)


def rows_kernel(slots, *refs):
    x_in, dyg_in = refs[:slots], refs[slots : 2 * slots]
    weights = refs[2 * slots : 2 * slots + 6]
    dxg, act = refs[2 * slots + 6 : 3 * slots + 6], refs[3 * slots + 6]
    x, dyg, w_gu, w_dn, sem = refs[3 * slots + 7 :]
    tokens, width = x_in[0].shape
    hidden = weights[2].shape[0]
    lanes = dyg.shape[1] - width
    copies = []

    def fetch(src, dst):
        copies.append(pltpu.make_async_copy(src, dst, sem.at[len(copies)]))
        copies[-1].start()
        return copies[-1]

    def fetch_weights(j):
        up = [
            fetch(weights[3 * j], w_gu.at[j, :, pl.ds(0, hidden)]),
            fetch(weights[3 * j + 1], w_gu.at[j, :, pl.ds(hidden, hidden)]),
        ]
        return up, [fetch(weights[3 * j + 2], w_dn.at[j])]

    got_x = [fetch(x_in[i], x.at[pl.ds(i * tokens, tokens)]) for i in range(slots)]
    own = fetch_weights(0)
    got_dy = [fetch(dyg_in[i], dyg.at[pl.ds(i * tokens, tokens)]) for i in range(slots)]
    sibling = fetch_weights(1)
    for c in got_x + own[0]:
        c.wait()

    rows = slots * tokens
    block = math.gcd(rows, max(ROW_BLOCK, tokens))
    me = lax.axis_index("expert")
    lane = lane_iota(block, lanes)

    def expert(j, at, after_up):
        here = pl.ds(at, block)
        pre = jnp.dot(x[here, :], w_gu[j], preferred_element_type=f32)
        after_up()
        back = lax.dot_general(dyg[here, :width], w_dn[j], nt, preferred_element_type=f32)
        column = lane == (me if j == 0 else me ^ 1)
        gate = jnp.sum(
            jnp.where(column, dyg[here, width:].astype(f32), 0.0), axis=1, keepdims=True
        )
        a, b = pre[:, :hidden], pre[:, hidden:]
        sig = jax.nn.sigmoid(a)
        silu = a * sig
        h = silu * b
        gg = jnp.sum(h.astype(bf16).astype(f32) * back, axis=1, keepdims=True)
        scaled = gate * back
        da = (scaled * b * sig * (1.0 + a * (1.0 - sig))).astype(bf16)
        db = (scaled * silu).astype(bf16)
        grads = jnp.concatenate([da, db], axis=1)
        first = j * 3 * hidden
        act[here, first : first + 2 * hidden] = grads
        act[here, first + 2 * hidden : first + 3 * hidden] = (gate * h).astype(bf16)
        dx = lax.dot_general(grads, w_gu[j], nt, preferred_element_type=f32)
        return dx, jnp.where(column, gg, 0.0)

    def wait_all(group):
        for c in group:
            c.wait()

    for at in range(0, rows, block):
        first = at == 0
        dx0, gg0 = expert(0, at, lambda: wait_all(got_dy + own[1]) if first else None)
        if first:
            wait_all(sibling[0] + sibling[1])
        dx1, gg1 = expert(1, at, lambda: None)
        dx = (dx0 + dx1).astype(bf16)
        gg = (gg0 + gg1).astype(bf16)
        for i in range(block // tokens):
            out = dxg[at // tokens + i]
            part = slice(i * tokens, (i + 1) * tokens)
            out[:, :width] = dx[part]
            out[:, width:] = gg[part]


def rows_grads(xs, dygs, weights):
    slots = len(xs)
    tokens, width = xs[0].shape
    full = dygs[0].shape[1]
    hidden = weights[2].shape[0]
    rows = slots * tokens
    flops = 2 * rows * 2 * 5 * width * hidden
    moved = 4 * rows * (width + full) + 12 * width * hidden + 4 * rows * full + 12 * rows * hidden
    return pl.pallas_call(
        functools.partial(rows_kernel, slots),
        out_shape=tuple(jax.ShapeDtypeStruct((tokens, full), bf16) for _ in xs)
        + (jax.ShapeDtypeStruct((rows, 6 * hidden), bf16),),
        in_specs=[ANY] * (2 * slots + 6),
        out_specs=(VMEM,) * (slots + 1),
        scratch_shapes=[
            pltpu.VMEM((rows, width), bf16),
            pltpu.VMEM((rows, full), bf16),
            pltpu.VMEM((2, width, 2 * hidden), bf16),
            pltpu.VMEM((2, hidden, width), bf16),
            pltpu.SemaphoreType.DMA((2 * slots + 6,)),
        ],
        compiler_params=params(20),
        cost_estimate=pl.CostEstimate(
            flops=flops, bytes_accessed=moved, transcendentals=2 * rows * hidden
        ),
        name="rows_grads",
    )(*xs, *dygs, *weights)


def weights_kernel(j, slots, steps, extra, *refs):
    x_in, dyg_in, act_in = refs[:slots], refs[slots : 2 * slots], refs[2 * slots : 2 * slots + steps]
    refs = refs[2 * slots + steps :]
    more, refs = refs[:extra], refs[extra:]
    gate_out, up_out, down_out = refs[:3]
    x, dy, act, sem = refs[3:]
    tokens, width = x_in[0].shape
    hidden = act.shape[1] // 3
    step_rows = act_in[0].shape[0]
    copies = []

    def fetch(src, dst):
        copies.append(pltpu.make_async_copy(src, dst, sem.at[len(copies)]))
        copies[-1].start()

    for i in range(steps):
        fetch(
            act_in[i].at[:, pl.ds(j * 3 * hidden, 3 * hidden)],
            act.at[pl.ds(i * step_rows, step_rows)],
        )
    for i in range(slots):
        fetch(x_in[i], x.at[pl.ds(i * tokens, tokens)])
    for i in range(slots):
        fetch(dyg_in[i].at[:, pl.ds(0, width)], dy.at[pl.ds(i * tokens, tokens)])
    for c in copies[: steps + slots]:
        c.wait()

    def put(out, here, value, k):
        if extra:
            value = value + more[k][here].astype(f32)
        if len(out.shape) == 3:
            out[0, here[0], here[1]] = value.astype(out.dtype)
        else:
            out[here[0], here[1]] = value.astype(out.dtype)

    part = math.gcd(width, 256)
    everything = slice(None)
    for m in range(0, width, part):
        here = (slice(m, m + part), everything)
        both = lax.dot_general(
            x[:, m : m + part], act[:, : 2 * hidden], tn, preferred_element_type=f32
        )
        put(gate_out, here, both[:, :hidden], 0)
        put(up_out, here, both[:, hidden:], 1)
    for c in copies[steps + slots :]:
        c.wait()
    part = math.gcd(hidden, 128)
    for m in range(0, hidden, part):
        here = (slice(m, m + part), everything)
        value = lax.dot_general(
            act[:, 2 * hidden + m : 2 * hidden + m + part], dy[...], tn, preferred_element_type=f32
        )
        put(down_out, here, value, 2)


def weights_grads(j, xs, dygs, acts, dtype, more=()):
    slots, steps = len(xs), len(acts)
    tokens, width = xs[0].shape
    hidden = acts[0].shape[1] // 6
    rows = slots * tokens
    lead = (1,) if more else ()
    return pl.pallas_call(
        functools.partial(weights_kernel, j, slots, steps, len(more)),
        out_shape=(
            jax.ShapeDtypeStruct(lead + (width, hidden), dtype),
            jax.ShapeDtypeStruct(lead + (width, hidden), dtype),
            jax.ShapeDtypeStruct(lead + (hidden, width), dtype),
        ),
        in_specs=[ANY] * (2 * slots + steps) + [VMEM] * len(more),
        out_specs=(VMEM,) * 3,
        scratch_shapes=[
            pltpu.VMEM((rows, width), bf16),
            pltpu.VMEM((rows, width), bf16),
            pltpu.VMEM((rows, 3 * hidden), bf16),
            pltpu.SemaphoreType.DMA((2 * slots + steps,)),
        ],
        compiler_params=params(20),
        cost_estimate=pl.CostEstimate(
            flops=6 * rows * width * hidden,
            bytes_accessed=rows * (4 * width + 6 * hidden) + 6 * width * hidden,
            transcendentals=0,
        ),
        name="weights_grads",
    )(*xs, *dygs, *acts, *more)


def finish_kernel(parts, ids, kept, *refs):
    pieces, (tokens_out, gates_out) = refs[:parts], refs[parts:]
    tokens, width = tokens_out.shape
    total = pieces[0][:, :width].astype(f32)
    gg = pieces[0][:, width:].astype(f32)
    for p in pieces[1:]:
        total = total + p[:, :width].astype(f32)
        gg = gg + p[:, width:].astype(f32)
    tokens_out[...] = total.astype(bf16)
    devices = kept.shape[0]
    gg = gg.T[:devices] * kept[...]
    expert = row_iota(devices, tokens)
    place = row_iota(TOP, tokens)
    out = jnp.zeros((TOP, tokens), f32)
    for k in range(TOP):
        value = jnp.sum(jnp.where(expert == ids[k : k + 1], gg, 0.0), axis=0, keepdims=True)
        out = jnp.where(place == k, value, out)
    gates_out[...] = out.astype(bf16)


def finish(ids, kept, pieces, width):
    tokens = ids.shape[1]
    return pl.pallas_call(
        functools.partial(finish_kernel, len(pieces)),
        out_shape=(
            jax.ShapeDtypeStruct((tokens, width), bf16),
            jax.ShapeDtypeStruct((TOP, tokens), bf16),
        ),
        in_specs=[VMEM] * (2 + len(pieces)),
        out_specs=(VMEM, VMEM),
        compiler_params=params(16),
        name="finish",
    )(ids, kept, *pieces)


def add(*terms):
    total = terms[0].astype(f32)
    for t in terms[1:]:
        total = total + t.astype(f32)
    return total.astype(bf16)


def on_device(tokens_in, grad_out, gates, expert_ids, replica_table, w_gate, w_up, w_down):
    devices = lax.axis_size("expert")
    tokens, width = tokens_in.shape
    lanes = -(-devices // LANES) * LANES
    chips = devices // CORES
    inner = 2 ** (int(math.log2(chips)) // 2)
    outer = chips // inner

    def moved(i, dz, dy):
        core, chip = i % CORES, i // CORES
        z, y = chip // inner, chip % inner
        return (((z + dz) % outer) * inner + (y + dy) % inner) * CORES + core

    def send_z(v):
        return lax.ppermute(v, "expert", [(i, moved(i, 1, 0)) for i in range(devices)])

    def send_y(v):
        return lax.ppermute(v, "expert", [(i, moved(i, 0, 1)) for i in range(devices)])

    def send_core(v):
        return lax.ppermute(v, "expert", [(i, i ^ 1) for i in range(devices)])

    ids = expert_ids.T
    dyg, kept = plan(replica_table[None], ids, gates.T, grad_out, devices, lanes)
    own = (w_gate[0], w_up[0], w_down[0])
    weights = own + tuple(send_core(w) for w in own)

    def together(*values):
        return lax.optimization_barrier(values)

    per = max(1, W_ROWS // (inner * tokens))
    groups = [range(z, min(outer, z + per)) for z in range(0, outer, per)]
    sums = [None, None]

    def partial(j, group, dtype, more=()):
        return weights_grads(
            j,
            [x for z in group for x in xs[z]],
            [d for z in group for d in dygs[z]],
            [acts[z] for z in group],
            dtype,
            more,
        )

    xs, dygs = [[tokens_in]], [[dyg]]
    dxs, acts, across = [], [], []

    def send_across(z):
        if inner > 1:
            total = dxs[z][1]
            for y in range(2, inner):
                total = add(send_y(total), dxs[z][y])
            across.append([send_y(total)])
        else:
            across.append([])

    for z in range(1, outer + 1):
        for k, stream in enumerate((xs, dygs)):
            last = stream[z - 1]
            ahead = None
            if z < outer:
                ahead = send_z(last[0])
            for y in range(1, inner):
                if k and z == outer > 1 and y == inner - 1:
                    last.append(send_z(stream[z - 2][y]))
                else:
                    last.append(send_y(last[y - 1]))
            done = [last[-1]] if inner > 1 else []
            if ahead is not None:
                done.append(ahead)
            if k == 0 and z == 1:
                done, kept, weights = together(done, hold(kept, HOLD), weights)
            elif k == 0:
                done, dxs[z - 2], acts[z - 2] = together(done, dxs[z - 2], acts[z - 2])
            else:
                (done,) = together(done)
            if ahead is not None:
                stream.append([done.pop()])
            if inner > 1:
                last[-1] = done.pop()
        if z > 2:
            send_across(z - 2)
        *dx, act = rows_grads(xs[z - 1], dygs[z - 1], weights)
        dxs.append(dx)
        acts.append(act)
        if len(groups) > 1 and z - 1 == groups[(z - 1) // per][-1]:
            for j in range(2):
                value = partial(j, groups[(z - 1) // per], f32)
                sums[j] = value if z <= per else [t + v for t, v in zip(sums[j], value)]
            if z < outer:
                sums, xs[z] = together(sums, xs[z])
    if outer > 1:
        send_across(outer - 1)
        dxs[0], acts[-1] = together(dxs[0], acts[-1])
    send_across(0)

    single = len(groups) == 1
    if single:
        other = [send_core(v) for v in partial(1, groups[0], bf16)]
    else:
        other = [send_core(v.astype(bf16)) for v in sums[1]]

    pieces = [dxs[0][0], *across[-1]]
    if outer > 1:
        total = add(dxs[1][0], *across[0])
        for z in range(2, outer):
            total = add(send_z(total), dxs[z][0], *across[z - 1])
        total, other = together(total, other)
        pieces.append(send_z(total))
    if single:
        grad_w = partial(0, groups[0], bf16, other)
    else:
        grad_w = [(v + o.astype(f32)).astype(bf16)[None] for v, o in zip(sums[0], other)]
    pieces, grad_w = together(pieces, grad_w)
    grad_tokens, grad_gates = finish(ids, kept, pieces, width)
    grad_gates = grad_gates.T
    return (grad_tokens, grad_gates, *grad_w)


def solution(mesh):
    both = ("groups", "expert")
    return jax.shard_map(
        on_device,
        mesh=mesh,
        in_specs=(
            P(both, None),
            P(both, None),
            P(both, None),
            P(both, None),
            P("groups"),
            P("expert", None, None),
            P("expert", None, None),
            P("expert", None, None),
        ),
        out_specs=(
            P(both, None),
            P(both, None),
            P(both, None, None),
            P(both, None, None),
            P(both, None, None),
        ),
        check_vma=False,
    )
```

```python
import functools
import math

import jax
import jax.numpy as jnp
from jax import lax
from jax.experimental import pallas as pl
from jax.experimental.pallas import tpu as pltpu
from jax.sharding import PartitionSpec as P

TOP = 8
CORES = 2
LANES = 128
ROW_BLOCK = 256
W_ROWS = 1024
HOLD = 10**10
PLAN_MIB = 60

f32 = jnp.float32
bf16 = jnp.bfloat16
nt = (((1,), (1,)), ((), ()))
tn = (((0,), (0,)), ((), ()))
VMEM = pl.BlockSpec(memory_space=pltpu.VMEM)
ANY = pl.BlockSpec(memory_space=pl.ANY)
HBM = pl.BlockSpec(memory_space=pltpu.HBM)


def params(mib):
    return pltpu.CompilerParams(vmem_limit_bytes=mib * 1024 * 1024)


def row_iota(rows, lanes):
    return lax.broadcasted_iota(jnp.int32, (rows, lanes), 0)


def lane_iota(rows, lanes):
    return lax.broadcasted_iota(jnp.int32, (rows, lanes), 1)


def plan_kernel(home_cap, rep_cap, table_in, ids_in, gates_in, x_in, xg, kept_out, *scratch):
    table, ids, gates, sem = scratch
    tokens, width = x_in.shape
    lanes = xg.shape[1] - width
    pairs = (
        (table_in, table),
        (ids_in, ids),
        (gates_in, gates),
        (x_in, xg.at[:, pl.ds(0, width)]),
    )
    copies = [pltpu.make_async_copy(src, dst, sem.at[i]) for i, (src, dst) in enumerate(pairs)]
    for c in copies:
        c.start()
    devices = table.shape[1]
    earlier = row_iota(tokens, tokens) < lane_iota(tokens, tokens)
    earlier = jnp.where(earlier, 1.0, 0.0).astype(bf16)
    expert = row_iota(devices, tokens)
    for c in copies[:3]:
        c.wait()
    hosts = jnp.where(table[...] == row_iota(devices, devices), 1.0, 0.0)
    copied = 1.0 + jnp.sum(hosts, axis=1, keepdims=True)
    named = jnp.zeros((devices, tokens), f32)
    weight = jnp.zeros((devices, tokens), f32)
    for k in range(TOP):
        hit = expert == ids[k : k + 1]
        named = jnp.where(hit, 1.0, named)
        weight = jnp.where(hit, gates[k : k + 1].astype(f32), weight)
    rank = jnp.dot(named.astype(bf16), earlier, preferred_element_type=f32)
    turn = rank + lax.axis_index("expert").astype(f32)
    at_home = turn == copied * jnp.floor(turn / copied + 0.5)
    cap = jnp.where(at_home, float(home_cap), float(rep_cap))
    kept = jnp.where((named > 0.0) & (rank < cap * copied), 1.0, 0.0)
    kept_out[...] = kept
    dense = (weight * kept).T
    if lanes > devices:
        dense = jnp.concatenate([dense, jnp.zeros((tokens, lanes - devices), f32)], axis=1)
    xg[:, width:] = dense.astype(bf16)
    copies[3].wait()


def plan(table, ids, gates, x, devices, lanes):
    tokens, width = x.shape
    home_cap = max(2, 5 * tokens * TOP // (4 * devices))
    rep_cap = max(2, tokens * TOP // (2 * devices))
    return pl.pallas_call(
        functools.partial(plan_kernel, home_cap, rep_cap),
        out_shape=(
            jax.ShapeDtypeStruct((tokens, width + lanes), bf16),
            jax.ShapeDtypeStruct((devices, tokens), f32),
        ),
        in_specs=[HBM] * 4,
        out_specs=(VMEM, VMEM),
        scratch_shapes=[
            pltpu.VMEM(table.shape, jnp.int32),
            pltpu.VMEM(ids.shape, jnp.int32),
            pltpu.VMEM(gates.shape, bf16),
            pltpu.SemaphoreType.DMA((4,)),
        ],
        compiler_params=params(PLAN_MIB),
        name="plan",
    )(table, ids, gates, x)


def hold(value, flops):
    return pl.pallas_call(
        lambda source, out: None,
        out_shape=jax.ShapeDtypeStruct(value.shape, value.dtype),
        in_specs=[ANY],
        out_specs=ANY,
        input_output_aliases={0: 0},
        cost_estimate=pl.CostEstimate(flops=flops, bytes_accessed=1000, transcendentals=0),
        name="hold",
    )(value)


def rows_kernel(slots, *refs):
    xg_in, dy_in = refs[:slots], refs[slots : 2 * slots]
    weights = refs[2 * slots : 2 * slots + 6]
    dxg, act = refs[2 * slots + 6 : 3 * slots + 6], refs[3 * slots + 6]
    xg, dy, w_gu, w_dn, sem = refs[3 * slots + 7 :]
    tokens, width = dy_in[0].shape
    hidden = weights[2].shape[0]
    lanes = xg.shape[1] - width
    copies = []

    def fetch(src, dst):
        copies.append(pltpu.make_async_copy(src, dst, sem.at[len(copies)]))
        copies[-1].start()
        return copies[-1]

    def fetch_weights(j):
        up = [
            fetch(weights[3 * j], w_gu.at[j, :, pl.ds(0, hidden)]),
            fetch(weights[3 * j + 1], w_gu.at[j, :, pl.ds(hidden, hidden)]),
        ]
        return up, [fetch(weights[3 * j + 2], w_dn.at[j])]

    got_x = [fetch(xg_in[i], xg.at[pl.ds(i * tokens, tokens)]) for i in range(slots)]
    own = fetch_weights(0)
    got_dy = [fetch(dy_in[i], dy.at[pl.ds(i * tokens, tokens)]) for i in range(slots)]
    sibling = fetch_weights(1)
    for c in got_x + own[0]:
        c.wait()

    rows = slots * tokens
    block = math.gcd(rows, max(ROW_BLOCK, tokens))
    me = lax.axis_index("expert")
    lane = lane_iota(block, lanes)

    def expert(j, at, after_up):
        here = pl.ds(at, block)
        pre = jnp.dot(xg[here, :width], w_gu[j], preferred_element_type=f32)
        after_up()
        back = lax.dot_general(dy[here, :], w_dn[j], nt, preferred_element_type=f32)
        column = lane == (me if j == 0 else me ^ 1)
        gate = jnp.sum(
            jnp.where(column, xg[here, width:].astype(f32), 0.0), axis=1, keepdims=True
        )
        a, b = pre[:, :hidden], pre[:, hidden:]
        sig = jax.nn.sigmoid(a)
        silu = a * sig
        h = silu * b
        gg = jnp.sum(h.astype(bf16).astype(f32) * back, axis=1, keepdims=True)
        scaled = gate * back
        da = (scaled * b * sig * (1.0 + a * (1.0 - sig))).astype(bf16)
        db = (scaled * silu).astype(bf16)
        grads = jnp.concatenate([da, db], axis=1)
        first = j * 3 * hidden
        act[here, first : first + 2 * hidden] = grads
        act[here, first + 2 * hidden : first + 3 * hidden] = (gate * h).astype(bf16)
        dx = lax.dot_general(grads, w_gu[j], nt, preferred_element_type=f32)
        return dx, jnp.where(column, gg, 0.0)

    def wait_all(group):
        for c in group:
            c.wait()

    for at in range(0, rows, block):
        first = at == 0
        dx0, gg0 = expert(0, at, lambda: wait_all(got_dy + own[1]) if first else None)
        if first:
            wait_all(sibling[0] + sibling[1])
        dx1, gg1 = expert(1, at, lambda: None)
        dx = (dx0 + dx1).astype(bf16)
        gg = (gg0 + gg1).astype(bf16)
        for i in range(block // tokens):
            out = dxg[at // tokens + i]
            part = slice(i * tokens, (i + 1) * tokens)
            out[:, :width] = dx[part]
            out[:, width:] = gg[part]


def rows_grads(xgs, dys, weights):
    slots = len(dys)
    tokens, width = dys[0].shape
    full = xgs[0].shape[1]
    hidden = weights[2].shape[0]
    rows = slots * tokens
    flops = 2 * rows * 2 * 5 * width * hidden
    moved = 4 * rows * (width + full) + 12 * width * hidden + 4 * rows * full + 12 * rows * hidden
    return pl.pallas_call(
        functools.partial(rows_kernel, slots),
        out_shape=tuple(jax.ShapeDtypeStruct((tokens, full), bf16) for _ in dys)
        + (jax.ShapeDtypeStruct((rows, 6 * hidden), bf16),),
        in_specs=[ANY] * (2 * slots + 6),
        out_specs=(VMEM,) * (slots + 1),
        scratch_shapes=[
            pltpu.VMEM((rows, full), bf16),
            pltpu.VMEM((rows, width), bf16),
            pltpu.VMEM((2, width, 2 * hidden), bf16),
            pltpu.VMEM((2, hidden, width), bf16),
            pltpu.SemaphoreType.DMA((2 * slots + 6,)),
        ],
        compiler_params=params(20),
        cost_estimate=pl.CostEstimate(
            flops=flops, bytes_accessed=moved, transcendentals=2 * rows * hidden
        ),
        name="rows_grads",
    )(*xgs, *dys, *weights)


def weights_kernel(j, slots, steps, extra, *refs):
    xg_in, dy_in, act_in = refs[:slots], refs[slots : 2 * slots], refs[2 * slots : 2 * slots + steps]
    refs = refs[2 * slots + steps :]
    more, refs = refs[:extra], refs[extra:]
    gate_out, up_out, down_out = refs[:3]
    x, dy, act, sem = refs[3:]
    tokens, width = dy_in[0].shape
    hidden = act.shape[1] // 3
    step_rows = act_in[0].shape[0]
    copies = []

    def fetch(src, dst):
        copies.append(pltpu.make_async_copy(src, dst, sem.at[len(copies)]))
        copies[-1].start()

    for i in range(steps):
        fetch(
            act_in[i].at[:, pl.ds(j * 3 * hidden, 3 * hidden)],
            act.at[pl.ds(i * step_rows, step_rows)],
        )
    for i in range(slots):
        fetch(xg_in[i].at[:, pl.ds(0, width)], x.at[pl.ds(i * tokens, tokens)])
    for i in range(slots):
        fetch(dy_in[i], dy.at[pl.ds(i * tokens, tokens)])
    for c in copies[: steps + slots]:
        c.wait()

    def put(out, here, value, k):
        if extra:
            value = value + more[k][here].astype(f32)
        if len(out.shape) == 3:
            out[0, here[0], here[1]] = value.astype(out.dtype)
        else:
            out[here[0], here[1]] = value.astype(out.dtype)

    part = math.gcd(width, 256)
    everything = slice(None)
    for m in range(0, width, part):
        here = (slice(m, m + part), everything)
        both = lax.dot_general(
            x[:, m : m + part], act[:, : 2 * hidden], tn, preferred_element_type=f32
        )
        put(gate_out, here, both[:, :hidden], 0)
        put(up_out, here, both[:, hidden:], 1)
    for c in copies[steps + slots :]:
        c.wait()
    part = math.gcd(hidden, 128)
    for m in range(0, hidden, part):
        here = (slice(m, m + part), everything)
        value = lax.dot_general(
            act[:, 2 * hidden + m : 2 * hidden + m + part], dy[...], tn, preferred_element_type=f32
        )
        put(down_out, here, value, 2)


def weights_grads(j, xgs, dys, acts, dtype, more=()):
    slots, steps = len(dys), len(acts)
    tokens, width = dys[0].shape
    hidden = acts[0].shape[1] // 6
    rows = slots * tokens
    lead = (1,) if more else ()
    return pl.pallas_call(
        functools.partial(weights_kernel, j, slots, steps, len(more)),
        out_shape=(
            jax.ShapeDtypeStruct(lead + (width, hidden), dtype),
            jax.ShapeDtypeStruct(lead + (width, hidden), dtype),
            jax.ShapeDtypeStruct(lead + (hidden, width), dtype),
        ),
        in_specs=[ANY] * (2 * slots + steps) + [VMEM] * len(more),
        out_specs=(VMEM,) * 3,
        scratch_shapes=[
            pltpu.VMEM((rows, width), bf16),
            pltpu.VMEM((rows, width), bf16),
            pltpu.VMEM((rows, 3 * hidden), bf16),
            pltpu.SemaphoreType.DMA((2 * slots + steps,)),
        ],
        compiler_params=params(20),
        cost_estimate=pl.CostEstimate(
            flops=6 * rows * width * hidden,
            bytes_accessed=rows * (4 * width + 6 * hidden) + 6 * width * hidden,
            transcendentals=0,
        ),
        name="weights_grads",
    )(*xgs, *dys, *acts, *more)


def finish_kernel(parts, ids, kept, *refs):
    pieces, (tokens_out, gates_out) = refs[:parts], refs[parts:]
    tokens, width = tokens_out.shape
    total = pieces[0][:, :width].astype(f32)
    gg = pieces[0][:, width:].astype(f32)
    for p in pieces[1:]:
        total = total + p[:, :width].astype(f32)
        gg = gg + p[:, width:].astype(f32)
    tokens_out[...] = total.astype(bf16)
    devices = kept.shape[0]
    gg = gg.T[:devices] * kept[...]
    expert = row_iota(devices, tokens)
    place = row_iota(TOP, tokens)
    out = jnp.zeros((TOP, tokens), f32)
    for k in range(TOP):
        value = jnp.sum(jnp.where(expert == ids[k : k + 1], gg, 0.0), axis=0, keepdims=True)
        out = jnp.where(place == k, value, out)
    gates_out[...] = out.astype(bf16)


def finish(ids, kept, pieces, width):
    tokens = ids.shape[1]
    return pl.pallas_call(
        functools.partial(finish_kernel, len(pieces)),
        out_shape=(
            jax.ShapeDtypeStruct((tokens, width), bf16),
            jax.ShapeDtypeStruct((TOP, tokens), bf16),
        ),
        in_specs=[VMEM] * (2 + len(pieces)),
        out_specs=(VMEM, VMEM),
        compiler_params=params(16),
        name="finish",
    )(ids, kept, *pieces)


def add(*terms):
    total = terms[0].astype(f32)
    for t in terms[1:]:
        total = total + t.astype(f32)
    return total.astype(bf16)


def on_device(tokens_in, grad_out, gates, expert_ids, replica_table, w_gate, w_up, w_down):
    devices = lax.axis_size("expert")
    tokens, width = tokens_in.shape
    lanes = -(-devices // LANES) * LANES
    chips = devices // CORES
    inner = 2 ** (int(math.log2(chips)) // 2)
    outer = chips // inner

    def moved(i, dz, dy):
        core, chip = i % CORES, i // CORES
        z, y = chip // inner, chip % inner
        return (((z + dz) % outer) * inner + (y + dy) % inner) * CORES + core

    def send_z(v):
        return lax.ppermute(v, "expert", [(i, moved(i, 1, 0)) for i in range(devices)])

    def send_down(v):
        return lax.ppermute(v, "expert", [(i, moved(i, -1, 0)) for i in range(devices)])

    def send_y(v):
        return lax.ppermute(v, "expert", [(i, moved(i, 0, 1)) for i in range(devices)])

    def send_core(v):
        return lax.ppermute(v, "expert", [(i, i ^ 1) for i in range(devices)])

    ids = expert_ids.T
    xg, kept = plan(replica_table[None], ids, gates.T, tokens_in, devices, lanes)
    own = (w_gate[0], w_up[0], w_down[0])
    weights = own + tuple(send_core(w) for w in own)

    def together(*values):
        return lax.optimization_barrier(values)

    per = max(1, W_ROWS // (inner * tokens))
    groups = [range(z, min(outer, z + per)) for z in range(0, outer, per)]
    sums = [None, None]

    def partial(j, group, dtype, more=()):
        return weights_grads(
            j,
            [x for z in group for x in xgs[z]],
            [d for z in group for d in dys[z]],
            [acts[z] for z in group],
            dtype,
            more,
        )

    xgs, dys = [[xg]], [[grad_out]]
    dxs, acts, across = [], [], []

    def send_across(z):
        if inner == 1:
            return []
        total = dxs[z][1]
        for y in range(2, inner):
            total = add(send_y(total), dxs[z][y])
        return [send_y(total)]

    for z in range(1, outer + 1):
        for k, stream in enumerate((xgs, dys)):
            last = stream[z - 1]
            ahead = None
            if z < outer:
                ahead = send_z(last[0])
            for y in range(1, inner):
                if k and z == outer > 1 and y == inner - 1:
                    last.append(send_z(stream[z - 2][y]))
                else:
                    last.append(send_y(last[y - 1]))
            done = [last[-1]] if inner > 1 else []
            if ahead is not None:
                done.append(ahead)
            if k == 0 and z == 1:
                kept, weights = together(kept, weights)
                done, kept = together(done, hold(kept, HOLD))
            elif k == 0:
                done, acts[z - 2] = together(done, acts[z - 2])
            else:
                (done,) = together(done)
            if ahead is not None:
                stream.append([done.pop()])
            if inner > 1:
                last[-1] = done.pop()
        *dx, act = rows_grads(xgs[z - 1], dys[z - 1], weights)
        dxs.append(dx)
        acts.append(act)
        if z > 2:
            across.append(send_across(z - 1))
        if len(groups) > 1 and z - 1 == groups[(z - 1) // per][-1]:
            for j in range(2):
                value = partial(j, groups[(z - 1) // per], f32)
                sums[j] = value if z <= per else [t + v for t, v in zip(sums[j], value)]
            if z < outer:
                sums, xgs[z] = together(sums, xgs[z])

    single = len(groups) == 1
    if single:
        other = [send_core(v) for v in partial(1, groups[0], bf16)]
    else:
        other = [send_core(v.astype(bf16)) for v in sums[1]]

    pieces = []
    if outer > 1:
        dxs[1], acts[-2] = together(dxs[1], acts[-2])
        back = [send_down(v) for v in dxs[1]]
        pieces.append(back[0])
        dxs[0] = [dxs[0][0]] + [add(v, o) for v, o in zip(dxs[0][1:], back[1:])]
    pieces += [dxs[0][0], *send_across(0)]
    if outer > 2:
        total = add(dxs[2][0], *across[0])
        for z in range(3, outer):
            total = add(send_z(total), dxs[z][0], *across[z - 2])
        total, other = together(total, other)
        pieces.append(send_z(total))
    if single:
        grad_w = partial(0, groups[0], bf16, other)
    else:
        grad_w = [(v + o.astype(f32)).astype(bf16)[None] for v, o in zip(sums[0], other)]
    pieces, grad_w = together(pieces, grad_w)
    grad_tokens, grad_gates = finish(ids, kept, pieces, width)
    grad_gates = grad_gates.T
    return (grad_tokens, grad_gates, *grad_w)


def solution(mesh):
    both = ("groups", "expert")
    return jax.shard_map(
        on_device,
        mesh=mesh,
        in_specs=(
            P(both, None),
            P(both, None),
            P(both, None),
            P(both, None),
            P("groups"),
            P("expert", None, None),
            P("expert", None, None),
            P("expert", None, None),
        ),
        out_specs=(
            P(both, None),
            P(both, None),
            P(both, None, None),
            P(both, None, None),
            P(both, None, None),
        ),
        check_vma=False,
    )
```

```python
import functools
import math

import jax
import jax.numpy as jnp
from jax import lax
from jax.experimental import pallas as pl
from jax.experimental.pallas import tpu as pltpu
from jax.sharding import PartitionSpec as P

TOP = 8
CORES = 2
LANES = 128
ROW_BLOCK = 256
W_ROWS = 1024
HOLD = 10**10
PLAN_MIB = 60

f32 = jnp.float32
bf16 = jnp.bfloat16
nt = (((1,), (1,)), ((), ()))
tn = (((0,), (0,)), ((), ()))
VMEM = pl.BlockSpec(memory_space=pltpu.VMEM)
ANY = pl.BlockSpec(memory_space=pl.ANY)
HBM = pl.BlockSpec(memory_space=pltpu.HBM)


def params(mib):
    return pltpu.CompilerParams(vmem_limit_bytes=mib * 1024 * 1024)


def row_iota(rows, lanes):
    return lax.broadcasted_iota(jnp.int32, (rows, lanes), 0)


def lane_iota(rows, lanes):
    return lax.broadcasted_iota(jnp.int32, (rows, lanes), 1)


def plan_kernel(home_cap, rep_cap, table_in, ids_in, gates_in, x_in, xg, kept_out, *scratch):
    table, ids, gates, sem = scratch
    tokens, width = x_in.shape
    lanes = xg.shape[1] - width
    pairs = (
        (table_in, table),
        (ids_in, ids),
        (gates_in, gates),
        (x_in, xg.at[:, pl.ds(0, width)]),
    )
    copies = [pltpu.make_async_copy(src, dst, sem.at[i]) for i, (src, dst) in enumerate(pairs)]
    for c in copies:
        c.start()
    devices = table.shape[1]
    earlier = row_iota(tokens, tokens) < lane_iota(tokens, tokens)
    earlier = jnp.where(earlier, 1.0, 0.0).astype(bf16)
    expert = row_iota(devices, tokens)
    for c in copies[:3]:
        c.wait()
    hosts = jnp.where(table[...] == row_iota(devices, devices), 1.0, 0.0)
    copied = 1.0 + jnp.sum(hosts, axis=1, keepdims=True)
    named = jnp.zeros((devices, tokens), f32)
    weight = jnp.zeros((devices, tokens), f32)
    for k in range(TOP):
        hit = expert == ids[k : k + 1]
        named = jnp.where(hit, 1.0, named)
        weight = jnp.where(hit, gates[k : k + 1].astype(f32), weight)
    rank = jnp.dot(named.astype(bf16), earlier, preferred_element_type=f32)
    turn = rank + lax.axis_index("expert").astype(f32)
    at_home = turn == copied * jnp.floor(turn / copied + 0.5)
    cap = jnp.where(at_home, float(home_cap), float(rep_cap))
    kept = jnp.where((named > 0.0) & (rank < cap * copied), 1.0, 0.0)
    kept_out[...] = kept
    dense = (weight * kept).T
    if lanes > devices:
        dense = jnp.concatenate([dense, jnp.zeros((tokens, lanes - devices), f32)], axis=1)
    xg[:, width:] = dense.astype(bf16)
    copies[3].wait()


def plan(table, ids, gates, x, devices, lanes):
    tokens, width = x.shape
    home_cap = max(2, 5 * tokens * TOP // (4 * devices))
    rep_cap = max(2, tokens * TOP // (2 * devices))
    return pl.pallas_call(
        functools.partial(plan_kernel, home_cap, rep_cap),
        out_shape=(
            jax.ShapeDtypeStruct((tokens, width + lanes), bf16),
            jax.ShapeDtypeStruct((devices, tokens), f32),
        ),
        in_specs=[HBM] * 4,
        out_specs=(VMEM, VMEM),
        scratch_shapes=[
            pltpu.VMEM(table.shape, jnp.int32),
            pltpu.VMEM(ids.shape, jnp.int32),
            pltpu.VMEM(gates.shape, bf16),
            pltpu.SemaphoreType.DMA((4,)),
        ],
        compiler_params=params(PLAN_MIB),
        name="plan",
    )(table, ids, gates, x)


def hold(value, flops):
    return pl.pallas_call(
        lambda source, out: None,
        out_shape=jax.ShapeDtypeStruct(value.shape, value.dtype),
        in_specs=[ANY],
        out_specs=ANY,
        input_output_aliases={0: 0},
        cost_estimate=pl.CostEstimate(flops=flops, bytes_accessed=1000, transcendentals=0),
        name="hold",
    )(value)


def rows_kernel(slots, *refs):
    xg_in, dy_in = refs[:slots], refs[slots : 2 * slots]
    weights = refs[2 * slots : 2 * slots + 6]
    dxg, act = refs[2 * slots + 6 : 3 * slots + 6], refs[3 * slots + 6]
    xg, dy, w_gu, w_dn, sem = refs[3 * slots + 7 :]
    tokens, width = dy_in[0].shape
    hidden = weights[2].shape[0]
    lanes = xg.shape[1] - width
    copies = []

    def fetch(src, dst):
        copies.append(pltpu.make_async_copy(src, dst, sem.at[len(copies)]))
        copies[-1].start()
        return copies[-1]

    def fetch_weights(j):
        up = [
            fetch(weights[3 * j], w_gu.at[j, :, pl.ds(0, hidden)]),
            fetch(weights[3 * j + 1], w_gu.at[j, :, pl.ds(hidden, hidden)]),
        ]
        return up, [fetch(weights[3 * j + 2], w_dn.at[j])]

    got_x = [fetch(xg_in[i], xg.at[pl.ds(i * tokens, tokens)]) for i in range(slots)]
    own = fetch_weights(0)
    got_dy = [fetch(dy_in[i], dy.at[pl.ds(i * tokens, tokens)]) for i in range(slots)]
    sibling = fetch_weights(1)
    for c in got_x + own[0]:
        c.wait()

    rows = slots * tokens
    block = math.gcd(rows, max(ROW_BLOCK, tokens))
    me = lax.axis_index("expert")
    lane = lane_iota(block, lanes)

    def expert(j, at, after_up):
        here = pl.ds(at, block)
        pre = jnp.dot(xg[here, :width], w_gu[j], preferred_element_type=f32)
        after_up()
        back = lax.dot_general(dy[here, :], w_dn[j], nt, preferred_element_type=f32)
        column = lane == (me if j == 0 else me ^ 1)
        gate = jnp.sum(
            jnp.where(column, xg[here, width:].astype(f32), 0.0), axis=1, keepdims=True
        )
        a, b = pre[:, :hidden], pre[:, hidden:]
        sig = jax.nn.sigmoid(a)
        silu = a * sig
        h = silu * b
        gg = jnp.sum(h.astype(bf16).astype(f32) * back, axis=1, keepdims=True)
        scaled = gate * back
        da = (scaled * b * sig * (1.0 + a * (1.0 - sig))).astype(bf16)
        db = (scaled * silu).astype(bf16)
        grads = jnp.concatenate([da, db], axis=1)
        first = j * 3 * hidden
        act[here, first : first + 2 * hidden] = grads
        act[here, first + 2 * hidden : first + 3 * hidden] = (gate * h).astype(bf16)
        dx = lax.dot_general(grads, w_gu[j], nt, preferred_element_type=f32)
        return dx, jnp.where(column, gg, 0.0)

    def wait_all(group):
        for c in group:
            c.wait()

    for at in range(0, rows, block):
        first = at == 0
        dx0, gg0 = expert(0, at, lambda: wait_all(got_dy + own[1]) if first else None)
        if first:
            wait_all(sibling[0] + sibling[1])
        dx1, gg1 = expert(1, at, lambda: None)
        dx = (dx0 + dx1).astype(bf16)
        gg = (gg0 + gg1).astype(bf16)
        for i in range(block // tokens):
            out = dxg[at // tokens + i]
            part = slice(i * tokens, (i + 1) * tokens)
            out[:, :width] = dx[part]
            out[:, width:] = gg[part]


def rows_grads(xgs, dys, weights):
    slots = len(dys)
    tokens, width = dys[0].shape
    full = xgs[0].shape[1]
    hidden = weights[2].shape[0]
    rows = slots * tokens
    flops = 2 * rows * 2 * 5 * width * hidden
    moved = 4 * rows * (width + full) + 12 * width * hidden + 4 * rows * full + 12 * rows * hidden
    return pl.pallas_call(
        functools.partial(rows_kernel, slots),
        out_shape=tuple(jax.ShapeDtypeStruct((tokens, full), bf16) for _ in dys)
        + (jax.ShapeDtypeStruct((rows, 6 * hidden), bf16),),
        in_specs=[ANY] * (2 * slots + 6),
        out_specs=(VMEM,) * (slots + 1),
        scratch_shapes=[
            pltpu.VMEM((rows, full), bf16),
            pltpu.VMEM((rows, width), bf16),
            pltpu.VMEM((2, width, 2 * hidden), bf16),
            pltpu.VMEM((2, hidden, width), bf16),
            pltpu.SemaphoreType.DMA((2 * slots + 6,)),
        ],
        compiler_params=params(20),
        cost_estimate=pl.CostEstimate(
            flops=flops, bytes_accessed=moved, transcendentals=2 * rows * hidden
        ),
        name="rows_grads",
    )(*xgs, *dys, *weights)


def weights_kernel(j, slots, steps, extra, *refs):
    xg_in, dy_in, act_in = refs[:slots], refs[slots : 2 * slots], refs[2 * slots : 2 * slots + steps]
    refs = refs[2 * slots + steps :]
    more, refs = refs[:extra], refs[extra:]
    gate_out, up_out, down_out = refs[:3]
    x, dy, act, sem = refs[3:]
    tokens, width = dy_in[0].shape
    hidden = act.shape[1] // 3
    step_rows = act_in[0].shape[0]
    copies = []

    def fetch(src, dst):
        copies.append(pltpu.make_async_copy(src, dst, sem.at[len(copies)]))
        copies[-1].start()

    for i in range(steps):
        fetch(
            act_in[i].at[:, pl.ds(j * 3 * hidden, 3 * hidden)],
            act.at[pl.ds(i * step_rows, step_rows)],
        )
    for i in range(slots):
        fetch(xg_in[i].at[:, pl.ds(0, width)], x.at[pl.ds(i * tokens, tokens)])
    for i in range(slots):
        fetch(dy_in[i], dy.at[pl.ds(i * tokens, tokens)])
    for c in copies[: steps + slots]:
        c.wait()

    def put(out, here, value, k):
        if extra:
            value = value + more[k][here].astype(f32)
        if len(out.shape) == 3:
            out[0, here[0], here[1]] = value.astype(out.dtype)
        else:
            out[here[0], here[1]] = value.astype(out.dtype)

    part = math.gcd(width, 256)
    everything = slice(None)
    for m in range(0, width, part):
        here = (slice(m, m + part), everything)
        both = lax.dot_general(
            x[:, m : m + part], act[:, : 2 * hidden], tn, preferred_element_type=f32
        )
        put(gate_out, here, both[:, :hidden], 0)
        put(up_out, here, both[:, hidden:], 1)
    for c in copies[steps + slots :]:
        c.wait()
    part = math.gcd(hidden, 128)
    for m in range(0, hidden, part):
        here = (slice(m, m + part), everything)
        value = lax.dot_general(
            act[:, 2 * hidden + m : 2 * hidden + m + part], dy[...], tn, preferred_element_type=f32
        )
        put(down_out, here, value, 2)


def weights_grads(j, xgs, dys, acts, dtype, more=()):
    slots, steps = len(dys), len(acts)
    tokens, width = dys[0].shape
    hidden = acts[0].shape[1] // 6
    rows = slots * tokens
    lead = (1,) if more else ()
    return pl.pallas_call(
        functools.partial(weights_kernel, j, slots, steps, len(more)),
        out_shape=(
            jax.ShapeDtypeStruct(lead + (width, hidden), dtype),
            jax.ShapeDtypeStruct(lead + (width, hidden), dtype),
            jax.ShapeDtypeStruct(lead + (hidden, width), dtype),
        ),
        in_specs=[ANY] * (2 * slots + steps) + [VMEM] * len(more),
        out_specs=(VMEM,) * 3,
        scratch_shapes=[
            pltpu.VMEM((rows, width), bf16),
            pltpu.VMEM((rows, width), bf16),
            pltpu.VMEM((rows, 3 * hidden), bf16),
            pltpu.SemaphoreType.DMA((2 * slots + steps,)),
        ],
        compiler_params=params(20),
        cost_estimate=pl.CostEstimate(
            flops=6 * rows * width * hidden,
            bytes_accessed=rows * (4 * width + 6 * hidden) + 6 * width * hidden,
            transcendentals=0,
        ),
        name="weights_grads",
    )(*xgs, *dys, *acts, *more)


def finish_kernel(parts, ids, kept, *refs):
    pieces, (tokens_out, gates_out) = refs[:parts], refs[parts:]
    tokens, width = tokens_out.shape
    total = pieces[0][:, :width].astype(f32)
    gg = pieces[0][:, width:].astype(f32)
    for p in pieces[1:]:
        total = total + p[:, :width].astype(f32)
        gg = gg + p[:, width:].astype(f32)
    tokens_out[...] = total.astype(bf16)
    devices = kept.shape[0]
    gg = gg.T[:devices] * kept[...]
    expert = row_iota(devices, tokens)
    place = row_iota(TOP, tokens)
    out = jnp.zeros((TOP, tokens), f32)
    for k in range(TOP):
        value = jnp.sum(jnp.where(expert == ids[k : k + 1], gg, 0.0), axis=0, keepdims=True)
        out = jnp.where(place == k, value, out)
    gates_out[...] = out.astype(bf16)


def finish(ids, kept, pieces, width):
    tokens = ids.shape[1]
    return pl.pallas_call(
        functools.partial(finish_kernel, len(pieces)),
        out_shape=(
            jax.ShapeDtypeStruct((tokens, width), bf16),
            jax.ShapeDtypeStruct((TOP, tokens), bf16),
        ),
        in_specs=[VMEM] * (2 + len(pieces)),
        out_specs=(VMEM, VMEM),
        compiler_params=params(16),
        name="finish",
    )(ids, kept, *pieces)


def add(*terms):
    total = terms[0].astype(f32)
    for t in terms[1:]:
        total = total + t.astype(f32)
    return total.astype(bf16)


def on_device(tokens_in, grad_out, gates, expert_ids, replica_table, w_gate, w_up, w_down):
    devices = lax.axis_size("expert")
    tokens, width = tokens_in.shape
    lanes = -(-devices // LANES) * LANES
    chips = devices // CORES
    inner = 2 ** (int(math.log2(chips)) // 2)
    outer = chips // inner

    def moved(i, dz, dy):
        core, chip = i % CORES, i // CORES
        z, y = chip // inner, chip % inner
        return (((z + dz) % outer) * inner + (y + dy) % inner) * CORES + core

    def send_z(v):
        return lax.ppermute(v, "expert", [(i, moved(i, 1, 0)) for i in range(devices)])

    def send_down(v):
        return lax.ppermute(v, "expert", [(i, moved(i, -1, 0)) for i in range(devices)])

    def send_y(v):
        return lax.ppermute(v, "expert", [(i, moved(i, 0, 1)) for i in range(devices)])

    def send_core(v):
        return lax.ppermute(v, "expert", [(i, i ^ 1) for i in range(devices)])

    def together(*values):
        return lax.optimization_barrier(values)

    ids = expert_ids.T
    xg, kept = plan(replica_table[None], ids, gates.T, tokens_in, devices, lanes)
    own = (w_gate[0], w_up[0], w_down[0])
    own, kept = together(own, kept)
    weights = own + tuple(send_core(w) for w in own)

    per = max(1, W_ROWS // (inner * tokens))
    groups = [range(z, min(outer, z + per)) for z in range(0, outer, per)]
    sums = [None, None]

    def partial(j, group, dtype, more=()):
        return weights_grads(
            j,
            [x for z in group for x in xgs[z]],
            [d for z in group for d in dys[z]],
            [acts[z] for z in group],
            dtype,
            more,
        )

    xgs, dys = [[xg]], [[grad_out]]
    dxs, acts, across = [], [], []

    def send_across(z):
        if inner == 1:
            return []
        total = dxs[z][1]
        for y in range(2, inner):
            total = add(send_y(total), dxs[z][y])
        return [send_y(total)]

    for z in range(1, outer + 1):
        for k, stream in enumerate((xgs, dys)):
            last = stream[z - 1]
            ahead = None
            if z < outer:
                ahead = send_z(last[0])
            for y in range(1, inner):
                if k and z == outer > 1 and y == inner - 1:
                    last.append(send_z(stream[z - 2][y]))
                else:
                    last.append(send_y(last[y - 1]))
            done = [] if ahead is None else [ahead]
            if inner > 1:
                done.append(last[-1])
            if k == 0 and z == 1:
                kept, weights = together(kept, weights)
                done, kept = together(done, hold(kept, HOLD))
            elif k == 0:
                done, acts[z - 2] = together(done, acts[z - 2])
            else:
                (done,) = together(done)
            if inner > 1:
                last[-1] = done.pop()
            if ahead is not None:
                stream.append([done.pop()])
        *dx, act = rows_grads(xgs[z - 1], dys[z - 1], weights)
        dxs.append(dx)
        acts.append(act)
        if z > 2:
            across.append(send_across(z - 1))
        if len(groups) > 1 and z - 1 == groups[(z - 1) // per][-1]:
            for j in range(2):
                value = partial(j, groups[(z - 1) // per], f32)
                sums[j] = value if z <= per else [t + v for t, v in zip(sums[j], value)]
            if z < outer:
                sums, xgs[z] = together(sums, xgs[z])

    single = len(groups) == 1
    if single:
        other = [send_core(v) for v in partial(1, groups[0], bf16)]
    else:
        other = [send_core(v.astype(bf16)) for v in sums[1]]

    pieces = []
    if outer > 1:
        dxs[1], acts[-2] = together(dxs[1], acts[-2])
        back = [send_down(v) for v in dxs[1]]
        pieces.append(back[0])
        dxs[0] = [dxs[0][0]] + [add(v, o) for v, o in zip(dxs[0][1:], back[1:])]
    pieces += [dxs[0][0], *send_across(0)]
    if outer > 2:
        total = add(dxs[2][0], *across[0])
        for z in range(3, outer):
            total = add(send_z(total), dxs[z][0], *across[z - 2])
        total, other = together(total, other)
        pieces.append(send_z(total))
    if single:
        grad_w = partial(0, groups[0], bf16, other)
    else:
        grad_w = [(v + o.astype(f32)).astype(bf16)[None] for v, o in zip(sums[0], other)]
    pieces, grad_w = together(pieces, grad_w)
    grad_tokens, grad_gates = finish(ids, kept, pieces, width)
    grad_gates = grad_gates.T
    return (grad_tokens, grad_gates, *grad_w)


def solution(mesh):
    both = ("groups", "expert")
    return jax.shard_map(
        on_device,
        mesh=mesh,
        in_specs=(
            P(both, None),
            P(both, None),
            P(both, None),
            P(both, None),
            P("groups"),
            P("expert", None, None),
            P("expert", None, None),
            P("expert", None, None),
        ),
        out_specs=(
            P(both, None),
            P(both, None),
            P(both, None, None),
            P(both, None, None),
            P(both, None, None),
        ),
        check_vma=False,
    )
```

```python
import functools
import math

import jax
import jax.numpy as jnp
from jax import lax
from jax.experimental import pallas as pl
from jax.experimental.pallas import tpu as pltpu
from jax.sharding import PartitionSpec as P

TOP = 8
CORES = 2
LANES = 128
ROW_BLOCK = 256
W_ROWS = 1024
HOLD = 10**10
PLAN_MIB = 60

f32 = jnp.float32
bf16 = jnp.bfloat16
nt = (((1,), (1,)), ((), ()))
tn = (((0,), (0,)), ((), ()))
VMEM = pl.BlockSpec(memory_space=pltpu.VMEM)
ANY = pl.BlockSpec(memory_space=pl.ANY)
HBM = pl.BlockSpec(memory_space=pltpu.HBM)


def params(mib):
    return pltpu.CompilerParams(vmem_limit_bytes=mib * 1024 * 1024)


def row_iota(rows, lanes):
    return lax.broadcasted_iota(jnp.int32, (rows, lanes), 0)


def lane_iota(rows, lanes):
    return lax.broadcasted_iota(jnp.int32, (rows, lanes), 1)


def plan_kernel(home_cap, rep_cap, table_in, ids_in, gates_in, x_in, xg, kept_out, *scratch):
    table, ids, gates, sem = scratch
    tokens, width = x_in.shape
    lanes = xg.shape[1] - width
    pairs = (
        (table_in, table),
        (ids_in, ids),
        (gates_in, gates),
        (x_in, xg.at[:, pl.ds(0, width)]),
    )
    copies = [pltpu.make_async_copy(src, dst, sem.at[i]) for i, (src, dst) in enumerate(pairs)]
    for c in copies:
        c.start()
    devices = table.shape[1]
    earlier = row_iota(tokens, tokens) < lane_iota(tokens, tokens)
    earlier = jnp.where(earlier, 1.0, 0.0).astype(bf16)
    expert = row_iota(devices, tokens)
    for c in copies[:3]:
        c.wait()
    hosts = jnp.where(table[...] == row_iota(devices, devices), 1.0, 0.0)
    copied = 1.0 + jnp.sum(hosts, axis=1, keepdims=True)
    named = jnp.zeros((devices, tokens), f32)
    weight = jnp.zeros((devices, tokens), f32)
    for k in range(TOP):
        hit = expert == ids[k : k + 1]
        named = jnp.where(hit, 1.0, named)
        weight = jnp.where(hit, gates[k : k + 1].astype(f32), weight)
    rank = jnp.dot(named.astype(bf16), earlier, preferred_element_type=f32)
    turn = rank + lax.axis_index("expert").astype(f32)
    at_home = turn == copied * jnp.floor(turn / copied + 0.5)
    cap = jnp.where(at_home, float(home_cap), float(rep_cap))
    kept = jnp.where((named > 0.0) & (rank < cap * copied), 1.0, 0.0)
    kept_out[...] = kept
    dense = (weight * kept).T
    if lanes > devices:
        dense = jnp.concatenate([dense, jnp.zeros((tokens, lanes - devices), f32)], axis=1)
    xg[:, width:] = dense.astype(bf16)
    copies[3].wait()


def plan(table, ids, gates, x, devices, lanes):
    tokens, width = x.shape
    home_cap = max(2, 5 * tokens * TOP // (4 * devices))
    rep_cap = max(2, tokens * TOP // (2 * devices))
    return pl.pallas_call(
        functools.partial(plan_kernel, home_cap, rep_cap),
        out_shape=(
            jax.ShapeDtypeStruct((tokens, width + lanes), bf16),
            jax.ShapeDtypeStruct((devices, tokens), f32),
        ),
        in_specs=[HBM] * 4,
        out_specs=(VMEM, VMEM),
        scratch_shapes=[
            pltpu.VMEM(table.shape, jnp.int32),
            pltpu.VMEM(ids.shape, jnp.int32),
            pltpu.VMEM(gates.shape, bf16),
            pltpu.SemaphoreType.DMA((4,)),
        ],
        compiler_params=params(PLAN_MIB),
        name="plan",
    )(table, ids, gates, x)


def hold(value, flops):
    return pl.pallas_call(
        lambda source, out: None,
        out_shape=jax.ShapeDtypeStruct(value.shape, value.dtype),
        in_specs=[ANY],
        out_specs=ANY,
        input_output_aliases={0: 0},
        compiler_params=params(1),
        cost_estimate=pl.CostEstimate(flops=flops, bytes_accessed=1000, transcendentals=0),
        name="hold",
    )(value)


def rows_kernel(slots, *refs):
    xg_in, dy_in = refs[:slots], refs[slots : 2 * slots]
    weights = refs[2 * slots : 2 * slots + 6]
    dxg, act = refs[2 * slots + 6 : 3 * slots + 6], refs[3 * slots + 6]
    xg, dy, w_gu, w_dn, sem = refs[3 * slots + 7 :]
    tokens, width = dy_in[0].shape
    hidden = weights[2].shape[0]
    lanes = xg.shape[1] - width
    copies = []

    def fetch(src, dst):
        copies.append(pltpu.make_async_copy(src, dst, sem.at[len(copies)]))
        copies[-1].start()
        return copies[-1]

    def fetch_weights(j):
        up = [
            fetch(weights[3 * j], w_gu.at[j, :, pl.ds(0, hidden)]),
            fetch(weights[3 * j + 1], w_gu.at[j, :, pl.ds(hidden, hidden)]),
        ]
        return up, [fetch(weights[3 * j + 2], w_dn.at[j])]

    got_x = [fetch(xg_in[i], xg.at[pl.ds(i * tokens, tokens)]) for i in range(slots)]
    own = fetch_weights(0)
    got_dy = [fetch(dy_in[i], dy.at[pl.ds(i * tokens, tokens)]) for i in range(slots)]
    sibling = fetch_weights(1)
    for c in got_x + own[0]:
        c.wait()

    rows = slots * tokens
    block = math.gcd(rows, max(ROW_BLOCK, tokens))
    me = lax.axis_index("expert")
    lane = lane_iota(block, lanes)

    def expert(j, at, after_up):
        here = pl.ds(at, block)
        pre = jnp.dot(xg[here, :width], w_gu[j], preferred_element_type=f32)
        after_up()
        back = lax.dot_general(dy[here, :], w_dn[j], nt, preferred_element_type=f32)
        column = lane == (me if j == 0 else me ^ 1)
        gate = jnp.sum(
            jnp.where(column, xg[here, width:].astype(f32), 0.0), axis=1, keepdims=True
        )
        a, b = pre[:, :hidden], pre[:, hidden:]
        sig = jax.nn.sigmoid(a)
        silu = a * sig
        h = silu * b
        gg = jnp.sum(h.astype(bf16).astype(f32) * back, axis=1, keepdims=True)
        scaled = gate * back
        da = (scaled * b * sig * (1.0 + a * (1.0 - sig))).astype(bf16)
        db = (scaled * silu).astype(bf16)
        grads = jnp.concatenate([da, db], axis=1)
        first = j * 3 * hidden
        act[here, first : first + 2 * hidden] = grads
        act[here, first + 2 * hidden : first + 3 * hidden] = (gate * h).astype(bf16)
        dx = lax.dot_general(grads, w_gu[j], nt, preferred_element_type=f32)
        return dx, jnp.where(column, gg, 0.0)

    def wait_all(group):
        for c in group:
            c.wait()

    for at in range(0, rows, block):
        first = at == 0
        dx0, gg0 = expert(0, at, lambda: wait_all(got_dy + own[1]) if first else None)
        if first:
            wait_all(sibling[0] + sibling[1])
        dx1, gg1 = expert(1, at, lambda: None)
        dx = (dx0 + dx1).astype(bf16)
        gg = (gg0 + gg1).astype(bf16)
        for i in range(block // tokens):
            out = dxg[at // tokens + i]
            part = slice(i * tokens, (i + 1) * tokens)
            out[:, :width] = dx[part]
            out[:, width:] = gg[part]


def rows_grads(xgs, dys, weights):
    slots = len(dys)
    tokens, width = dys[0].shape
    full = xgs[0].shape[1]
    hidden = weights[2].shape[0]
    rows = slots * tokens
    flops = 2 * rows * 2 * 5 * width * hidden
    moved = 4 * rows * (width + full) + 12 * width * hidden + 4 * rows * full + 12 * rows * hidden
    return pl.pallas_call(
        functools.partial(rows_kernel, slots),
        out_shape=tuple(jax.ShapeDtypeStruct((tokens, full), bf16) for _ in dys)
        + (jax.ShapeDtypeStruct((rows, 6 * hidden), bf16),),
        in_specs=[ANY] * (2 * slots + 6),
        out_specs=(VMEM,) * (slots + 1),
        scratch_shapes=[
            pltpu.VMEM((rows, full), bf16),
            pltpu.VMEM((rows, width), bf16),
            pltpu.VMEM((2, width, 2 * hidden), bf16),
            pltpu.VMEM((2, hidden, width), bf16),
            pltpu.SemaphoreType.DMA((2 * slots + 6,)),
        ],
        compiler_params=params(20),
        cost_estimate=pl.CostEstimate(
            flops=flops, bytes_accessed=moved, transcendentals=2 * rows * hidden
        ),
        name="rows_grads",
    )(*xgs, *dys, *weights)


def weights_kernel(j, slots, steps, extra, *refs):
    xg_in, dy_in, act_in = refs[:slots], refs[slots : 2 * slots], refs[2 * slots : 2 * slots + steps]
    refs = refs[2 * slots + steps :]
    more, refs = refs[:extra], refs[extra:]
    gate_out, up_out, down_out = refs[:3]
    x, dy, act, sem = refs[3:]
    tokens, width = dy_in[0].shape
    hidden = act.shape[1] // 3
    step_rows = act_in[0].shape[0]
    copies = []

    def fetch(src, dst):
        copies.append(pltpu.make_async_copy(src, dst, sem.at[len(copies)]))
        copies[-1].start()

    for i in range(steps):
        fetch(
            act_in[i].at[:, pl.ds(j * 3 * hidden, 3 * hidden)],
            act.at[pl.ds(i * step_rows, step_rows)],
        )
    for i in range(slots):
        fetch(xg_in[i].at[:, pl.ds(0, width)], x.at[pl.ds(i * tokens, tokens)])
    for i in range(slots):
        fetch(dy_in[i], dy.at[pl.ds(i * tokens, tokens)])
    for c in copies[: steps + slots]:
        c.wait()

    def put(out, here, value, k):
        if extra:
            value = value + more[k][here].astype(f32)
        if len(out.shape) == 3:
            out[0, here[0], here[1]] = value.astype(out.dtype)
        else:
            out[here[0], here[1]] = value.astype(out.dtype)

    part = math.gcd(width, 256)
    everything = slice(None)
    for m in range(0, width, part):
        here = (slice(m, m + part), everything)
        both = lax.dot_general(
            x[:, m : m + part], act[:, : 2 * hidden], tn, preferred_element_type=f32
        )
        put(gate_out, here, both[:, :hidden], 0)
        put(up_out, here, both[:, hidden:], 1)
    for c in copies[steps + slots :]:
        c.wait()
    part = math.gcd(hidden, 128)
    for m in range(0, hidden, part):
        here = (slice(m, m + part), everything)
        value = lax.dot_general(
            act[:, 2 * hidden + m : 2 * hidden + m + part], dy[...], tn, preferred_element_type=f32
        )
        put(down_out, here, value, 2)


def weights_grads(j, xgs, dys, acts, dtype, more=()):
    slots, steps = len(dys), len(acts)
    tokens, width = dys[0].shape
    hidden = acts[0].shape[1] // 6
    rows = slots * tokens
    lead = (1,) if more else ()
    return pl.pallas_call(
        functools.partial(weights_kernel, j, slots, steps, len(more)),
        out_shape=(
            jax.ShapeDtypeStruct(lead + (width, hidden), dtype),
            jax.ShapeDtypeStruct(lead + (width, hidden), dtype),
            jax.ShapeDtypeStruct(lead + (hidden, width), dtype),
        ),
        in_specs=[ANY] * (2 * slots + steps) + [VMEM] * len(more),
        out_specs=(VMEM,) * 3,
        scratch_shapes=[
            pltpu.VMEM((rows, width), bf16),
            pltpu.VMEM((rows, width), bf16),
            pltpu.VMEM((rows, 3 * hidden), bf16),
            pltpu.SemaphoreType.DMA((2 * slots + steps,)),
        ],
        compiler_params=params(20),
        cost_estimate=pl.CostEstimate(
            flops=6 * rows * width * hidden,
            bytes_accessed=rows * (4 * width + 6 * hidden) + 6 * width * hidden,
            transcendentals=0,
        ),
        name="weights_grads",
    )(*xgs, *dys, *acts, *more)


def finish_kernel(parts, ids, kept, *refs):
    pieces, (tokens_out, gates_out) = refs[:parts], refs[parts:]
    tokens, width = tokens_out.shape
    total = pieces[0][:, :width].astype(f32)
    gg = pieces[0][:, width:].astype(f32)
    for p in pieces[1:]:
        total = total + p[:, :width].astype(f32)
        gg = gg + p[:, width:].astype(f32)
    tokens_out[...] = total.astype(bf16)
    devices = kept.shape[0]
    gg = gg.T[:devices] * kept[...]
    expert = row_iota(devices, tokens)
    place = row_iota(TOP, tokens)
    out = jnp.zeros((TOP, tokens), f32)
    for k in range(TOP):
        value = jnp.sum(jnp.where(expert == ids[k : k + 1], gg, 0.0), axis=0, keepdims=True)
        out = jnp.where(place == k, value, out)
    gates_out[...] = out.astype(bf16)


def finish(ids, kept, pieces, width):
    tokens = ids.shape[1]
    return pl.pallas_call(
        functools.partial(finish_kernel, len(pieces)),
        out_shape=(
            jax.ShapeDtypeStruct((tokens, width), bf16),
            jax.ShapeDtypeStruct((TOP, tokens), bf16),
        ),
        in_specs=[VMEM] * (2 + len(pieces)),
        out_specs=(VMEM, VMEM),
        compiler_params=params(16),
        name="finish",
    )(ids, kept, *pieces)


def add(*terms):
    total = terms[0].astype(f32)
    for t in terms[1:]:
        total = total + t.astype(f32)
    return total.astype(bf16)


def on_device(tokens_in, grad_out, gates, expert_ids, replica_table, w_gate, w_up, w_down):
    devices = lax.axis_size("expert")
    tokens, width = tokens_in.shape
    lanes = -(-devices // LANES) * LANES
    chips = devices // CORES
    inner = 2 ** (int(math.log2(chips)) // 2)
    outer = chips // inner

    def moved(i, dz, dy):
        core, chip = i % CORES, i // CORES
        z, y = chip // inner, chip % inner
        return (((z + dz) % outer) * inner + (y + dy) % inner) * CORES + core

    def send_z(v):
        return lax.ppermute(v, "expert", [(i, moved(i, 1, 0)) for i in range(devices)])

    def send_down(v):
        return lax.ppermute(v, "expert", [(i, moved(i, -1, 0)) for i in range(devices)])

    def send_y(v):
        return lax.ppermute(v, "expert", [(i, moved(i, 0, 1)) for i in range(devices)])

    def send_core(v):
        return lax.ppermute(v, "expert", [(i, i ^ 1) for i in range(devices)])

    def together(*values):
        return lax.optimization_barrier(values)

    ids = expert_ids.T
    xg, kept = plan(replica_table[None], ids, gates.T, tokens_in, devices, lanes)
    own = (w_gate[0], w_up[0], w_down[0])
    own, kept = together(own, kept)
    weights = own + tuple(send_core(w) for w in own)

    per = max(1, W_ROWS // (inner * tokens))
    groups = [range(z, min(outer, z + per)) for z in range(0, outer, per)]
    sums = [None, None]

    def partial(j, group, dtype, more=()):
        return weights_grads(
            j,
            [x for z in group for x in xgs[z]],
            [d for z in group for d in dys[z]],
            [acts[z] for z in group],
            dtype,
            more,
        )

    xgs, dys = [[xg]], [[grad_out]]
    dxs, acts, across = [], [], []

    def send_across(z):
        if inner == 1:
            return []
        total = dxs[z][1]
        for y in range(2, inner):
            total = add(send_y(total), dxs[z][y])
        return [send_y(total)]

    for z in range(1, outer + 1):
        for k, stream in enumerate((xgs, dys)):
            last = stream[z - 1]
            ahead = None
            if z < outer:
                ahead = send_z(last[0])
            for y in range(1, inner):
                if k and z == outer > 1 and y == inner - 1:
                    last.append(send_z(stream[z - 2][y]))
                else:
                    last.append(send_y(last[y - 1]))
            done = [] if ahead is None else [ahead]
            if inner > 1:
                done.append(last[-1])
            if k == 0 and z == 1:
                kept, weights = together(kept, weights)
                done, kept = together(done, hold(kept, HOLD))
            elif k == 0:
                done, acts[z - 2] = together(done, acts[z - 2])
            else:
                (done,) = together(done)
            if inner > 1:
                last[-1] = done.pop()
            if ahead is not None:
                stream.append([done.pop()])
        *dx, act = rows_grads(xgs[z - 1], dys[z - 1], weights)
        dxs.append(dx)
        acts.append(act)
        if z > 2:
            across.append(send_across(z - 1))
        if len(groups) > 1 and z - 1 == groups[(z - 1) // per][-1]:
            for j in range(2):
                value = partial(j, groups[(z - 1) // per], f32)
                sums[j] = value if z <= per else [t + v for t, v in zip(sums[j], value)]
            if z < outer:
                sums, xgs[z] = together(sums, xgs[z])

    single = len(groups) == 1
    if single:
        other = [send_core(v) for v in partial(1, groups[0], bf16)]
    else:
        other = [send_core(v.astype(bf16)) for v in sums[1]]

    pieces = []
    if outer > 1:
        dxs[1], acts[-2] = together(dxs[1], acts[-2])
        back = [send_down(v) for v in dxs[1]]
        pieces.append(back[0])
        dxs[0] = [dxs[0][0]] + [add(v, o) for v, o in zip(dxs[0][1:], back[1:])]
    pieces += [dxs[0][0], *send_across(0)]
    if outer > 2:
        total = add(dxs[2][0], *across[0])
        for z in range(3, outer):
            total = add(send_z(total), dxs[z][0], *across[z - 2])
        total, other = together(total, other)
        pieces.append(send_z(total))
    if single:
        grad_w = partial(0, groups[0], bf16, other)
    else:
        grad_w = [(v + o.astype(f32)).astype(bf16)[None] for v, o in zip(sums[0], other)]
    pieces, grad_w = together(pieces, grad_w)
    grad_tokens, grad_gates = finish(ids, kept, pieces, width)
    grad_gates = grad_gates.T
    return (grad_tokens, grad_gates, *grad_w)


def solution(mesh):
    both = ("groups", "expert")
    return jax.shard_map(
        on_device,
        mesh=mesh,
        in_specs=(
            P(both, None),
            P(both, None),
            P(both, None),
            P(both, None),
            P("groups"),
            P("expert", None, None),
            P("expert", None, None),
            P("expert", None, None),
        ),
        out_specs=(
            P(both, None),
            P(both, None),
            P(both, None, None),
            P(both, None, None),
            P(both, None, None),
        ),
        check_vma=False,
    )
```

```python
import functools
import math

import jax
import jax.numpy as jnp
from jax import lax
from jax.experimental import pallas as pl
from jax.experimental.pallas import tpu as pltpu
from jax.sharding import PartitionSpec as P

TOP = 8
CORES = 2
LANES = 128
ROW_BLOCK = 256
W_ROWS = 1024
HOLD = 10**10
PLAN_MIB = 60

f32 = jnp.float32
bf16 = jnp.bfloat16
nt = (((1,), (1,)), ((), ()))
tn = (((0,), (0,)), ((), ()))
VMEM = pl.BlockSpec(memory_space=pltpu.VMEM)
ANY = pl.BlockSpec(memory_space=pl.ANY)
HBM = pl.BlockSpec(memory_space=pltpu.HBM)


def params(mib):
    return pltpu.CompilerParams(vmem_limit_bytes=mib * 1024 * 1024)


def row_iota(rows, lanes):
    return lax.broadcasted_iota(jnp.int32, (rows, lanes), 0)


def lane_iota(rows, lanes):
    return lax.broadcasted_iota(jnp.int32, (rows, lanes), 1)


def plan_kernel(home_cap, rep_cap, table_in, ids_in, gates_in, x_in, xg, kept_out, *scratch):
    table, ids, gates, sem = scratch
    tokens, width = x_in.shape
    lanes = xg.shape[1] - width
    pairs = (
        (table_in, table),
        (ids_in, ids),
        (gates_in, gates),
        (x_in, xg.at[:, pl.ds(0, width)]),
    )
    copies = [pltpu.make_async_copy(src, dst, sem.at[i]) for i, (src, dst) in enumerate(pairs)]
    for c in copies:
        c.start()
    devices = table.shape[1]
    earlier = row_iota(tokens, tokens) < lane_iota(tokens, tokens)
    earlier = jnp.where(earlier, 1.0, 0.0).astype(bf16)
    expert = row_iota(devices, tokens)
    for c in copies[:3]:
        c.wait()
    hosts = jnp.where(table[...] == row_iota(devices, devices), 1.0, 0.0)
    copied = 1.0 + jnp.sum(hosts, axis=1, keepdims=True)
    named = jnp.zeros((devices, tokens), f32)
    weight = jnp.zeros((devices, tokens), f32)
    for k in range(TOP):
        hit = expert == ids[k : k + 1]
        named = jnp.where(hit, 1.0, named)
        weight = jnp.where(hit, gates[k : k + 1].astype(f32), weight)
    rank = jnp.dot(named.astype(bf16), earlier, preferred_element_type=f32)
    turn = rank + lax.axis_index("expert").astype(f32)
    at_home = turn == copied * jnp.floor(turn / copied + 0.5)
    cap = jnp.where(at_home, float(home_cap), float(rep_cap))
    kept = jnp.where((named > 0.0) & (rank < cap * copied), 1.0, 0.0)
    kept_out[...] = kept
    dense = (weight * kept).T
    if lanes > devices:
        dense = jnp.concatenate([dense, jnp.zeros((tokens, lanes - devices), f32)], axis=1)
    xg[:, width:] = dense.astype(bf16)
    copies[3].wait()


def plan(table, ids, gates, x, devices, lanes):
    tokens, width = x.shape
    home_cap = max(2, 5 * tokens * TOP // (4 * devices))
    rep_cap = max(2, tokens * TOP // (2 * devices))
    return pl.pallas_call(
        functools.partial(plan_kernel, home_cap, rep_cap),
        out_shape=(
            jax.ShapeDtypeStruct((tokens, width + lanes), bf16),
            jax.ShapeDtypeStruct((devices, tokens), f32),
        ),
        in_specs=[HBM] * 4,
        out_specs=(VMEM, VMEM),
        scratch_shapes=[
            pltpu.VMEM(table.shape, jnp.int32),
            pltpu.VMEM(ids.shape, jnp.int32),
            pltpu.VMEM(gates.shape, bf16),
            pltpu.SemaphoreType.DMA((4,)),
        ],
        compiler_params=params(PLAN_MIB),
        name="plan",
    )(table, ids, gates, x)


def hold(value, flops):
    return pl.pallas_call(
        lambda source, out: None,
        out_shape=jax.ShapeDtypeStruct(value.shape, value.dtype),
        in_specs=[ANY],
        out_specs=ANY,
        input_output_aliases={0: 0},
        compiler_params=params(1),
        cost_estimate=pl.CostEstimate(flops=flops, bytes_accessed=1000, transcendentals=0),
        name="hold",
    )(value)


def rows_kernel(slots, *refs):
    xg, dy = refs[:slots], refs[slots : 2 * slots]
    weights = refs[2 * slots : 2 * slots + 6]
    dxg, act = refs[2 * slots + 6 : 3 * slots + 6], refs[3 * slots + 6]
    tokens, width = dy[0].shape
    hidden = weights[2].shape[0]
    lanes = xg[0].shape[1] - width
    per = max(1, ROW_BLOCK // tokens)
    me = lax.axis_index("expert")

    def stack(parts):
        return parts[0] if len(parts) == 1 else jnp.concatenate(parts, axis=0)

    for at in range(0, slots, per):
        group = range(at, min(slots, at + per))
        x = stack([xg[i][:, :width] for i in group])
        up_grad = stack([dy[i][...] for i in group])
        gates = stack([xg[i][:, width:].astype(f32) for i in group])
        here = pl.ds(at * tokens, len(group) * tokens)
        lane = lane_iota(len(group) * tokens, lanes)
        dx, gg = 0.0, 0.0
        for j in range(2):
            w_gate, w_up, w_down = weights[3 * j : 3 * j + 3]
            a = jnp.dot(x, w_gate[...], preferred_element_type=f32)
            b = jnp.dot(x, w_up[...], preferred_element_type=f32)
            back = lax.dot_general(up_grad, w_down[...], nt, preferred_element_type=f32)
            column = lane == (me if j == 0 else me ^ 1)
            gate = jnp.sum(jnp.where(column, gates, 0.0), axis=1, keepdims=True)
            sig = jax.nn.sigmoid(a)
            silu = a * sig
            h = silu * b
            dots = jnp.sum(h.astype(bf16).astype(f32) * back, axis=1, keepdims=True)
            scaled = gate * back
            da = (scaled * b * sig * (1.0 + a * (1.0 - sig))).astype(bf16)
            db = (scaled * silu).astype(bf16)
            first = j * 3 * hidden
            act[here, first : first + hidden] = da
            act[here, first + hidden : first + 2 * hidden] = db
            act[here, first + 2 * hidden : first + 3 * hidden] = (gate * h).astype(bf16)
            dx += lax.dot_general(da, w_gate[...], nt, preferred_element_type=f32)
            dx += lax.dot_general(db, w_up[...], nt, preferred_element_type=f32)
            gg += jnp.where(column, dots, 0.0)
        for k, i in enumerate(group):
            part = slice(k * tokens, (k + 1) * tokens)
            dxg[i][:, :width] = dx[part].astype(bf16)
            dxg[i][:, width:] = gg[part].astype(bf16)


def rows_grads(xgs, dys, weights):
    slots = len(dys)
    tokens, width = dys[0].shape
    full = xgs[0].shape[1]
    hidden = weights[2].shape[0]
    rows = slots * tokens
    flops = 2 * rows * 2 * 5 * width * hidden
    moved = 4 * rows * (width + full) + 12 * width * hidden + 4 * rows * full + 12 * rows * hidden
    return pl.pallas_call(
        functools.partial(rows_kernel, slots),
        out_shape=tuple(jax.ShapeDtypeStruct((tokens, full), bf16) for _ in dys)
        + (jax.ShapeDtypeStruct((rows, 6 * hidden), bf16),),
        in_specs=[VMEM] * (2 * slots + 6),
        out_specs=(VMEM,) * (slots + 1),
        compiler_params=params(20),
        cost_estimate=pl.CostEstimate(
            flops=flops, bytes_accessed=moved, transcendentals=2 * rows * hidden
        ),
        name="rows_grads",
    )(*xgs, *dys, *weights)


def weights_kernel(j, slots, steps, extra, *refs):
    xg_in, dy_in, act_in = refs[:slots], refs[slots : 2 * slots], refs[2 * slots : 2 * slots + steps]
    refs = refs[2 * slots + steps :]
    more, refs = refs[:extra], refs[extra:]
    gate_out, up_out, down_out = refs[:3]
    x, dy, act, sem = refs[3:]
    tokens, width = dy_in[0].shape
    hidden = act.shape[1] // 3
    copies = []

    def fetch(src, dst):
        copies.append(pltpu.make_async_copy(src, dst, sem.at[len(copies)]))
        copies[-1].start()

    row = 0
    for i in range(steps):
        step_rows = act_in[i].shape[0]
        fetch(
            act_in[i].at[:, pl.ds(j * 3 * hidden, 3 * hidden)],
            act.at[pl.ds(row, step_rows)],
        )
        row += step_rows
    for i in range(slots):
        fetch(xg_in[i].at[:, pl.ds(0, width)], x.at[pl.ds(i * tokens, tokens)])
    for i in range(slots):
        fetch(dy_in[i], dy.at[pl.ds(i * tokens, tokens)])
    for c in copies[: steps + slots]:
        c.wait()

    def put(out, here, value, k):
        if extra:
            value = value + more[k][here].astype(f32)
        if len(out.shape) == 3:
            out[0, here[0], here[1]] = value.astype(out.dtype)
        else:
            out[here[0], here[1]] = value.astype(out.dtype)

    part = math.gcd(width, 256)
    everything = slice(None)
    for m in range(0, width, part):
        here = (slice(m, m + part), everything)
        both = lax.dot_general(
            x[:, m : m + part], act[:, : 2 * hidden], tn, preferred_element_type=f32
        )
        put(gate_out, here, both[:, :hidden], 0)
        put(up_out, here, both[:, hidden:], 1)
    for c in copies[steps + slots :]:
        c.wait()
    part = math.gcd(hidden, 128)
    for m in range(0, hidden, part):
        here = (slice(m, m + part), everything)
        value = lax.dot_general(
            act[:, 2 * hidden + m : 2 * hidden + m + part], dy[...], tn, preferred_element_type=f32
        )
        put(down_out, here, value, 2)


def weights_grads(j, xgs, dys, acts, dtype, more=()):
    slots, steps = len(dys), len(acts)
    tokens, width = dys[0].shape
    hidden = acts[0].shape[1] // 6
    rows = slots * tokens
    lead = (1,) if more else ()
    return pl.pallas_call(
        functools.partial(weights_kernel, j, slots, steps, len(more)),
        out_shape=(
            jax.ShapeDtypeStruct(lead + (width, hidden), dtype),
            jax.ShapeDtypeStruct(lead + (width, hidden), dtype),
            jax.ShapeDtypeStruct(lead + (hidden, width), dtype),
        ),
        in_specs=[ANY] * (2 * slots + steps) + [VMEM] * len(more),
        out_specs=(VMEM,) * 3,
        scratch_shapes=[
            pltpu.VMEM((rows, width), bf16),
            pltpu.VMEM((rows, width), bf16),
            pltpu.VMEM((rows, 3 * hidden), bf16),
            pltpu.SemaphoreType.DMA((2 * slots + steps,)),
        ],
        compiler_params=params(20),
        cost_estimate=pl.CostEstimate(
            flops=6 * rows * width * hidden,
            bytes_accessed=rows * (4 * width + 6 * hidden) + 6 * width * hidden,
            transcendentals=0,
        ),
        name="weights_grads",
    )(*xgs, *dys, *acts, *more)


def finish_kernel(parts, ids, kept, *refs):
    pieces, (tokens_out, gates_out) = refs[:parts], refs[parts:]
    tokens, width = tokens_out.shape
    total = pieces[0][:, :width].astype(f32)
    gg = pieces[0][:, width:].astype(f32)
    for p in pieces[1:]:
        total = total + p[:, :width].astype(f32)
        gg = gg + p[:, width:].astype(f32)
    tokens_out[...] = total.astype(bf16)
    devices = kept.shape[0]
    gg = gg.T[:devices] * kept[...]
    expert = row_iota(devices, tokens)
    place = row_iota(TOP, tokens)
    out = jnp.zeros((TOP, tokens), f32)
    for k in range(TOP):
        value = jnp.sum(jnp.where(expert == ids[k : k + 1], gg, 0.0), axis=0, keepdims=True)
        out = jnp.where(place == k, value, out)
    gates_out[...] = out.astype(bf16)


def finish(ids, kept, pieces, width):
    tokens = ids.shape[1]
    return pl.pallas_call(
        functools.partial(finish_kernel, len(pieces)),
        out_shape=(
            jax.ShapeDtypeStruct((tokens, width), bf16),
            jax.ShapeDtypeStruct((TOP, tokens), bf16),
        ),
        in_specs=[VMEM] * (2 + len(pieces)),
        out_specs=(VMEM, VMEM),
        compiler_params=params(16),
        name="finish",
    )(ids, kept, *pieces)


def add(*terms):
    total = terms[0].astype(f32)
    for t in terms[1:]:
        total = total + t.astype(f32)
    return total.astype(bf16)


def on_device(tokens_in, grad_out, gates, expert_ids, replica_table, w_gate, w_up, w_down):
    devices = lax.axis_size("expert")
    tokens, width = tokens_in.shape
    lanes = -(-devices // LANES) * LANES
    chips = devices // CORES
    inner = 2 ** (int(math.log2(chips)) // 2)
    outer = chips // inner

    def moved(i, dz, dy):
        core, chip = i % CORES, i // CORES
        z, y = chip // inner, chip % inner
        return (((z + dz) % outer) * inner + (y + dy) % inner) * CORES + core

    def send_z(v):
        return lax.ppermute(v, "expert", [(i, moved(i, 1, 0)) for i in range(devices)])

    def send_down(v):
        return lax.ppermute(v, "expert", [(i, moved(i, -1, 0)) for i in range(devices)])

    def send_y(v):
        return lax.ppermute(v, "expert", [(i, moved(i, 0, 1)) for i in range(devices)])

    def send_core(v):
        return lax.ppermute(v, "expert", [(i, i ^ 1) for i in range(devices)])

    def together(*values):
        return lax.optimization_barrier(values)

    ids = expert_ids.T
    xg, kept = plan(replica_table[None], ids, gates.T, tokens_in, devices, lanes)
    own = (w_gate[0], w_up[0], w_down[0])
    weights = own + tuple(send_core(w) for w in own)

    per = max(1, W_ROWS // (inner * tokens))
    groups = [range(z, min(outer, z + per)) for z in range(0, outer, per)]
    sums = [None, None]

    def partial(j, group, dtype, more=()):
        return weights_grads(
            j,
            [x for z in group for x in xgs[z]],
            [d for z in group for d in dys[z]],
            [act for z in group for act in acts[z]],
            dtype,
            more,
        )

    xgs, dys = [[xg]], [[grad_out]]
    dxs, acts, across = [], [], []

    def send_across(z):
        if inner == 1:
            return []
        total = dxs[z][1]
        for y in range(2, inner):
            total = add(send_y(total), dxs[z][y])
        return [send_y(total)]

    for z in range(1, outer + 1):
        for k, stream in enumerate((xgs, dys)):
            last = stream[z - 1]
            ahead = None
            if z < outer:
                ahead = send_z(last[0])
            for y in range(1, inner):
                if k == 0 and z == outer > 1 and y == inner - 1:
                    last.append(send_z(stream[z - 2][y]))
                else:
                    last.append(send_y(last[y - 1]))
            done = [] if ahead is None else [ahead]
            if inner > 1:
                done.append(last[-1])
            if k == 0 and z == 1:
                done, weights = together(done, weights)
            elif z == 1:
                done, kept = together(done, hold(kept, HOLD))
            elif k == 0:
                done, acts[z - 2] = together(done, acts[z - 2])
            else:
                (done,) = together(done)
            if inner > 1:
                last[-1] = done.pop()
            if ahead is not None:
                stream.append([done.pop()])
        cut = inner - 1 if z > 2 else inner
        dxs.append([])
        acts.append([])
        for part in (slice(0, cut), slice(cut, inner)):
            if xgs[z - 1][part]:
                *dx, act = rows_grads(xgs[z - 1][part], dys[z - 1][part], weights)
                dxs[-1] += dx
                acts[-1].append(act)
        if z > 2:
            across.append(send_across(z - 1))
        if len(groups) > 1 and z - 1 == groups[(z - 1) // per][-1]:
            for j in range(2):
                value = partial(j, groups[(z - 1) // per], f32)
                sums[j] = value if z <= per else [t + v for t, v in zip(sums[j], value)]
            if z < outer:
                sums, xgs[z] = together(sums, xgs[z])

    single = len(groups) == 1
    if single:
        other = [send_core(v) for v in partial(1, groups[0], bf16)]
    else:
        other = [send_core(v.astype(bf16)) for v in sums[1]]

    pieces = []
    if outer > 1:
        dxs[1], acts[-2] = together(dxs[1], acts[-2])
        back = [send_down(v) for v in dxs[1]]
        pieces.append(back[0])
        dxs[0] = [dxs[0][0]] + [add(v, o) for v, o in zip(dxs[0][1:], back[1:])]
    pieces += [dxs[0][0], *send_across(0)]
    if outer > 2:
        total = add(dxs[2][0], *across[0])
        for z in range(3, outer):
            total = add(send_z(total), dxs[z][0], *across[z - 2])
        total, other = together(total, other)
        pieces.append(send_z(total))
    if single:
        grad_w = partial(0, groups[0], bf16, other)
    else:
        grad_w = [(v + o.astype(f32)).astype(bf16)[None] for v, o in zip(sums[0], other)]
    pieces, grad_w = together(pieces, grad_w)
    grad_tokens, grad_gates = finish(ids, kept, pieces, width)
    grad_gates = grad_gates.T
    return (grad_tokens, grad_gates, *grad_w)


def solution(mesh):
    both = ("groups", "expert")
    return jax.shard_map(
        on_device,
        mesh=mesh,
        in_specs=(
            P(both, None),
            P(both, None),
            P(both, None),
            P(both, None),
            P("groups"),
            P("expert", None, None),
            P("expert", None, None),
            P("expert", None, None),
        ),
        out_specs=(
            P(both, None),
            P(both, None),
            P(both, None, None),
            P(both, None, None),
            P(both, None, None),
        ),
        check_vma=False,
    )
```

```python
import functools
import math

import jax
import jax.numpy as jnp
from jax import lax
from jax.experimental import pallas as pl
from jax.experimental.pallas import tpu as pltpu
from jax.sharding import PartitionSpec as P

TOP = 8
CORES = 2
LANES = 128
ROW_BLOCK = 256
W_ROWS = 1024
HOLD = 10**10
PLAN_MIB = 60

f32 = jnp.float32
bf16 = jnp.bfloat16
nt = (((1,), (1,)), ((), ()))
tn = (((0,), (0,)), ((), ()))
VMEM = pl.BlockSpec(memory_space=pltpu.VMEM)
ANY = pl.BlockSpec(memory_space=pl.ANY)
HBM = pl.BlockSpec(memory_space=pltpu.HBM)


def params(mib):
    return pltpu.CompilerParams(vmem_limit_bytes=mib * 1024 * 1024)


def row_iota(rows, lanes):
    return lax.broadcasted_iota(jnp.int32, (rows, lanes), 0)


def lane_iota(rows, lanes):
    return lax.broadcasted_iota(jnp.int32, (rows, lanes), 1)


def plan_kernel(home_cap, rep_cap, table_in, ids_in, gates_in, x_in, xg, kept_out, *scratch):
    table, ids, gates, sem = scratch
    tokens, width = x_in.shape
    lanes = xg.shape[1] - width
    pairs = (
        (table_in, table),
        (ids_in, ids),
        (gates_in, gates),
        (x_in, xg.at[:, pl.ds(0, width)]),
    )
    copies = [pltpu.make_async_copy(src, dst, sem.at[i]) for i, (src, dst) in enumerate(pairs)]
    for c in copies:
        c.start()
    devices = table.shape[1]
    earlier = row_iota(tokens, tokens) < lane_iota(tokens, tokens)
    earlier = jnp.where(earlier, 1.0, 0.0).astype(bf16)
    expert = row_iota(devices, tokens)
    for c in copies[:3]:
        c.wait()
    hosts = jnp.where(table[...] == row_iota(devices, devices), 1.0, 0.0)
    copied = 1.0 + jnp.sum(hosts, axis=1, keepdims=True)
    named = jnp.zeros((devices, tokens), f32)
    weight = jnp.zeros((devices, tokens), f32)
    for k in range(TOP):
        hit = expert == ids[k : k + 1]
        named = jnp.where(hit, 1.0, named)
        weight = jnp.where(hit, gates[k : k + 1].astype(f32), weight)
    rank = jnp.dot(named.astype(bf16), earlier, preferred_element_type=f32)
    turn = rank + lax.axis_index("expert").astype(f32)
    at_home = turn == copied * jnp.floor(turn / copied + 0.5)
    cap = jnp.where(at_home, float(home_cap), float(rep_cap))
    kept = jnp.where((named > 0.0) & (rank < cap * copied), 1.0, 0.0)
    kept_out[...] = kept
    dense = (weight * kept).T
    if lanes > devices:
        dense = jnp.concatenate([dense, jnp.zeros((tokens, lanes - devices), f32)], axis=1)
    xg[:, width:] = dense.astype(bf16)
    copies[3].wait()


def plan(table, ids, gates, x, devices, lanes):
    tokens, width = x.shape
    home_cap = max(2, 5 * tokens * TOP // (4 * devices))
    rep_cap = max(2, tokens * TOP // (2 * devices))
    return pl.pallas_call(
        functools.partial(plan_kernel, home_cap, rep_cap),
        out_shape=(
            jax.ShapeDtypeStruct((tokens, width + lanes), bf16),
            jax.ShapeDtypeStruct((devices, tokens), f32),
        ),
        in_specs=[HBM] * 4,
        out_specs=(VMEM, VMEM),
        scratch_shapes=[
            pltpu.VMEM(table.shape, jnp.int32),
            pltpu.VMEM(ids.shape, jnp.int32),
            pltpu.VMEM(gates.shape, bf16),
            pltpu.SemaphoreType.DMA((4,)),
        ],
        compiler_params=params(PLAN_MIB),
        name="plan",
    )(table, ids, gates, x)


def hold(value, flops):
    return pl.pallas_call(
        lambda source, out: None,
        out_shape=jax.ShapeDtypeStruct(value.shape, value.dtype),
        in_specs=[ANY],
        out_specs=ANY,
        input_output_aliases={0: 0},
        compiler_params=params(1),
        cost_estimate=pl.CostEstimate(flops=flops, bytes_accessed=1000, transcendentals=0),
        name="hold",
    )(value)


def rows_kernel(slots, *refs):
    xg, dy = refs[:slots], refs[slots : 2 * slots]
    weights = refs[2 * slots : 2 * slots + 6]
    dxg, act = refs[2 * slots + 6 : 3 * slots + 6], refs[3 * slots + 6]
    tokens, width = dy[0].shape
    hidden = weights[2].shape[0]
    lanes = xg[0].shape[1] - width
    per = max(1, ROW_BLOCK // tokens)
    me = lax.axis_index("expert")

    def stack(parts):
        return parts[0] if len(parts) == 1 else jnp.concatenate(parts, axis=0)

    for at in range(0, slots, per):
        group = range(at, min(slots, at + per))
        x = stack([xg[i][:, :width] for i in group])
        up_grad = stack([dy[i][...] for i in group])
        gates = stack([xg[i][:, width:].astype(f32) for i in group])
        here = pl.ds(at * tokens, len(group) * tokens)
        lane = lane_iota(len(group) * tokens, lanes)
        dx, gg = 0.0, 0.0
        for j in range(2):
            w_gate, w_up, w_down = weights[3 * j : 3 * j + 3]
            a = jnp.dot(x, w_gate[...], preferred_element_type=f32)
            b = jnp.dot(x, w_up[...], preferred_element_type=f32)
            back = lax.dot_general(up_grad, w_down[...], nt, preferred_element_type=f32)
            column = lane == (me if j == 0 else me ^ 1)
            gate = jnp.sum(jnp.where(column, gates, 0.0), axis=1, keepdims=True)
            sig = jax.nn.sigmoid(a)
            silu = a * sig
            h = silu * b
            dots = jnp.sum(h.astype(bf16).astype(f32) * back, axis=1, keepdims=True)
            scaled = gate * back
            da = (scaled * b * sig * (1.0 + a * (1.0 - sig))).astype(bf16)
            db = (scaled * silu).astype(bf16)
            first = j * 3 * hidden
            act[here, first : first + hidden] = da
            act[here, first + hidden : first + 2 * hidden] = db
            act[here, first + 2 * hidden : first + 3 * hidden] = (gate * h).astype(bf16)
            dx += lax.dot_general(da, w_gate[...], nt, preferred_element_type=f32)
            dx += lax.dot_general(db, w_up[...], nt, preferred_element_type=f32)
            gg += jnp.where(column, dots, 0.0)
        for k, i in enumerate(group):
            part = slice(k * tokens, (k + 1) * tokens)
            dxg[i][:, :width] = dx[part].astype(bf16)
            dxg[i][:, width:] = gg[part].astype(bf16)


def rows_grads(xgs, dys, weights):
    slots = len(dys)
    tokens, width = dys[0].shape
    full = xgs[0].shape[1]
    hidden = weights[2].shape[0]
    rows = slots * tokens
    flops = 2 * rows * 2 * 5 * width * hidden
    moved = 4 * rows * (width + full) + 12 * width * hidden + 4 * rows * full + 12 * rows * hidden
    return pl.pallas_call(
        functools.partial(rows_kernel, slots),
        out_shape=tuple(jax.ShapeDtypeStruct((tokens, full), bf16) for _ in dys)
        + (jax.ShapeDtypeStruct((rows, 6 * hidden), bf16),),
        in_specs=[VMEM] * (2 * slots + 6),
        out_specs=(VMEM,) * (slots + 1),
        compiler_params=params(20),
        cost_estimate=pl.CostEstimate(
            flops=flops, bytes_accessed=moved, transcendentals=2 * rows * hidden
        ),
        name="rows_grads",
    )(*xgs, *dys, *weights)


def weights_kernel(j, slots, steps, extra, *refs):
    xg_in, dy_in, act_in = refs[:slots], refs[slots : 2 * slots], refs[2 * slots : 2 * slots + steps]
    refs = refs[2 * slots + steps :]
    more, refs = refs[:extra], refs[extra:]
    gate_out, up_out, down_out = refs[:3]
    x, dy, act, sem = refs[3:]
    tokens, width = dy_in[0].shape
    hidden = act.shape[1] // 3
    step_rows = act_in[0].shape[0]
    copies = []

    def fetch(src, dst):
        copies.append(pltpu.make_async_copy(src, dst, sem.at[len(copies)]))
        copies[-1].start()

    for i in range(steps):
        fetch(
            act_in[i].at[:, pl.ds(j * 3 * hidden, 3 * hidden)],
            act.at[pl.ds(i * step_rows, step_rows)],
        )
    for i in range(slots):
        fetch(xg_in[i].at[:, pl.ds(0, width)], x.at[pl.ds(i * tokens, tokens)])
    for i in range(slots):
        fetch(dy_in[i], dy.at[pl.ds(i * tokens, tokens)])
    for c in copies[: steps + slots]:
        c.wait()

    def put(out, here, value, k):
        if extra:
            value = value + more[k][here].astype(f32)
        if len(out.shape) == 3:
            out[0, here[0], here[1]] = value.astype(out.dtype)
        else:
            out[here[0], here[1]] = value.astype(out.dtype)

    part = math.gcd(width, 256)
    everything = slice(None)
    for m in range(0, width, part):
        here = (slice(m, m + part), everything)
        both = lax.dot_general(
            x[:, m : m + part], act[:, : 2 * hidden], tn, preferred_element_type=f32
        )
        put(gate_out, here, both[:, :hidden], 0)
        put(up_out, here, both[:, hidden:], 1)
    for c in copies[steps + slots :]:
        c.wait()
    part = math.gcd(hidden, 128)
    for m in range(0, hidden, part):
        here = (slice(m, m + part), everything)
        value = lax.dot_general(
            act[:, 2 * hidden + m : 2 * hidden + m + part], dy[...], tn, preferred_element_type=f32
        )
        put(down_out, here, value, 2)


def weights_grads(j, xgs, dys, acts, dtype, more=()):
    slots, steps = len(dys), len(acts)
    tokens, width = dys[0].shape
    hidden = acts[0].shape[1] // 6
    rows = slots * tokens
    lead = (1,) if more else ()
    return pl.pallas_call(
        functools.partial(weights_kernel, j, slots, steps, len(more)),
        out_shape=(
            jax.ShapeDtypeStruct(lead + (width, hidden), dtype),
            jax.ShapeDtypeStruct(lead + (width, hidden), dtype),
            jax.ShapeDtypeStruct(lead + (hidden, width), dtype),
        ),
        in_specs=[ANY] * (2 * slots + steps) + [VMEM] * len(more),
        out_specs=(VMEM,) * 3,
        scratch_shapes=[
            pltpu.VMEM((rows, width), bf16),
            pltpu.VMEM((rows, width), bf16),
            pltpu.VMEM((rows, 3 * hidden), bf16),
            pltpu.SemaphoreType.DMA((2 * slots + steps,)),
        ],
        compiler_params=params(20),
        cost_estimate=pl.CostEstimate(
            flops=6 * rows * width * hidden,
            bytes_accessed=rows * (4 * width + 6 * hidden) + 6 * width * hidden,
            transcendentals=0,
        ),
        name="weights_grads",
    )(*xgs, *dys, *acts, *more)


def finish_kernel(parts, ids, kept, *refs):
    pieces, (tokens_out, gates_out) = refs[:parts], refs[parts:]
    tokens, width = tokens_out.shape
    total = pieces[0][:, :width].astype(f32)
    gg = pieces[0][:, width:].astype(f32)
    for p in pieces[1:]:
        total = total + p[:, :width].astype(f32)
        gg = gg + p[:, width:].astype(f32)
    tokens_out[...] = total.astype(bf16)
    devices = kept.shape[0]
    gg = gg.T[:devices] * kept[...]
    expert = row_iota(devices, tokens)
    place = row_iota(TOP, tokens)
    out = jnp.zeros((TOP, tokens), f32)
    for k in range(TOP):
        value = jnp.sum(jnp.where(expert == ids[k : k + 1], gg, 0.0), axis=0, keepdims=True)
        out = jnp.where(place == k, value, out)
    gates_out[...] = out.astype(bf16)


def finish(ids, kept, pieces, width):
    tokens = ids.shape[1]
    return pl.pallas_call(
        functools.partial(finish_kernel, len(pieces)),
        out_shape=(
            jax.ShapeDtypeStruct((tokens, width), bf16),
            jax.ShapeDtypeStruct((TOP, tokens), bf16),
        ),
        in_specs=[VMEM] * (2 + len(pieces)),
        out_specs=(VMEM, VMEM),
        compiler_params=params(16),
        name="finish",
    )(ids, kept, *pieces)


def add(*terms):
    total = terms[0].astype(f32)
    for t in terms[1:]:
        total = total + t.astype(f32)
    return total.astype(bf16)


def on_device(tokens_in, grad_out, gates, expert_ids, replica_table, w_gate, w_up, w_down):
    devices = lax.axis_size("expert")
    tokens, width = tokens_in.shape
    lanes = -(-devices // LANES) * LANES
    chips = devices // CORES
    inner = 2 ** (int(math.log2(chips)) // 2)
    outer = chips // inner

    def moved(i, dz, dy):
        core, chip = i % CORES, i // CORES
        z, y = chip // inner, chip % inner
        return (((z + dz) % outer) * inner + (y + dy) % inner) * CORES + core

    def send_z(v):
        return lax.ppermute(v, "expert", [(i, moved(i, 1, 0)) for i in range(devices)])

    def send_down(v):
        return lax.ppermute(v, "expert", [(i, moved(i, -1, 0)) for i in range(devices)])

    def send_y(v):
        return lax.ppermute(v, "expert", [(i, moved(i, 0, 1)) for i in range(devices)])

    def send_core(v):
        return lax.ppermute(v, "expert", [(i, i ^ 1) for i in range(devices)])

    def together(*values):
        return lax.optimization_barrier(values)

    ids = expert_ids.T
    xg, kept = plan(replica_table[None], ids, gates.T, tokens_in, devices, lanes)
    own = (w_gate[0], w_up[0], w_down[0])
    own, kept = together(own, kept)
    weights = own + tuple(send_core(w) for w in own)

    per = max(1, W_ROWS // (inner * tokens))
    groups = [range(z, min(outer, z + per)) for z in range(0, outer, per)]
    sums = [None, None]

    def partial(j, group, dtype, more=()):
        return weights_grads(
            j,
            [x for z in group for x in xgs[z]],
            [d for z in group for d in dys[z]],
            [acts[z] for z in group],
            dtype,
            more,
        )

    xgs, dys = [[xg]], [[grad_out]]
    dxs, acts, across = [], [], []

    def send_across(z):
        if inner == 1:
            return []
        total = dxs[z][1]
        for y in range(2, inner):
            total = add(send_y(total), dxs[z][y])
        return [send_y(total)]

    for z in range(1, outer + 1):
        for k, stream in enumerate((xgs, dys)):
            last = stream[z - 1]
            ahead = None
            if z < outer:
                ahead = send_z(last[0])
            for y in range(1, inner):
                if k and z == outer > 1 and y == inner - 1:
                    last.append(send_z(stream[z - 2][y]))
                else:
                    last.append(send_y(last[y - 1]))
            done = [] if ahead is None else [ahead]
            if inner > 1:
                done.append(last[-1])
            if k == 0 and z == 1:
                kept, weights = together(kept, weights)
                done, kept = together(done, hold(kept, HOLD))
            elif k == 0:
                done, acts[z - 2] = together(done, acts[z - 2])
            else:
                (done,) = together(done)
            if inner > 1:
                last[-1] = done.pop()
            if ahead is not None:
                stream.append([done.pop()])
        if z == outer > 2:
            first, xgs[z - 1] = together(send_z(dxs[1][0]), xgs[z - 1])
        *dx, act = rows_grads(xgs[z - 1], dys[z - 1], weights)
        dxs.append(dx)
        acts.append(act)
        if z > 2:
            across.append(send_across(z - 1))
        if len(groups) > 1 and z - 1 == groups[(z - 1) // per][-1]:
            for j in range(2):
                value = partial(j, groups[(z - 1) // per], f32)
                sums[j] = value if z <= per else [t + v for t, v in zip(sums[j], value)]
            if z < outer:
                sums, xgs[z] = together(sums, xgs[z])

    single = len(groups) == 1
    if single:
        other = [send_core(v) for v in partial(1, groups[0], bf16)]
    else:
        other = [send_core(v.astype(bf16)) for v in sums[1]]

    pieces = []
    if outer > 1:
        if outer == 2:
            pieces.append(send_z(dxs[1][0]))
        dxs[1], acts[-2] = together(dxs[1], acts[-2])
        down = [send_down(v) for v in dxs[1][1:]]
        dxs[0] = [dxs[0][0]] + [add(v, o) for v, o in zip(dxs[0][1:], down)]
    pieces += [dxs[0][0], *send_across(0)]
    if outer > 2:
        total = add(dxs[2][0], first, *across[0])
        for z in range(3, outer):
            total = add(send_z(total), dxs[z][0], *across[z - 2])
        total, other = together(total, other)
        pieces.append(send_z(total))
    if single:
        grad_w = partial(0, groups[0], bf16, other)
    else:
        grad_w = [(v + o.astype(f32)).astype(bf16)[None] for v, o in zip(sums[0], other)]
    pieces, grad_w = together(pieces, grad_w)
    grad_tokens, grad_gates = finish(ids, kept, pieces, width)
    grad_gates = grad_gates.T
    return (grad_tokens, grad_gates, *grad_w)


def solution(mesh):
    both = ("groups", "expert")
    return jax.shard_map(
        on_device,
        mesh=mesh,
        in_specs=(
            P(both, None),
            P(both, None),
            P(both, None),
            P(both, None),
            P("groups"),
            P("expert", None, None),
            P("expert", None, None),
            P("expert", None, None),
        ),
        out_specs=(
            P(both, None),
            P(both, None),
            P(both, None, None),
            P(both, None, None),
            P(both, None, None),
        ),
        check_vma=False,
    )
```

```python
import functools
import math

import jax
import jax.numpy as jnp
from jax import lax
from jax.experimental import pallas as pl
from jax.experimental.pallas import tpu as pltpu
from jax.sharding import PartitionSpec as P

TOP = 8
CORES = 2
LANES = 128
ROW_BLOCK = 256
W_ROWS = 1024
HOLD = 10**10
PLAN_MIB = 60

f32 = jnp.float32
bf16 = jnp.bfloat16
nt = (((1,), (1,)), ((), ()))
tn = (((0,), (0,)), ((), ()))
VMEM = pl.BlockSpec(memory_space=pltpu.VMEM)
ANY = pl.BlockSpec(memory_space=pl.ANY)
HBM = pl.BlockSpec(memory_space=pltpu.HBM)


def params(mib):
    return pltpu.CompilerParams(vmem_limit_bytes=mib * 1024 * 1024)


def row_iota(rows, lanes):
    return lax.broadcasted_iota(jnp.int32, (rows, lanes), 0)


def lane_iota(rows, lanes):
    return lax.broadcasted_iota(jnp.int32, (rows, lanes), 1)


def plan_kernel(home_cap, rep_cap, table_in, ids_in, gates_in, x_in, xg, kept_out, *scratch):
    table, ids, gates, sem = scratch
    tokens, width = x_in.shape
    extra = xg.shape[0] - tokens
    pairs = (
        (table_in, table),
        (ids_in, ids),
        (gates_in, gates),
        (x_in, xg.at[pl.ds(0, tokens)]),
    )
    copies = [pltpu.make_async_copy(src, dst, sem.at[i]) for i, (src, dst) in enumerate(pairs)]
    for c in copies:
        c.start()
    devices = table.shape[1]
    earlier = row_iota(tokens, tokens) < lane_iota(tokens, tokens)
    earlier = jnp.where(earlier, 1.0, 0.0).astype(bf16)
    expert = row_iota(devices, tokens)
    for c in copies[:3]:
        c.wait()
    hosts = jnp.where(table[...] == row_iota(devices, devices), 1.0, 0.0)
    copied = 1.0 + jnp.sum(hosts, axis=1, keepdims=True)
    named = jnp.zeros((devices, tokens), f32)
    weight = jnp.zeros((devices, tokens), f32)
    for k in range(TOP):
        hit = expert == ids[k : k + 1]
        named = jnp.where(hit, 1.0, named)
        weight = jnp.where(hit, gates[k : k + 1].astype(f32), weight)
    rank = jnp.dot(named.astype(bf16), earlier, preferred_element_type=f32)
    turn = rank + lax.axis_index("expert").astype(f32)
    at_home = turn == copied * jnp.floor(turn / copied + 0.5)
    cap = jnp.where(at_home, float(home_cap), float(rep_cap))
    kept = jnp.where((named > 0.0) & (rank < cap * copied), 1.0, 0.0)
    kept_out[...] = kept
    dense = weight * kept
    for k in range(width // tokens):
        part = jnp.zeros((extra, tokens), f32)
        if k * extra < devices:
            part = dense[k * extra : (k + 1) * extra]
        xg[tokens:, k * tokens : (k + 1) * tokens] = part.astype(bf16)
    copies[3].wait()


def plan(table, ids, gates, x, devices, extra):
    tokens, width = x.shape
    home_cap = max(2, 5 * tokens * TOP // (4 * devices))
    rep_cap = max(2, tokens * TOP // (2 * devices))
    return pl.pallas_call(
        functools.partial(plan_kernel, home_cap, rep_cap),
        out_shape=(
            jax.ShapeDtypeStruct((tokens + extra, width), bf16),
            jax.ShapeDtypeStruct((devices, tokens), f32),
        ),
        in_specs=[HBM] * 4,
        out_specs=(VMEM, VMEM),
        scratch_shapes=[
            pltpu.VMEM(table.shape, jnp.int32),
            pltpu.VMEM(ids.shape, jnp.int32),
            pltpu.VMEM(gates.shape, bf16),
            pltpu.SemaphoreType.DMA((4,)),
        ],
        compiler_params=params(PLAN_MIB),
        name="plan",
    )(table, ids, gates, x)


def hold(value, flops):
    return pl.pallas_call(
        lambda source, out: None,
        out_shape=jax.ShapeDtypeStruct(value.shape, value.dtype),
        in_specs=[ANY],
        out_specs=ANY,
        input_output_aliases={0: 0},
        compiler_params=params(1),
        cost_estimate=pl.CostEstimate(flops=flops, bytes_accessed=1000, transcendentals=0),
        name="hold",
    )(value)


def rows_kernel(slots, *refs):
    xg, dy = refs[:slots], refs[slots : 2 * slots]
    weights = refs[2 * slots : 2 * slots + 6]
    dxg, act = refs[2 * slots + 6 : 3 * slots + 6], refs[3 * slots + 6]
    tokens, width = dy[0].shape
    hidden = weights[2].shape[0]
    extra = xg[0].shape[0] - tokens
    per = max(1, ROW_BLOCK // tokens)
    me = lax.axis_index("expert")

    def stack(parts):
        return parts[0] if len(parts) == 1 else jnp.concatenate(parts, axis=0)

    def unpack(ref):
        total = jnp.zeros((extra, tokens), f32)
        for c in range(width // tokens):
            part = ref[tokens:, c * tokens : (c + 1) * tokens].astype(f32)
            total = jnp.where(me // extra == c, part, total)
        return total.T

    for at in range(0, slots, per):
        group = range(at, min(slots, at + per))
        x = stack([xg[i][:tokens] for i in group])
        up_grad = stack([dy[i][...] for i in group])
        rows = len(group) * tokens
        here = pl.ds(at * tokens, rows)
        gates = stack([unpack(xg[i]) for i in group])
        lane = lane_iota(rows, LANES)
        dx, gg = 0.0, 0.0
        for j in range(2):
            w_gate, w_up, w_down = weights[3 * j : 3 * j + 3]
            a = jnp.dot(x, w_gate[...], preferred_element_type=f32)
            b = jnp.dot(x, w_up[...], preferred_element_type=f32)
            back = lax.dot_general(up_grad, w_down[...], nt, preferred_element_type=f32)
            column = (me if j == 0 else me ^ 1) % extra
            gate = jnp.sum(
                jnp.where(lane_iota(rows, extra) == column, gates, 0.0), axis=1, keepdims=True
            )
            sig = jax.nn.sigmoid(a)
            silu = a * sig
            h = silu * b
            dots = jnp.sum(h.astype(bf16).astype(f32) * back, axis=1, keepdims=True)
            scaled = gate * back
            da = (scaled * b * sig * (1.0 + a * (1.0 - sig))).astype(bf16)
            db = (scaled * silu).astype(bf16)
            first = j * 3 * hidden
            act[here, first : first + hidden] = da
            act[here, first + hidden : first + 2 * hidden] = db
            act[here, first + 2 * hidden : first + 3 * hidden] = (gate * h).astype(bf16)
            dx += lax.dot_general(da, w_gate[...], nt, preferred_element_type=f32)
            dx += lax.dot_general(db, w_up[...], nt, preferred_element_type=f32)
            gg += jnp.where(lane == column, dots, 0.0)
        for k, i in enumerate(group):
            part = slice(k * tokens, (k + 1) * tokens)
            dxg[i][:tokens] = dx[part].astype(bf16)
            packed = gg[part].T[:extra]
            for c in range(width // tokens):
                dxg[i][tokens:, c * tokens : (c + 1) * tokens] = jnp.where(
                    me // extra == c, packed, 0.0
                ).astype(bf16)


def rows_grads(xgs, dys, weights):
    slots = len(dys)
    tokens, width = dys[0].shape
    full = xgs[0].shape[0]
    hidden = weights[2].shape[0]
    rows = slots * tokens
    flops = 2 * rows * 2 * 5 * width * hidden
    moved = 12 * rows * width + 12 * width * hidden + 12 * rows * hidden
    return pl.pallas_call(
        functools.partial(rows_kernel, slots),
        out_shape=tuple(jax.ShapeDtypeStruct((full, width), bf16) for _ in dys)
        + (jax.ShapeDtypeStruct((rows, 6 * hidden), bf16),),
        in_specs=[VMEM] * (2 * slots + 6),
        out_specs=(VMEM,) * (slots + 1),
        compiler_params=params(20),
        cost_estimate=pl.CostEstimate(
            flops=flops, bytes_accessed=moved, transcendentals=2 * rows * hidden
        ),
        name="rows_grads",
    )(*xgs, *dys, *weights)


def weights_kernel(j, slots, steps, extra, *refs):
    xg_in, dy_in, act_in = refs[:slots], refs[slots : 2 * slots], refs[2 * slots : 2 * slots + steps]
    refs = refs[2 * slots + steps :]
    more, refs = refs[:extra], refs[extra:]
    gate_out, up_out, down_out = refs[:3]
    x, dy, act, sem = refs[3:]
    tokens, width = dy_in[0].shape
    hidden = act.shape[1] // 3
    step_rows = act_in[0].shape[0]
    copies = []

    def fetch(src, dst):
        copies.append(pltpu.make_async_copy(src, dst, sem.at[len(copies)]))
        copies[-1].start()

    for i in range(steps):
        fetch(
            act_in[i].at[:, pl.ds(j * 3 * hidden, 3 * hidden)],
            act.at[pl.ds(i * step_rows, step_rows)],
        )
    for i in range(slots):
        fetch(xg_in[i].at[pl.ds(0, tokens)], x.at[pl.ds(i * tokens, tokens)])
    for i in range(slots):
        fetch(dy_in[i], dy.at[pl.ds(i * tokens, tokens)])
    for c in copies[: steps + slots]:
        c.wait()

    def put(out, here, value, k):
        if extra:
            value = value + more[k][here].astype(f32)
        if len(out.shape) == 3:
            out[0, here[0], here[1]] = value.astype(out.dtype)
        else:
            out[here[0], here[1]] = value.astype(out.dtype)

    part = math.gcd(width, 256)
    everything = slice(None)
    for m in range(0, width, part):
        here = (slice(m, m + part), everything)
        both = lax.dot_general(
            x[:, m : m + part], act[:, : 2 * hidden], tn, preferred_element_type=f32
        )
        put(gate_out, here, both[:, :hidden], 0)
        put(up_out, here, both[:, hidden:], 1)
    for c in copies[steps + slots :]:
        c.wait()
    part = math.gcd(hidden, 128)
    for m in range(0, hidden, part):
        here = (slice(m, m + part), everything)
        value = lax.dot_general(
            act[:, 2 * hidden + m : 2 * hidden + m + part], dy[...], tn, preferred_element_type=f32
        )
        put(down_out, here, value, 2)


def weights_grads(j, xgs, dys, acts, dtype, more=()):
    slots, steps = len(dys), len(acts)
    tokens, width = dys[0].shape
    hidden = acts[0].shape[1] // 6
    rows = slots * tokens
    lead = (1,) if more else ()
    return pl.pallas_call(
        functools.partial(weights_kernel, j, slots, steps, len(more)),
        out_shape=(
            jax.ShapeDtypeStruct(lead + (width, hidden), dtype),
            jax.ShapeDtypeStruct(lead + (width, hidden), dtype),
            jax.ShapeDtypeStruct(lead + (hidden, width), dtype),
        ),
        in_specs=[ANY] * (2 * slots + steps) + [VMEM] * len(more),
        out_specs=(VMEM,) * 3,
        scratch_shapes=[
            pltpu.VMEM((rows, width), bf16),
            pltpu.VMEM((rows, width), bf16),
            pltpu.VMEM((rows, 3 * hidden), bf16),
            pltpu.SemaphoreType.DMA((2 * slots + steps,)),
        ],
        compiler_params=params(20),
        cost_estimate=pl.CostEstimate(
            flops=1000,
            bytes_accessed=1000,
            transcendentals=0,
        ),
        name="weights_grads",
    )(*xgs, *dys, *acts, *more)


def finish_kernel(parts, ids, kept, *refs):
    pieces, (tokens_out, gates_out) = refs[:parts], refs[parts:]
    tokens, width = tokens_out.shape
    total = pieces[0][...].astype(f32)
    for p in pieces[1:]:
        total = total + p[...].astype(f32)
    tokens_out[...] = total[:tokens].astype(bf16)
    devices = kept.shape[0]
    extra = pieces[0].shape[0] - tokens
    gg = [total[tokens:, k * tokens : (k + 1) * tokens] for k in range(devices // extra)]
    gg = jnp.concatenate(gg, axis=0) * kept[...]
    expert = row_iota(devices, tokens)
    place = row_iota(TOP, tokens)
    out = jnp.zeros((TOP, tokens), f32)
    for k in range(TOP):
        value = jnp.sum(jnp.where(expert == ids[k : k + 1], gg, 0.0), axis=0, keepdims=True)
        out = jnp.where(place == k, value, out)
    gates_out[...] = out.astype(bf16)


def finish(ids, kept, pieces, width):
    tokens = ids.shape[1]
    return pl.pallas_call(
        functools.partial(finish_kernel, len(pieces)),
        out_shape=(
            jax.ShapeDtypeStruct((tokens, width), bf16),
            jax.ShapeDtypeStruct((TOP, tokens), bf16),
        ),
        in_specs=[VMEM] * (2 + len(pieces)),
        out_specs=(VMEM, VMEM),
        compiler_params=params(16),
        name="finish",
    )(ids, kept, *pieces)


def add(*terms):
    total = terms[0].astype(f32)
    for t in terms[1:]:
        total = total + t.astype(f32)
    return total.astype(bf16)


def on_device(tokens_in, grad_out, gates, expert_ids, replica_table, w_gate, w_up, w_down):
    devices = lax.axis_size("expert")
    tokens, width = tokens_in.shape
    extra = 8 * -(-devices * tokens // (8 * width))
    chips = devices // CORES
    inner = 2 ** (int(math.log2(chips)) // 2)
    outer = chips // inner

    def moved(i, dz, dy):
        core, chip = i % CORES, i // CORES
        z, y = chip // inner, chip % inner
        return (((z + dz) % outer) * inner + (y + dy) % inner) * CORES + core

    def send_z(v):
        return lax.ppermute(v, "expert", [(i, moved(i, 1, 0)) for i in range(devices)])

    def send_down(v):
        return lax.ppermute(v, "expert", [(i, moved(i, -1, 0)) for i in range(devices)])

    def send_y(v):
        return lax.ppermute(v, "expert", [(i, moved(i, 0, 1)) for i in range(devices)])

    def send_core(v):
        return lax.ppermute(v, "expert", [(i, i ^ 1) for i in range(devices)])

    def together(*values):
        return lax.optimization_barrier(values)

    ids = expert_ids.T
    xg, kept = plan(replica_table[None], ids, gates.T, tokens_in, devices, extra)
    own = (w_gate[0], w_up[0], w_down[0])
    weights = own + tuple(send_core(w) for w in own)

    per = max(1, W_ROWS // (inner * tokens))
    groups = [range(z, min(outer, z + per)) for z in range(0, outer, per)]
    sums = [None, None]

    def partial(j, group, dtype, more=()):
        return weights_grads(
            j,
            [x for z in group for x in xgs[z]],
            [d for z in group for d in dys[z]],
            [acts[z] for z in group],
            dtype,
            more,
        )

    xgs, dys = [[xg]], [[grad_out]]
    dxs, acts, across = [], [], []

    def send_across(z):
        if inner == 1:
            return []
        total = dxs[z][1]
        for y in range(2, inner):
            total = add(send_y(total), dxs[z][y])
        return [send_y(total)]

    for z in range(1, outer + 1):
        for k, stream in enumerate((xgs, dys)):
            last = stream[z - 1]
            ahead = None
            if z < outer:
                ahead = send_z(last[0])
            for y in range(1, inner):
                if k and z == outer > 1 and y == inner - 1:
                    last.append(send_z(stream[z - 2][y]))
                else:
                    last.append(send_y(last[y - 1]))
            done = [last[-1]] if inner > 1 else []
            if ahead is not None:
                done.append(ahead)
            if k == 0 and z == 1:
                kept, weights = together(kept, weights)
                done, kept = together(done, hold(kept, HOLD))
            elif k == 0:
                done, acts[z - 2] = together(done, acts[z - 2])
            else:
                (done,) = together(done)
            if ahead is not None:
                stream.append([done.pop()])
            if inner > 1:
                last[-1] = done.pop()
        if z == outer > 2:
            first, xgs[z - 1] = together(send_z(dxs[1][0]), xgs[z - 1])
        *dx, act = rows_grads(xgs[z - 1], dys[z - 1], weights)
        dxs.append(dx)
        acts.append(act)
        if z > 2:
            across.append(send_across(z - 1))
        if len(groups) > 1 and z - 1 == groups[(z - 1) // per][-1]:
            for j in range(2):
                value = partial(j, groups[(z - 1) // per], f32)
                sums[j] = value if z <= per else [t + v for t, v in zip(sums[j], value)]
            if z < outer:
                sums, xgs[z] = together(sums, xgs[z])

    single = len(groups) == 1
    if single:
        other = [send_core(v) for v in partial(1, groups[0], bf16)]
    else:
        other = [send_core(v.astype(bf16)) for v in sums[1]]

    pieces = []
    if outer > 1:
        if outer == 2:
            pieces.append(send_z(dxs[1][0]))
        dxs[1], acts[-2] = together(dxs[1], acts[-2])
        down = [send_down(v) for v in dxs[1][1:]]
        dxs[0] = [dxs[0][0]] + [add(v, o) for v, o in zip(dxs[0][1:], down)]
    pieces += [dxs[0][0], *send_across(0)]
    if outer > 2:
        total = add(dxs[2][0], first, *across[0])
        for z in range(3, outer):
            total = add(send_z(total), dxs[z][0], *across[z - 2])
        _, other = together(total, other)
        pieces.append(send_z(total))
    if single:
        grad_w = partial(0, groups[0], bf16, other)
    else:
        grad_w = [(v + o.astype(f32)).astype(bf16)[None] for v, o in zip(sums[0], other)]
    pieces, grad_w = together(pieces, grad_w)
    grad_tokens, grad_gates = finish(ids, kept, pieces, width)
    grad_gates = grad_gates.T
    return (grad_tokens, grad_gates, *grad_w)


def solution(mesh):
    both = ("groups", "expert")
    return jax.shard_map(
        on_device,
        mesh=mesh,
        in_specs=(
            P(both, None),
            P(both, None),
            P(both, None),
            P(both, None),
            P("groups"),
            P("expert", None, None),
            P("expert", None, None),
            P("expert", None, None),
        ),
        out_specs=(
            P(both, None),
            P(both, None),
            P(both, None, None),
            P(both, None, None),
            P(both, None, None),
        ),
        check_vma=False,
    )
```

```python
import functools
import math

import jax
import jax.numpy as jnp
from jax import lax
from jax.experimental import pallas as pl
from jax.experimental.pallas import tpu as pltpu
from jax.sharding import PartitionSpec as P

TOP = 8
CORES = 2
LANES = 128
ROW_BLOCK = 256
W_ROWS = 1024
HOLD = 10**10
PLAN_MIB = 60

f32 = jnp.float32
bf16 = jnp.bfloat16
nt = (((1,), (1,)), ((), ()))
tn = (((0,), (0,)), ((), ()))
VMEM = pl.BlockSpec(memory_space=pltpu.VMEM)
ANY = pl.BlockSpec(memory_space=pl.ANY)
HBM = pl.BlockSpec(memory_space=pltpu.HBM)


def params(mib):
    return pltpu.CompilerParams(vmem_limit_bytes=mib * 1024 * 1024)


def row_iota(rows, lanes):
    return lax.broadcasted_iota(jnp.int32, (rows, lanes), 0)


def lane_iota(rows, lanes):
    return lax.broadcasted_iota(jnp.int32, (rows, lanes), 1)


def plan_kernel(home_cap, rep_cap, table_in, ids_in, gates_in, x_in, xg, kept_out, *scratch):
    table, ids, gates, sem = scratch
    tokens, width = x_in.shape
    extra = xg.shape[0] - tokens
    pairs = (
        (table_in, table),
        (ids_in, ids),
        (gates_in, gates),
        (x_in, xg.at[pl.ds(0, tokens)]),
    )
    copies = [pltpu.make_async_copy(src, dst, sem.at[i]) for i, (src, dst) in enumerate(pairs)]
    for c in copies:
        c.start()
    devices = table.shape[1]
    earlier = row_iota(tokens, tokens) < lane_iota(tokens, tokens)
    earlier = jnp.where(earlier, 1.0, 0.0).astype(bf16)
    expert = row_iota(devices, tokens)
    for c in copies[:3]:
        c.wait()
    hosts = jnp.where(table[...] == row_iota(devices, devices), 1.0, 0.0)
    copied = 1.0 + jnp.sum(hosts, axis=1, keepdims=True)
    named = jnp.zeros((devices, tokens), f32)
    weight = jnp.zeros((devices, tokens), f32)
    for k in range(TOP):
        hit = expert == ids[k : k + 1]
        named = jnp.where(hit, 1.0, named)
        weight = jnp.where(hit, gates[k : k + 1].astype(f32), weight)
    rank = jnp.dot(named.astype(bf16), earlier, preferred_element_type=f32)
    turn = rank + lax.axis_index("expert").astype(f32)
    at_home = turn == copied * jnp.floor(turn / copied + 0.5)
    cap = jnp.where(at_home, float(home_cap), float(rep_cap))
    kept = jnp.where((named > 0.0) & (rank < cap * copied), 1.0, 0.0)
    kept_out[...] = kept
    dense = weight * kept
    for k in range(width // tokens):
        part = jnp.zeros((extra, tokens), f32)
        if k * extra < devices:
            part = dense[k * extra : (k + 1) * extra]
        xg[tokens:, k * tokens : (k + 1) * tokens] = part.astype(bf16)
    copies[3].wait()


def plan(table, ids, gates, x, devices, extra):
    tokens, width = x.shape
    home_cap = max(2, 5 * tokens * TOP // (4 * devices))
    rep_cap = max(2, tokens * TOP // (2 * devices))
    return pl.pallas_call(
        functools.partial(plan_kernel, home_cap, rep_cap),
        out_shape=(
            jax.ShapeDtypeStruct((tokens + extra, width), bf16),
            jax.ShapeDtypeStruct((devices, tokens), f32),
        ),
        in_specs=[HBM] * 4,
        out_specs=(VMEM, VMEM),
        scratch_shapes=[
            pltpu.VMEM(table.shape, jnp.int32),
            pltpu.VMEM(ids.shape, jnp.int32),
            pltpu.VMEM(gates.shape, bf16),
            pltpu.SemaphoreType.DMA((4,)),
        ],
        compiler_params=params(PLAN_MIB),
        name="plan",
    )(table, ids, gates, x)


def hold(value, flops):
    return pl.pallas_call(
        lambda source, out: None,
        out_shape=jax.ShapeDtypeStruct(value.shape, value.dtype),
        in_specs=[ANY],
        out_specs=ANY,
        input_output_aliases={0: 0},
        compiler_params=params(1),
        cost_estimate=pl.CostEstimate(flops=flops, bytes_accessed=1000, transcendentals=0),
        name="hold",
    )(value)


def rows_kernel(slots, *refs):
    xg, dy = refs[:slots], refs[slots : 2 * slots]
    weights = refs[2 * slots : 2 * slots + 6]
    dxg, act = refs[2 * slots + 6 : 3 * slots + 6], refs[3 * slots + 6]
    tokens, width = dy[0].shape
    hidden = weights[2].shape[0]
    extra = xg[0].shape[0] - tokens
    per = max(1, ROW_BLOCK // tokens)
    me = lax.axis_index("expert")

    def stack(parts):
        return parts[0] if len(parts) == 1 else jnp.concatenate(parts, axis=0)

    def unpack(ref):
        total = jnp.zeros((extra, tokens), f32)
        for c in range(width // tokens):
            part = ref[tokens:, c * tokens : (c + 1) * tokens].astype(f32)
            total = jnp.where(me // extra == c, part, total)
        return total.T

    for at in range(0, slots, per):
        group = range(at, min(slots, at + per))
        x = stack([xg[i][:tokens] for i in group])
        up_grad = stack([dy[i][...] for i in group])
        rows = len(group) * tokens
        here = pl.ds(at * tokens, rows)
        gates = stack([unpack(xg[i]) for i in group])
        lane = lane_iota(rows, LANES)
        dx, gg = 0.0, 0.0
        for j in range(2):
            w_gate, w_up, w_down = weights[3 * j : 3 * j + 3]
            a = jnp.dot(x, w_gate[...], preferred_element_type=f32)
            b = jnp.dot(x, w_up[...], preferred_element_type=f32)
            back = lax.dot_general(up_grad, w_down[...], nt, preferred_element_type=f32)
            column = (me if j == 0 else me ^ 1) % extra
            gate = jnp.sum(
                jnp.where(lane_iota(rows, extra) == column, gates, 0.0), axis=1, keepdims=True
            )
            sig = jax.nn.sigmoid(a)
            silu = a * sig
            h = silu * b
            dots = jnp.sum(h.astype(bf16).astype(f32) * back, axis=1, keepdims=True)
            scaled = gate * back
            da = (scaled * b * sig * (1.0 + a * (1.0 - sig))).astype(bf16)
            db = (scaled * silu).astype(bf16)
            first = j * 3 * hidden
            act[here, first : first + hidden] = da
            act[here, first + hidden : first + 2 * hidden] = db
            act[here, first + 2 * hidden : first + 3 * hidden] = (gate * h).astype(bf16)
            dx += lax.dot_general(da, w_gate[...], nt, preferred_element_type=f32)
            dx += lax.dot_general(db, w_up[...], nt, preferred_element_type=f32)
            gg += jnp.where(lane == column, dots, 0.0)
        for k, i in enumerate(group):
            part = slice(k * tokens, (k + 1) * tokens)
            dxg[i][:tokens] = dx[part].astype(bf16)
            packed = gg[part].T[:extra]
            for c in range(width // tokens):
                dxg[i][tokens:, c * tokens : (c + 1) * tokens] = jnp.where(
                    me // extra == c, packed, 0.0
                ).astype(bf16)


def rows_grads(xgs, dys, weights):
    slots = len(dys)
    tokens, width = dys[0].shape
    full = xgs[0].shape[0]
    hidden = weights[2].shape[0]
    rows = slots * tokens
    flops = 1 * rows * 2 * 5 * width * hidden
    moved = 12 * rows * width + 12 * width * hidden + 12 * rows * hidden
    return pl.pallas_call(
        functools.partial(rows_kernel, slots),
        out_shape=tuple(jax.ShapeDtypeStruct((full, width), bf16) for _ in dys)
        + (jax.ShapeDtypeStruct((rows, 6 * hidden), bf16),),
        in_specs=[VMEM] * (2 * slots + 6),
        out_specs=(VMEM,) * (slots + 1),
        compiler_params=params(20),
        cost_estimate=pl.CostEstimate(
            flops=flops, bytes_accessed=moved, transcendentals=2 * rows * hidden
        ),
        name="rows_grads",
    )(*xgs, *dys, *weights)


def weights_kernel(j, slots, steps, extra, *refs):
    xg_in, dy_in, act_in = refs[:slots], refs[slots : 2 * slots], refs[2 * slots : 2 * slots + steps]
    refs = refs[2 * slots + steps :]
    more, refs = refs[:extra], refs[extra:]
    gate_out, up_out, down_out = refs[:3]
    x, dy, act, sem = refs[3:]
    tokens, width = dy_in[0].shape
    hidden = act.shape[1] // 3
    step_rows = act_in[0].shape[0]
    copies = []

    def fetch(src, dst):
        copies.append(pltpu.make_async_copy(src, dst, sem.at[len(copies)]))
        copies[-1].start()

    for i in range(steps):
        fetch(
            act_in[i].at[:, pl.ds(j * 3 * hidden, 3 * hidden)],
            act.at[pl.ds(i * step_rows, step_rows)],
        )
    for i in range(slots):
        fetch(xg_in[i].at[pl.ds(0, tokens)], x.at[pl.ds(i * tokens, tokens)])
    for i in range(slots):
        fetch(dy_in[i], dy.at[pl.ds(i * tokens, tokens)])
    for c in copies[: steps + slots]:
        c.wait()

    def put(out, here, value, k):
        if extra:
            value = value + more[k][here].astype(f32)
        if len(out.shape) == 3:
            out[0, here[0], here[1]] = value.astype(out.dtype)
        else:
            out[here[0], here[1]] = value.astype(out.dtype)

    part = math.gcd(width, 256)
    everything = slice(None)
    for m in range(0, width, part):
        here = (slice(m, m + part), everything)
        both = lax.dot_general(
            x[:, m : m + part], act[:, : 2 * hidden], tn, preferred_element_type=f32
        )
        put(gate_out, here, both[:, :hidden], 0)
        put(up_out, here, both[:, hidden:], 1)
    for c in copies[steps + slots :]:
        c.wait()
    part = math.gcd(hidden, 128)
    for m in range(0, hidden, part):
        here = (slice(m, m + part), everything)
        value = lax.dot_general(
            act[:, 2 * hidden + m : 2 * hidden + m + part], dy[...], tn, preferred_element_type=f32
        )
        put(down_out, here, value, 2)


def weights_grads(j, xgs, dys, acts, dtype, more=()):
    slots, steps = len(dys), len(acts)
    tokens, width = dys[0].shape
    hidden = acts[0].shape[1] // 6
    rows = slots * tokens
    lead = (1,) if more else ()
    return pl.pallas_call(
        functools.partial(weights_kernel, j, slots, steps, len(more)),
        out_shape=(
            jax.ShapeDtypeStruct(lead + (width, hidden), dtype),
            jax.ShapeDtypeStruct(lead + (width, hidden), dtype),
            jax.ShapeDtypeStruct(lead + (hidden, width), dtype),
        ),
        in_specs=[ANY] * (2 * slots + steps) + [VMEM] * len(more),
        out_specs=(VMEM,) * 3,
        scratch_shapes=[
            pltpu.VMEM((rows, width), bf16),
            pltpu.VMEM((rows, width), bf16),
            pltpu.VMEM((rows, 3 * hidden), bf16),
            pltpu.SemaphoreType.DMA((2 * slots + steps,)),
        ],
        compiler_params=params(20),
        cost_estimate=pl.CostEstimate(
            flops=1000,
            bytes_accessed=1000,
            transcendentals=0,
        ),
        name="weights_grads",
    )(*xgs, *dys, *acts, *more)


def finish_kernel(parts, ids, kept, *refs):
    pieces, (tokens_out, gates_out) = refs[:parts], refs[parts:]
    tokens, width = tokens_out.shape
    total = pieces[0][...].astype(f32)
    for p in pieces[1:]:
        total = total + p[...].astype(f32)
    tokens_out[...] = total[:tokens].astype(bf16)
    devices = kept.shape[0]
    extra = pieces[0].shape[0] - tokens
    gg = [total[tokens:, k * tokens : (k + 1) * tokens] for k in range(devices // extra)]
    gg = jnp.concatenate(gg, axis=0) * kept[...]
    expert = row_iota(devices, tokens)
    place = row_iota(TOP, tokens)
    out = jnp.zeros((TOP, tokens), f32)
    for k in range(TOP):
        value = jnp.sum(jnp.where(expert == ids[k : k + 1], gg, 0.0), axis=0, keepdims=True)
        out = jnp.where(place == k, value, out)
    gates_out[...] = out.astype(bf16)


def finish(ids, kept, pieces, width):
    tokens = ids.shape[1]
    return pl.pallas_call(
        functools.partial(finish_kernel, len(pieces)),
        out_shape=(
            jax.ShapeDtypeStruct((tokens, width), bf16),
            jax.ShapeDtypeStruct((TOP, tokens), bf16),
        ),
        in_specs=[VMEM] * (2 + len(pieces)),
        out_specs=(VMEM, VMEM),
        compiler_params=params(16),
        name="finish",
    )(ids, kept, *pieces)


def add(*terms):
    total = terms[0].astype(f32)
    for t in terms[1:]:
        total = total + t.astype(f32)
    return total.astype(bf16)


def on_device(tokens_in, grad_out, gates, expert_ids, replica_table, w_gate, w_up, w_down):
    devices = lax.axis_size("expert")
    tokens, width = tokens_in.shape
    extra = 8 * -(-devices * tokens // (8 * width))
    chips = devices // CORES
    inner = 2 ** (int(math.log2(chips)) // 2)
    outer = chips // inner

    def moved(i, dz, dy):
        core, chip = i % CORES, i // CORES
        z, y = chip // inner, chip % inner
        return (((z + dz) % outer) * inner + (y + dy) % inner) * CORES + core

    def send_z(v):
        return lax.ppermute(v, "expert", [(i, moved(i, 1, 0)) for i in range(devices)])

    def send_down(v):
        return lax.ppermute(v, "expert", [(i, moved(i, -1, 0)) for i in range(devices)])

    def send_y(v):
        return lax.ppermute(v, "expert", [(i, moved(i, 0, 1)) for i in range(devices)])

    def send_core(v):
        return lax.ppermute(v, "expert", [(i, i ^ 1) for i in range(devices)])

    def together(*values):
        return lax.optimization_barrier(values)

    ids = expert_ids.T
    xg, kept = plan(replica_table[None], ids, gates.T, tokens_in, devices, extra)
    own = (w_gate[0], w_up[0], w_down[0])
    weights = own + tuple(send_core(w) for w in own)

    per = max(1, W_ROWS // (inner * tokens))
    groups = [range(z, min(outer, z + per)) for z in range(0, outer, per)]
    sums = [None, None]

    def partial(j, group, dtype, more=()):
        return weights_grads(
            j,
            [x for z in group for x in xgs[z]],
            [d for z in group for d in dys[z]],
            [acts[z] for z in group],
            dtype,
            more,
        )

    xgs, dys = [[xg]], [[grad_out]]
    dxs, acts, across = [], [], []

    def send_across(z):
        if inner == 1:
            return []
        total = dxs[z][1]
        for y in range(2, inner):
            total = add(send_y(total), dxs[z][y])
        return [send_y(total)]

    for z in range(1, outer + 1):
        for k, stream in enumerate((xgs, dys)):
            last = stream[z - 1]
            ahead = None
            if z < outer:
                ahead = send_z(last[0])
            for y in range(1, inner):
                if k and z == outer > 1 and y == inner - 1:
                    last.append(send_z(stream[z - 2][y]))
                else:
                    last.append(send_y(last[y - 1]))
            done = [last[-1]] if inner > 1 else []
            if ahead is not None:
                done.append(ahead)
            if k == 0 and z == 1:
                done, kept, held = together(done, hold(kept, HOLD), weights[3:5])
                weights = own + held + weights[5:]
            elif z == 1:
                done, held = together(done, weights[5:])
                weights = weights[:5] + held
            elif k == 0:
                done, acts[z - 2] = together(done, acts[z - 2])
            else:
                (done,) = together(done)
            if ahead is not None:
                stream.append([done.pop()])
            if inner > 1:
                last[-1] = done.pop()
        if z == outer > 2:
            first, xgs[z - 1] = together(send_z(dxs[1][0]), xgs[z - 1])
        *dx, act = rows_grads(xgs[z - 1], dys[z - 1], weights)
        dxs.append(dx)
        acts.append(act)
        if z > 2:
            across.append(send_across(z - 1))
        if len(groups) > 1 and z - 1 == groups[(z - 1) // per][-1]:
            for j in range(2):
                value = partial(j, groups[(z - 1) // per], f32)
                sums[j] = value if z <= per else [t + v for t, v in zip(sums[j], value)]
            if z < outer:
                sums, xgs[z] = together(sums, xgs[z])

    single = len(groups) == 1
    if single:
        other = [send_core(v) for v in partial(1, groups[0], bf16)]
    else:
        other = [send_core(v.astype(bf16)) for v in sums[1]]

    pieces = []
    if outer > 1:
        if outer == 2:
            pieces.append(send_z(dxs[1][0]))
        dxs[1], acts[-2] = together(dxs[1], acts[-2])
        down = [send_down(v) for v in dxs[1][1:]]
        dxs[0] = [dxs[0][0]] + [add(v, o) for v, o in zip(dxs[0][1:], down)]
    pieces += [dxs[0][0], *send_across(0)]
    if outer > 2:
        total = add(dxs[2][0], first, *across[0])
        for z in range(3, outer):
            total = add(send_z(total), dxs[z][0], *across[z - 2])
        _, other = together(total, other)
        pieces.append(send_z(total))
    if single:
        grad_w = partial(0, groups[0], bf16, other)
    else:
        grad_w = [(v + o.astype(f32)).astype(bf16)[None] for v, o in zip(sums[0], other)]
    pieces, grad_w = together(pieces, grad_w)
    grad_tokens, grad_gates = finish(ids, kept, pieces, width)
    grad_gates = grad_gates.T
    return (grad_tokens, grad_gates, *grad_w)


def solution(mesh):
    both = ("groups", "expert")
    return jax.shard_map(
        on_device,
        mesh=mesh,
        in_specs=(
            P(both, None),
            P(both, None),
            P(both, None),
            P(both, None),
            P("groups"),
            P("expert", None, None),
            P("expert", None, None),
            P("expert", None, None),
        ),
        out_specs=(
            P(both, None),
            P(both, None),
            P(both, None, None),
            P(both, None, None),
            P(both, None, None),
        ),
        check_vma=False,
    )
```

```python
import functools
import math

import jax
import jax.numpy as jnp
from jax import lax
from jax.experimental import pallas as pl
from jax.experimental.pallas import tpu as pltpu
from jax.sharding import PartitionSpec as P

TOP = 8
CORES = 2
LANES = 128
ROW_BLOCK = 256
W_ROWS = 1024
HOLD = 10**10
PLAN_MIB = 60

f32 = jnp.float32
bf16 = jnp.bfloat16
nt = (((1,), (1,)), ((), ()))
tn = (((0,), (0,)), ((), ()))
VMEM = pl.BlockSpec(memory_space=pltpu.VMEM)
ANY = pl.BlockSpec(memory_space=pl.ANY)
HBM = pl.BlockSpec(memory_space=pltpu.HBM)


def params(mib):
    return pltpu.CompilerParams(vmem_limit_bytes=mib * 1024 * 1024)


def row_iota(rows, lanes):
    return lax.broadcasted_iota(jnp.int32, (rows, lanes), 0)


def lane_iota(rows, lanes):
    return lax.broadcasted_iota(jnp.int32, (rows, lanes), 1)


def plan_kernel(home_cap, rep_cap, table_in, ids_in, gates_in, x_in, xg, kept_out, *scratch):
    table, ids, gates, sem = scratch
    tokens, width = x_in.shape
    extra = xg.shape[0] - tokens
    pairs = (
        (table_in, table),
        (ids_in, ids),
        (gates_in, gates),
        (x_in, xg.at[pl.ds(0, tokens)]),
    )
    copies = [pltpu.make_async_copy(src, dst, sem.at[i]) for i, (src, dst) in enumerate(pairs)]
    for c in copies:
        c.start()
    devices = table.shape[1]
    earlier = row_iota(tokens, tokens) < lane_iota(tokens, tokens)
    earlier = jnp.where(earlier, 1.0, 0.0).astype(bf16)
    expert = row_iota(devices, tokens)
    for c in copies[:3]:
        c.wait()
    hosts = jnp.where(table[...] == row_iota(devices, devices), 1.0, 0.0)
    copied = 1.0 + jnp.sum(hosts, axis=1, keepdims=True)
    named = jnp.zeros((devices, tokens), f32)
    weight = jnp.zeros((devices, tokens), f32)
    for k in range(TOP):
        hit = expert == ids[k : k + 1]
        named = jnp.where(hit, 1.0, named)
        weight = jnp.where(hit, gates[k : k + 1].astype(f32), weight)
    rank = jnp.dot(named.astype(bf16), earlier, preferred_element_type=f32)
    turn = rank + lax.axis_index("expert").astype(f32)
    at_home = turn == copied * jnp.floor(turn / copied + 0.5)
    cap = jnp.where(at_home, float(home_cap), float(rep_cap))
    kept = jnp.where((named > 0.0) & (rank < cap * copied), 1.0, 0.0)
    kept_out[...] = kept
    dense = weight * kept
    for k in range(width // tokens):
        part = jnp.zeros((extra, tokens), f32)
        if k * extra < devices:
            part = dense[k * extra : (k + 1) * extra]
        xg[tokens:, k * tokens : (k + 1) * tokens] = part.astype(bf16)
    copies[3].wait()


def plan(table, ids, gates, x, devices, extra):
    tokens, width = x.shape
    home_cap = max(2, 5 * tokens * TOP // (4 * devices))
    rep_cap = max(2, tokens * TOP // (2 * devices))
    return pl.pallas_call(
        functools.partial(plan_kernel, home_cap, rep_cap),
        out_shape=(
            jax.ShapeDtypeStruct((tokens + extra, width), bf16),
            jax.ShapeDtypeStruct((devices, tokens), f32),
        ),
        in_specs=[HBM] * 4,
        out_specs=(VMEM, VMEM),
        scratch_shapes=[
            pltpu.VMEM(table.shape, jnp.int32),
            pltpu.VMEM(ids.shape, jnp.int32),
            pltpu.VMEM(gates.shape, bf16),
            pltpu.SemaphoreType.DMA((4,)),
        ],
        compiler_params=params(PLAN_MIB),
        name="plan",
    )(table, ids, gates, x)


def hold_kernel(out):
    out[...] = jnp.zeros_like(out)


def hold(flops):
    return pl.pallas_call(
        hold_kernel,
        out_shape=jax.ShapeDtypeStruct((8, LANES), f32),
        out_specs=VMEM,
        compiler_params=params(1),
        cost_estimate=pl.CostEstimate(flops=flops, bytes_accessed=1000, transcendentals=0),
        name="hold",
    )()


def rows_kernel(slots, *refs):
    xg, dy = refs[:slots], refs[slots : 2 * slots]
    weights = refs[2 * slots : 2 * slots + 6]
    dxg, act = refs[2 * slots + 6 : 3 * slots + 6], refs[3 * slots + 6]
    tokens, width = dy[0].shape
    hidden = weights[2].shape[0]
    extra = xg[0].shape[0] - tokens
    per = max(1, ROW_BLOCK // tokens)
    me = lax.axis_index("expert")

    def stack(parts):
        return parts[0] if len(parts) == 1 else jnp.concatenate(parts, axis=0)

    def unpack(ref):
        total = jnp.zeros((extra, tokens), f32)
        for c in range(width // tokens):
            part = ref[tokens:, c * tokens : (c + 1) * tokens].astype(f32)
            total = jnp.where(me // extra == c, part, total)
        return total.T

    for at in range(0, slots, per):
        group = range(at, min(slots, at + per))
        x = stack([xg[i][:tokens] for i in group])
        up_grad = stack([dy[i][...] for i in group])
        rows = len(group) * tokens
        here = pl.ds(at * tokens, rows)
        gates = stack([unpack(xg[i]) for i in group])
        lane = lane_iota(rows, LANES)
        dx, gg = 0.0, 0.0
        for j in range(2):
            w_gate, w_up, w_down = weights[3 * j : 3 * j + 3]
            a = jnp.dot(x, w_gate[...], preferred_element_type=f32)
            b = jnp.dot(x, w_up[...], preferred_element_type=f32)
            back = lax.dot_general(up_grad, w_down[...], nt, preferred_element_type=f32)
            column = (me if j == 0 else me ^ 1) % extra
            gate = jnp.sum(
                jnp.where(lane_iota(rows, extra) == column, gates, 0.0), axis=1, keepdims=True
            )
            sig = jax.nn.sigmoid(a)
            silu = a * sig
            h = silu * b
            dots = jnp.sum(h.astype(bf16).astype(f32) * back, axis=1, keepdims=True)
            scaled = gate * back
            da = (scaled * b * sig * (1.0 + a * (1.0 - sig))).astype(bf16)
            db = (scaled * silu).astype(bf16)
            first = j * 3 * hidden
            act[here, first : first + hidden] = da
            act[here, first + hidden : first + 2 * hidden] = db
            act[here, first + 2 * hidden : first + 3 * hidden] = (gate * h).astype(bf16)
            dx += lax.dot_general(da, w_gate[...], nt, preferred_element_type=f32)
            dx += lax.dot_general(db, w_up[...], nt, preferred_element_type=f32)
            gg += jnp.where(lane == column, dots, 0.0)
        for k, i in enumerate(group):
            part = slice(k * tokens, (k + 1) * tokens)
            dxg[i][:tokens] = dx[part].astype(bf16)
            packed = gg[part].T[:extra]
            for c in range(width // tokens):
                dxg[i][tokens:, c * tokens : (c + 1) * tokens] = jnp.where(
                    me // extra == c, packed, 0.0
                ).astype(bf16)


def rows_grads(xgs, dys, weights):
    slots = len(dys)
    tokens, width = dys[0].shape
    full = xgs[0].shape[0]
    hidden = weights[2].shape[0]
    rows = slots * tokens
    flops = 1 * rows * 2 * 5 * width * hidden
    moved = 12 * rows * width + 12 * width * hidden + 12 * rows * hidden
    return pl.pallas_call(
        functools.partial(rows_kernel, slots),
        out_shape=tuple(jax.ShapeDtypeStruct((full, width), bf16) for _ in dys)
        + (jax.ShapeDtypeStruct((rows, 6 * hidden), bf16),),
        in_specs=[VMEM] * (2 * slots + 6),
        out_specs=(VMEM,) * (slots + 1),
        compiler_params=params(20),
        cost_estimate=pl.CostEstimate(
            flops=flops, bytes_accessed=moved, transcendentals=2 * rows * hidden
        ),
        name="rows_grads",
    )(*xgs, *dys, *weights)


def weights_kernel(j, slots, steps, extra, *refs):
    xg_in, dy_in, act_in = refs[:slots], refs[slots : 2 * slots], refs[2 * slots : 2 * slots + steps]
    refs = refs[2 * slots + steps :]
    more, refs = refs[:extra], refs[extra:]
    gate_out, up_out, down_out = refs[:3]
    x, dy, act, sem = refs[3:]
    tokens, width = dy_in[0].shape
    hidden = act.shape[1] // 3
    step_rows = act_in[0].shape[0]
    copies = []

    def fetch(src, dst):
        copies.append(pltpu.make_async_copy(src, dst, sem.at[len(copies)]))
        copies[-1].start()

    for i in range(steps):
        fetch(
            act_in[i].at[:, pl.ds(j * 3 * hidden, 3 * hidden)],
            act.at[pl.ds(i * step_rows, step_rows)],
        )
    for i in range(slots):
        fetch(xg_in[i].at[pl.ds(0, tokens)], x.at[pl.ds(i * tokens, tokens)])
    for i in range(slots):
        fetch(dy_in[i], dy.at[pl.ds(i * tokens, tokens)])
    for c in copies[: steps + slots]:
        c.wait()

    def put(out, here, value, k):
        if extra:
            value = value + more[k][here].astype(f32)
        if len(out.shape) == 3:
            out[0, here[0], here[1]] = value.astype(out.dtype)
        else:
            out[here[0], here[1]] = value.astype(out.dtype)

    part = math.gcd(width, 256)
    everything = slice(None)
    for m in range(0, width, part):
        here = (slice(m, m + part), everything)
        both = lax.dot_general(
            x[:, m : m + part], act[:, : 2 * hidden], tn, preferred_element_type=f32
        )
        put(gate_out, here, both[:, :hidden], 0)
        put(up_out, here, both[:, hidden:], 1)
    for c in copies[steps + slots :]:
        c.wait()
    part = math.gcd(hidden, 128)
    for m in range(0, hidden, part):
        here = (slice(m, m + part), everything)
        value = lax.dot_general(
            act[:, 2 * hidden + m : 2 * hidden + m + part], dy[...], tn, preferred_element_type=f32
        )
        put(down_out, here, value, 2)


def weights_grads(j, xgs, dys, acts, dtype, more=()):
    slots, steps = len(dys), len(acts)
    tokens, width = dys[0].shape
    hidden = acts[0].shape[1] // 6
    rows = slots * tokens
    lead = (1,) if more else ()
    return pl.pallas_call(
        functools.partial(weights_kernel, j, slots, steps, len(more)),
        out_shape=(
            jax.ShapeDtypeStruct(lead + (width, hidden), dtype),
            jax.ShapeDtypeStruct(lead + (width, hidden), dtype),
            jax.ShapeDtypeStruct(lead + (hidden, width), dtype),
        ),
        in_specs=[ANY] * (2 * slots + steps) + [VMEM] * len(more),
        out_specs=(VMEM,) * 3,
        scratch_shapes=[
            pltpu.VMEM((rows, width), bf16),
            pltpu.VMEM((rows, width), bf16),
            pltpu.VMEM((rows, 3 * hidden), bf16),
            pltpu.SemaphoreType.DMA((2 * slots + steps,)),
        ],
        compiler_params=params(20),
        cost_estimate=pl.CostEstimate(
            flops=1000,
            bytes_accessed=1000,
            transcendentals=0,
        ),
        name="weights_grads",
    )(*xgs, *dys, *acts, *more)


def finish_kernel(parts, ids, kept, *refs):
    pieces, (_, tokens_out, gates_out) = refs[:parts], refs[parts:]
    tokens, width = tokens_out.shape
    total = pieces[0][...].astype(f32)
    for p in pieces[1:]:
        total = total + p[...].astype(f32)
    tokens_out[...] = total[:tokens].astype(bf16)
    devices = kept.shape[0]
    extra = pieces[0].shape[0] - tokens
    gg = [total[tokens:, k * tokens : (k + 1) * tokens] for k in range(devices // extra)]
    gg = jnp.concatenate(gg, axis=0) * kept[...]
    expert = row_iota(devices, tokens)
    place = row_iota(TOP, tokens)
    out = jnp.zeros((TOP, tokens), f32)
    for k in range(TOP):
        value = jnp.sum(jnp.where(expert == ids[k : k + 1], gg, 0.0), axis=0, keepdims=True)
        out = jnp.where(place == k, value, out)
    gates_out[...] = out.astype(bf16)


def finish(ids, kept, pieces, mark, width):
    tokens = ids.shape[1]
    return pl.pallas_call(
        functools.partial(finish_kernel, len(pieces)),
        out_shape=(
            jax.ShapeDtypeStruct((tokens, width), bf16),
            jax.ShapeDtypeStruct((TOP, tokens), bf16),
        ),
        in_specs=[VMEM] * (2 + len(pieces)) + [ANY],
        out_specs=(VMEM, VMEM),
        compiler_params=params(16),
        name="finish",
    )(ids, kept, *pieces, mark)


def add(*terms):
    total = terms[0].astype(f32)
    for t in terms[1:]:
        total = total + t.astype(f32)
    return total.astype(bf16)


def on_device(tokens_in, grad_out, gates, expert_ids, replica_table, w_gate, w_up, w_down):
    devices = lax.axis_size("expert")
    tokens, width = tokens_in.shape
    extra = 8 * -(-devices * tokens // (8 * width))
    chips = devices // CORES
    inner = 2 ** (int(math.log2(chips)) // 2)
    outer = chips // inner

    def moved(i, dz, dy):
        core, chip = i % CORES, i // CORES
        z, y = chip // inner, chip % inner
        return (((z + dz) % outer) * inner + (y + dy) % inner) * CORES + core

    def send_z(v):
        return lax.ppermute(v, "expert", [(i, moved(i, 1, 0)) for i in range(devices)])

    def send_down(v):
        return lax.ppermute(v, "expert", [(i, moved(i, -1, 0)) for i in range(devices)])

    def send_y(v):
        return lax.ppermute(v, "expert", [(i, moved(i, 0, 1)) for i in range(devices)])

    def send_core(v):
        return lax.ppermute(v, "expert", [(i, i ^ 1) for i in range(devices)])

    def together(*values):
        return lax.optimization_barrier(values)

    ids = expert_ids.T
    xg, kept = plan(replica_table[None], ids, gates.T, tokens_in, devices, extra)
    own = (w_gate[0], w_up[0], w_down[0])
    weights = own + tuple(send_core(w) for w in own)

    per = max(1, W_ROWS // (inner * tokens))
    groups = [range(z, min(outer, z + per)) for z in range(0, outer, per)]
    sums = [None, None]

    def partial(j, group, dtype, more=()):
        return weights_grads(
            j,
            [x for z in group for x in xgs[z]],
            [d for z in group for d in dys[z]],
            [acts[z] for z in group],
            dtype,
            more,
        )

    xgs, dys, mark = [[xg]], [[grad_out]], kept
    dxs, acts, across = [], [], []

    def send_across(z):
        if inner == 1:
            return []
        total = dxs[z][1]
        for y in range(2, inner):
            total = add(send_y(total), dxs[z][y])
        return [send_y(total)]

    for z in range(1, outer + 1):
        for k, stream in enumerate((xgs, dys)):
            last = stream[z - 1]
            ahead = None
            if z < outer:
                ahead = send_z(last[0])
            for y in range(1, inner):
                if k and z == outer > 1 and y == inner - 1:
                    last.append(send_z(stream[z - 2][y]))
                else:
                    last.append(send_y(last[y - 1]))
            done = [last[-1]] if inner > 1 else []
            if ahead is not None:
                done.append(ahead)
            if k == 0 and z == 1:
                done, mark, held = together(done, hold(HOLD), weights[3:5])
                weights = own + held + weights[5:]
            elif z == 1:
                done, held = together(done, weights[5:])
                weights = weights[:5] + held
            elif k == 0:
                done, acts[z - 2] = together(done, acts[z - 2])
            else:
                (done,) = together(done)
            if ahead is not None:
                stream.append([done.pop()])
            if inner > 1:
                last[-1] = done.pop()
        if z == outer > 2:
            first, xgs[z - 1] = together(send_z(dxs[1][0]), xgs[z - 1])
        *dx, act = rows_grads(xgs[z - 1], dys[z - 1], weights)
        dxs.append(dx)
        acts.append(act)
        if z > 2:
            across.append(send_across(z - 1))
        if len(groups) > 1 and z - 1 == groups[(z - 1) // per][-1]:
            for j in range(2):
                value = partial(j, groups[(z - 1) // per], f32)
                sums[j] = value if z <= per else [t + v for t, v in zip(sums[j], value)]
            if z < outer:
                sums, xgs[z] = together(sums, xgs[z])

    single = len(groups) == 1
    if single:
        other = [send_core(v) for v in partial(1, groups[0], bf16)]
    else:
        other = [send_core(v.astype(bf16)) for v in sums[1]]

    pieces = []
    if outer > 1:
        if outer == 2:
            pieces.append(send_z(dxs[1][0]))
        dxs[1], acts[-2] = together(dxs[1], acts[-2])
        down = [send_down(v) for v in dxs[1][1:]]
        dxs[0] = [dxs[0][0]] + [add(v, o) for v, o in zip(dxs[0][1:], down)]
    pieces += [dxs[0][0], *send_across(0)]
    if outer > 2:
        total = add(dxs[2][0], first, *across[0])
        for z in range(3, outer):
            total = add(send_z(total), dxs[z][0], *across[z - 2])
        _, other = together(total, other)
        pieces.append(send_z(total))
    if single:
        grad_w = partial(0, groups[0], bf16, other)
    else:
        grad_w = [(v + o.astype(f32)).astype(bf16)[None] for v, o in zip(sums[0], other)]
    pieces, grad_w = together(pieces, grad_w)
    grad_tokens, grad_gates = finish(ids, kept, pieces, mark, width)
    grad_gates = grad_gates.T
    return (grad_tokens, grad_gates, *grad_w)


def solution(mesh):
    both = ("groups", "expert")
    return jax.shard_map(
        on_device,
        mesh=mesh,
        in_specs=(
            P(both, None),
            P(both, None),
            P(both, None),
            P(both, None),
            P("groups"),
            P("expert", None, None),
            P("expert", None, None),
            P("expert", None, None),
        ),
        out_specs=(
            P(both, None),
            P(both, None),
            P(both, None, None),
            P(both, None, None),
            P(both, None, None),
        ),
        check_vma=False,
    )
```

```python
import functools
import math

import jax
import jax.numpy as jnp
from jax import lax
from jax.experimental import pallas as pl
from jax.experimental.pallas import tpu as pltpu
from jax.sharding import PartitionSpec as P

TOP = 8
CORES = 2
LANES = 128
ROW_BLOCK = 256
W_ROWS = 1024
HOLD = 10**10
PLAN_MIB = 60

f32 = jnp.float32
bf16 = jnp.bfloat16
nt = (((1,), (1,)), ((), ()))
tn = (((0,), (0,)), ((), ()))
VMEM = pl.BlockSpec(memory_space=pltpu.VMEM)
ANY = pl.BlockSpec(memory_space=pl.ANY)
HBM = pl.BlockSpec(memory_space=pltpu.HBM)


def params(mib):
    return pltpu.CompilerParams(vmem_limit_bytes=mib * 1024 * 1024)


def row_iota(rows, lanes):
    return lax.broadcasted_iota(jnp.int32, (rows, lanes), 0)


def lane_iota(rows, lanes):
    return lax.broadcasted_iota(jnp.int32, (rows, lanes), 1)


def plan_kernel(home_cap, rep_cap, table_in, ids_in, gates_in, x_in, xg, kept_out, *scratch):
    table, ids, gates, sem = scratch
    tokens, width = x_in.shape
    extra = xg.shape[0] - tokens
    pairs = (
        (table_in, table),
        (ids_in, ids),
        (gates_in, gates),
        (x_in, xg.at[pl.ds(0, tokens)]),
    )
    copies = [pltpu.make_async_copy(src, dst, sem.at[i]) for i, (src, dst) in enumerate(pairs)]
    for c in copies:
        c.start()
    devices = table.shape[1]
    earlier = row_iota(tokens, tokens) < lane_iota(tokens, tokens)
    earlier = jnp.where(earlier, 1.0, 0.0).astype(bf16)
    expert = row_iota(devices, tokens)
    for c in copies[:3]:
        c.wait()
    hosts = jnp.where(table[...] == row_iota(devices, devices), 1.0, 0.0)
    copied = 1.0 + jnp.sum(hosts, axis=1, keepdims=True)
    named = jnp.zeros((devices, tokens), f32)
    weight = jnp.zeros((devices, tokens), f32)
    for k in range(TOP):
        hit = expert == ids[k : k + 1]
        named = jnp.where(hit, 1.0, named)
        weight = jnp.where(hit, gates[k : k + 1].astype(f32), weight)
    rank = jnp.dot(named.astype(bf16), earlier, preferred_element_type=f32)
    turn = rank + lax.axis_index("expert").astype(f32)
    at_home = turn == copied * jnp.floor(turn / copied + 0.5)
    cap = jnp.where(at_home, float(home_cap), float(rep_cap))
    kept = jnp.where((named > 0.0) & (rank < cap * copied), 1.0, 0.0)
    kept_out[...] = kept
    dense = weight * kept
    for k in range(width // tokens):
        part = jnp.zeros((extra, tokens), f32)
        if k * extra < devices:
            part = dense[k * extra : (k + 1) * extra]
        xg[tokens:, k * tokens : (k + 1) * tokens] = part.astype(bf16)
    copies[3].wait()


def plan(table, ids, gates, x, devices, extra):
    tokens, width = x.shape
    home_cap = max(2, 5 * tokens * TOP // (4 * devices))
    rep_cap = max(2, tokens * TOP // (2 * devices))
    return pl.pallas_call(
        functools.partial(plan_kernel, home_cap, rep_cap),
        out_shape=(
            jax.ShapeDtypeStruct((tokens + extra, width), bf16),
            jax.ShapeDtypeStruct((devices, tokens), f32),
        ),
        in_specs=[HBM] * 4,
        out_specs=(VMEM, VMEM),
        scratch_shapes=[
            pltpu.VMEM(table.shape, jnp.int32),
            pltpu.VMEM(ids.shape, jnp.int32),
            pltpu.VMEM(gates.shape, bf16),
            pltpu.SemaphoreType.DMA((4,)),
        ],
        compiler_params=params(PLAN_MIB),
        name="plan",
    )(table, ids, gates, x)


def hold_kernel(out):
    out[...] = jnp.zeros_like(out)


def hold(flops):
    return pl.pallas_call(
        hold_kernel,
        out_shape=jax.ShapeDtypeStruct((8, LANES), f32),
        out_specs=VMEM,
        compiler_params=params(1),
        cost_estimate=pl.CostEstimate(flops=flops, bytes_accessed=1000, transcendentals=0),
        name="hold",
    )()


def rows_kernel(slots, *refs):
    xg, dy = refs[:slots], refs[slots : 2 * slots]
    weights = refs[2 * slots : 2 * slots + 6]
    dxg, act = refs[2 * slots + 6 : 3 * slots + 6], refs[3 * slots + 6]
    tokens, width = dy[0].shape
    hidden = weights[2].shape[0]
    extra = xg[0].shape[0] - tokens
    per = max(1, ROW_BLOCK // tokens)
    me = lax.axis_index("expert")

    def stack(parts):
        return parts[0] if len(parts) == 1 else jnp.concatenate(parts, axis=0)

    def unpack(ref):
        total = jnp.zeros((extra, tokens), f32)
        for c in range(width // tokens):
            part = ref[tokens:, c * tokens : (c + 1) * tokens].astype(f32)
            total = jnp.where(me // extra == c, part, total)
        return total.T

    for at in range(0, slots, per):
        group = range(at, min(slots, at + per))
        x = stack([xg[i][:tokens] for i in group])
        up_grad = stack([dy[i][...] for i in group])
        rows = len(group) * tokens
        here = pl.ds(at * tokens, rows)
        gates = stack([unpack(xg[i]) for i in group])
        lane = lane_iota(rows, LANES)
        dx, gg = 0.0, 0.0
        for j in range(2):
            w_gate, w_up, w_down = weights[3 * j : 3 * j + 3]
            a = jnp.dot(x, w_gate[...], preferred_element_type=f32)
            b = jnp.dot(x, w_up[...], preferred_element_type=f32)
            back = lax.dot_general(up_grad, w_down[...], nt, preferred_element_type=f32)
            column = (me if j == 0 else me ^ 1) % extra
            gate = jnp.sum(
                jnp.where(lane_iota(rows, extra) == column, gates, 0.0), axis=1, keepdims=True
            )
            sig = jax.nn.sigmoid(a)
            silu = a * sig
            h = silu * b
            dots = jnp.sum(h.astype(bf16).astype(f32) * back, axis=1, keepdims=True)
            scaled = gate * back
            da = (scaled * b * sig * (1.0 + a * (1.0 - sig))).astype(bf16)
            db = (scaled * silu).astype(bf16)
            first = j * 3 * hidden
            act[here, first : first + hidden] = da
            act[here, first + hidden : first + 2 * hidden] = db
            act[here, first + 2 * hidden : first + 3 * hidden] = (gate * h).astype(bf16)
            dx += lax.dot_general(da, w_gate[...], nt, preferred_element_type=f32)
            dx += lax.dot_general(db, w_up[...], nt, preferred_element_type=f32)
            gg += jnp.where(lane == column, dots, 0.0)
        for k, i in enumerate(group):
            part = slice(k * tokens, (k + 1) * tokens)
            dxg[i][:tokens] = dx[part].astype(bf16)
            packed = gg[part].T[:extra]
            for c in range(width // tokens):
                dxg[i][tokens:, c * tokens : (c + 1) * tokens] = jnp.where(
                    me // extra == c, packed, 0.0
                ).astype(bf16)


def rows_grads(xgs, dys, weights):
    slots = len(dys)
    tokens, width = dys[0].shape
    full = xgs[0].shape[0]
    hidden = weights[2].shape[0]
    rows = slots * tokens
    flops = 1 * rows * 2 * 5 * width * hidden
    moved = 12 * rows * width + 12 * width * hidden + 12 * rows * hidden
    return pl.pallas_call(
        functools.partial(rows_kernel, slots),
        out_shape=tuple(jax.ShapeDtypeStruct((full, width), bf16) for _ in dys)
        + (jax.ShapeDtypeStruct((rows, 6 * hidden), bf16),),
        in_specs=[VMEM] * (2 * slots + 6),
        out_specs=(VMEM,) * (slots + 1),
        compiler_params=params(20),
        cost_estimate=pl.CostEstimate(
            flops=flops, bytes_accessed=moved, transcendentals=2 * rows * hidden
        ),
        name="rows_grads",
    )(*xgs, *dys, *weights)


def weights_kernel(j, slots, steps, extra, *refs):
    xg_in, dy_in, act_in = refs[:slots], refs[slots : 2 * slots], refs[2 * slots : 2 * slots + steps]
    refs = refs[2 * slots + steps :]
    more, refs = refs[:extra], refs[extra:]
    gate_out, up_out, down_out = refs[:3]
    x, dy, act, sem = refs[3:]
    tokens, width = dy_in[0].shape
    hidden = act.shape[1] // 3
    step_rows = act_in[0].shape[0]
    copies = []

    def fetch(src, dst):
        copies.append(pltpu.make_async_copy(src, dst, sem.at[len(copies)]))
        copies[-1].start()

    for i in range(steps):
        fetch(
            act_in[i].at[:, pl.ds(j * 3 * hidden, 3 * hidden)],
            act.at[pl.ds(i * step_rows, step_rows)],
        )
    for i in range(slots):
        fetch(xg_in[i].at[pl.ds(0, tokens)], x.at[pl.ds(i * tokens, tokens)])
    for i in range(slots):
        fetch(dy_in[i], dy.at[pl.ds(i * tokens, tokens)])
    for c in copies[: steps + slots]:
        c.wait()

    def put(out, here, value, k):
        if extra:
            value = value + more[k][here].astype(f32)
        if len(out.shape) == 3:
            out[0, here[0], here[1]] = value.astype(out.dtype)
        else:
            out[here[0], here[1]] = value.astype(out.dtype)

    part = math.gcd(width, 256)
    everything = slice(None)
    for m in range(0, width, part):
        here = (slice(m, m + part), everything)
        both = lax.dot_general(
            x[:, m : m + part], act[:, : 2 * hidden], tn, preferred_element_type=f32
        )
        put(gate_out, here, both[:, :hidden], 0)
        put(up_out, here, both[:, hidden:], 1)
    for c in copies[steps + slots :]:
        c.wait()
    part = math.gcd(hidden, 128)
    for m in range(0, hidden, part):
        here = (slice(m, m + part), everything)
        value = lax.dot_general(
            act[:, 2 * hidden + m : 2 * hidden + m + part], dy[...], tn, preferred_element_type=f32
        )
        put(down_out, here, value, 2)


def weights_grads(j, xgs, dys, acts, dtype, more=()):
    slots, steps = len(dys), len(acts)
    tokens, width = dys[0].shape
    hidden = acts[0].shape[1] // 6
    rows = slots * tokens
    lead = (1,) if more else ()
    return pl.pallas_call(
        functools.partial(weights_kernel, j, slots, steps, len(more)),
        out_shape=(
            jax.ShapeDtypeStruct(lead + (width, hidden), dtype),
            jax.ShapeDtypeStruct(lead + (width, hidden), dtype),
            jax.ShapeDtypeStruct(lead + (hidden, width), dtype),
        ),
        in_specs=[ANY] * (2 * slots + steps) + [VMEM] * len(more),
        out_specs=(VMEM,) * 3,
        scratch_shapes=[
            pltpu.VMEM((rows, width), bf16),
            pltpu.VMEM((rows, width), bf16),
            pltpu.VMEM((rows, 3 * hidden), bf16),
            pltpu.SemaphoreType.DMA((2 * slots + steps,)),
        ],
        compiler_params=params(20),
        cost_estimate=pl.CostEstimate(
            flops=1000,
            bytes_accessed=1000,
            transcendentals=0,
        ),
        name="weights_grads",
    )(*xgs, *dys, *acts, *more)


def finish_kernel(parts, ids, kept, *refs):
    pieces, (_, tokens_out, gates_out) = refs[:parts], refs[parts:]
    tokens, width = tokens_out.shape
    total = pieces[0][...].astype(f32)
    for p in pieces[1:]:
        total = total + p[...].astype(f32)
    tokens_out[...] = total[:tokens].astype(bf16)
    devices = kept.shape[0]
    extra = pieces[0].shape[0] - tokens
    gg = [total[tokens:, k * tokens : (k + 1) * tokens] for k in range(devices // extra)]
    gg = jnp.concatenate(gg, axis=0) * kept[...]
    expert = row_iota(devices, tokens)
    place = row_iota(TOP, tokens)
    out = jnp.zeros((TOP, tokens), f32)
    for k in range(TOP):
        value = jnp.sum(jnp.where(expert == ids[k : k + 1], gg, 0.0), axis=0, keepdims=True)
        out = jnp.where(place == k, value, out)
    gates_out[...] = out.astype(bf16)


def finish(ids, kept, pieces, mark, width):
    tokens = ids.shape[1]
    return pl.pallas_call(
        functools.partial(finish_kernel, len(pieces)),
        out_shape=(
            jax.ShapeDtypeStruct((tokens, width), bf16),
            jax.ShapeDtypeStruct((TOP, tokens), bf16),
        ),
        in_specs=[VMEM] * (2 + len(pieces)) + [ANY],
        out_specs=(VMEM, VMEM),
        compiler_params=params(16),
        name="finish",
    )(ids, kept, *pieces, mark)


def add(*terms):
    total = terms[0].astype(f32)
    for t in terms[1:]:
        total = total + t.astype(f32)
    return total.astype(bf16)


def on_device(tokens_in, grad_out, gates, expert_ids, replica_table, w_gate, w_up, w_down):
    devices = lax.axis_size("expert")
    tokens, width = tokens_in.shape
    extra = 8 * -(-devices * tokens // (8 * width))
    chips = devices // CORES
    inner = 2 ** (int(math.log2(chips)) // 2)
    outer = chips // inner

    def moved(i, dz, dy):
        core, chip = i % CORES, i // CORES
        z, y = chip // inner, chip % inner
        return (((z + dz) % outer) * inner + (y + dy) % inner) * CORES + core

    def send_z(v):
        return lax.ppermute(v, "expert", [(i, moved(i, 1, 0)) for i in range(devices)])

    def send_down(v):
        return lax.ppermute(v, "expert", [(i, moved(i, -1, 0)) for i in range(devices)])

    def send_y(v):
        return lax.ppermute(v, "expert", [(i, moved(i, 0, 1)) for i in range(devices)])

    def send_core(v):
        return lax.ppermute(v, "expert", [(i, i ^ 1) for i in range(devices)])

    def together(*values):
        return lax.optimization_barrier(values)

    ids = expert_ids.T
    xg, kept = plan(replica_table[None], ids, gates.T, tokens_in, devices, extra)
    own = (w_gate[0], w_up[0], w_down[0])
    weights = own + tuple(send_core(w) for w in own)

    per = max(1, W_ROWS // (inner * tokens))
    groups = [range(z, min(outer, z + per)) for z in range(0, outer, per)]
    sums = [None, None]

    def partial(j, group, dtype, more=()):
        return weights_grads(
            j,
            [x for z in group for x in xgs[z]],
            [d for z in group for d in dys[z]],
            [acts[z] for z in group],
            dtype,
            more,
        )

    xgs, dys, mark = [[xg]], [[grad_out]], kept
    dxs, acts, across = [], [], []

    def send_across(z):
        if inner == 1:
            return []
        total = dxs[z][1]
        for y in range(2, inner):
            total = add(send_y(total), dxs[z][y])
        return [send_y(total)]

    for z in range(1, outer + 1):
        for k, stream in enumerate((xgs, dys)):
            last = stream[z - 1]
            ahead = None
            if z < outer:
                ahead = send_z(last[0])
            for y in range(1, inner):
                if k and z == outer > 1 and y == inner - 1:
                    last.append(send_z(stream[z - 2][y]))
                else:
                    last.append(send_y(last[y - 1]))
            done = [last[-1]] if inner > 1 else []
            if ahead is not None:
                done.append(ahead)
            if k == 0 and z == 1:
                done, mark, held = together(done, hold(HOLD), weights[3:5])
                weights = own + held + weights[5:]
            elif z == 1:
                done, held = together(done, weights[5:])
                weights = weights[:5] + held
            elif k == 0:
                done, acts[z - 2] = together(done, acts[z - 2])
            else:
                (done,) = together(done)
            if ahead is not None:
                stream.append([done.pop()])
            if inner > 1:
                last[-1] = done.pop()
        if z == outer > 2:
            first, xgs[z - 1] = together(send_z(dxs[1][0]), xgs[z - 1])
        *dx, act = rows_grads(xgs[z - 1], dys[z - 1], weights)
        dxs.append(dx)
        acts.append(act)
        if z > 2:
            across.append(send_across(z - 1))
        if len(groups) > 1 and z - 1 == groups[(z - 1) // per][-1]:
            for j in range(2):
                value = partial(j, groups[(z - 1) // per], f32)
                sums[j] = value if z <= per else [t + v for t, v in zip(sums[j], value)]
            if z < outer:
                sums, xgs[z] = together(sums, xgs[z])

    if outer > 1:
        down = [send_down(v) for v in dxs[1][1:]]
    single = len(groups) == 1
    if single:
        other = [send_core(v) for v in partial(1, groups[0], bf16)]
    else:
        other = [send_core(v.astype(bf16)) for v in sums[1]]

    pieces = []
    if outer > 1:
        if outer == 2:
            pieces.append(send_z(dxs[1][0]))
        dxs[0] = [dxs[0][0]] + [add(v, o) for v, o in zip(dxs[0][1:], down)]
    pieces += [dxs[0][0], *send_across(0)]
    if outer > 2:
        total = add(dxs[2][0], first, *across[0])
        for z in range(3, outer):
            total = add(send_z(total), dxs[z][0], *across[z - 2])
        _, other = together(total, other)
        pieces.append(send_z(total))
    if single:
        grad_w = partial(0, groups[0], bf16, other)
    else:
        grad_w = [(v + o.astype(f32)).astype(bf16)[None] for v, o in zip(sums[0], other)]
    pieces, grad_w = together(pieces, grad_w)
    grad_tokens, grad_gates = finish(ids, kept, pieces, mark, width)
    grad_gates = grad_gates.T
    return (grad_tokens, grad_gates, *grad_w)


def solution(mesh):
    both = ("groups", "expert")
    return jax.shard_map(
        on_device,
        mesh=mesh,
        in_specs=(
            P(both, None),
            P(both, None),
            P(both, None),
            P(both, None),
            P("groups"),
            P("expert", None, None),
            P("expert", None, None),
            P("expert", None, None),
        ),
        out_specs=(
            P(both, None),
            P(both, None),
            P(both, None, None),
            P(both, None, None),
            P(both, None, None),
        ),
        check_vma=False,
    )
```

```python
import functools
import math

import jax
import jax.numpy as jnp
from jax import lax
from jax.experimental import pallas as pl
from jax.experimental.pallas import tpu as pltpu
from jax.sharding import PartitionSpec as P

TOP = 8
CORES = 2
LANES = 128
ROW_BLOCK = 256
W_ROWS = 1024
HOLD = 10**10
PLAN_MIB = 60

f32 = jnp.float32
bf16 = jnp.bfloat16
nt = (((1,), (1,)), ((), ()))
tn = (((0,), (0,)), ((), ()))
VMEM = pl.BlockSpec(memory_space=pltpu.VMEM)
ANY = pl.BlockSpec(memory_space=pl.ANY)
HBM = pl.BlockSpec(memory_space=pltpu.HBM)


def params(mib):
    return pltpu.CompilerParams(vmem_limit_bytes=mib * 1024 * 1024)


def row_iota(rows, lanes):
    return lax.broadcasted_iota(jnp.int32, (rows, lanes), 0)


def lane_iota(rows, lanes):
    return lax.broadcasted_iota(jnp.int32, (rows, lanes), 1)


def plan_kernel(home_cap, rep_cap, table_in, ids_in, gates_in, x_in, xg, kept_out, *scratch):
    table, ids, gates, sem = scratch
    tokens, width = x_in.shape
    extra = xg.shape[0] - tokens
    pairs = (
        (table_in, table),
        (ids_in, ids),
        (gates_in, gates),
        (x_in, xg.at[pl.ds(0, tokens)]),
    )
    copies = [pltpu.make_async_copy(src, dst, sem.at[i]) for i, (src, dst) in enumerate(pairs)]
    for c in copies:
        c.start()
    devices = table.shape[1]
    earlier = row_iota(tokens, tokens) < lane_iota(tokens, tokens)
    earlier = jnp.where(earlier, 1.0, 0.0).astype(bf16)
    expert = row_iota(devices, tokens)
    for c in copies[:3]:
        c.wait()
    hosts = jnp.where(table[...] == row_iota(devices, devices), 1.0, 0.0)
    copied = 1.0 + jnp.sum(hosts, axis=1, keepdims=True)
    named = jnp.zeros((devices, tokens), f32)
    weight = jnp.zeros((devices, tokens), f32)
    for k in range(TOP):
        hit = expert == ids[k : k + 1]
        named = jnp.where(hit, 1.0, named)
        weight = jnp.where(hit, gates[k : k + 1].astype(f32), weight)
    rank = jnp.dot(named.astype(bf16), earlier, preferred_element_type=f32)
    turn = rank + lax.axis_index("expert").astype(f32)
    at_home = turn == copied * jnp.floor(turn / copied + 0.5)
    cap = jnp.where(at_home, float(home_cap), float(rep_cap))
    kept = jnp.where((named > 0.0) & (rank < cap * copied), 1.0, 0.0)
    kept_out[...] = kept
    dense = weight * kept
    for k in range(width // tokens):
        part = jnp.zeros((extra, tokens), f32)
        if k * extra < devices:
            part = dense[k * extra : (k + 1) * extra]
        xg[tokens:, k * tokens : (k + 1) * tokens] = part.astype(bf16)
    copies[3].wait()


def plan(table, ids, gates, x, devices, extra):
    tokens, width = x.shape
    home_cap = max(2, 5 * tokens * TOP // (4 * devices))
    rep_cap = max(2, tokens * TOP // (2 * devices))
    return pl.pallas_call(
        functools.partial(plan_kernel, home_cap, rep_cap),
        out_shape=(
            jax.ShapeDtypeStruct((tokens + extra, width), bf16),
            jax.ShapeDtypeStruct((devices, tokens), f32),
        ),
        in_specs=[HBM] * 4,
        out_specs=(VMEM, VMEM),
        scratch_shapes=[
            pltpu.VMEM(table.shape, jnp.int32),
            pltpu.VMEM(ids.shape, jnp.int32),
            pltpu.VMEM(gates.shape, bf16),
            pltpu.SemaphoreType.DMA((4,)),
        ],
        compiler_params=params(PLAN_MIB),
        name="plan",
    )(table, ids, gates, x)


def hold_kernel(out):
    out[...] = jnp.zeros_like(out)


def hold(flops):
    return pl.pallas_call(
        hold_kernel,
        out_shape=jax.ShapeDtypeStruct((8, LANES), f32),
        out_specs=VMEM,
        compiler_params=params(1),
        cost_estimate=pl.CostEstimate(flops=flops, bytes_accessed=1000, transcendentals=0),
        name="hold",
    )()


def rows_kernel(slots, *refs):
    xg, dy = refs[:slots], refs[slots : 2 * slots]
    weights = refs[2 * slots : 2 * slots + 6]
    dxg, act = refs[2 * slots + 6 : 3 * slots + 6], refs[3 * slots + 6]
    tokens, width = dy[0].shape
    hidden = weights[2].shape[0]
    extra = xg[0].shape[0] - tokens
    per = max(1, ROW_BLOCK // tokens)
    me = lax.axis_index("expert")

    def stack(parts):
        return parts[0] if len(parts) == 1 else jnp.concatenate(parts, axis=0)

    def unpack(ref):
        total = jnp.zeros((extra, tokens), f32)
        for c in range(width // tokens):
            part = ref[tokens:, c * tokens : (c + 1) * tokens].astype(f32)
            total = jnp.where(me // extra == c, part, total)
        return total.T

    for at in range(0, slots, per):
        group = range(at, min(slots, at + per))
        x = stack([xg[i][:tokens] for i in group])
        up_grad = stack([dy[i][...] for i in group])
        rows = len(group) * tokens
        here = pl.ds(at * tokens, rows)
        gates = stack([unpack(xg[i]) for i in group])
        lane = lane_iota(rows, LANES)
        dx, gg = 0.0, 0.0
        for j in range(2):
            w_gate, w_up, w_down = weights[3 * j : 3 * j + 3]
            a = jnp.dot(x, w_gate[...], preferred_element_type=f32)
            b = jnp.dot(x, w_up[...], preferred_element_type=f32)
            back = lax.dot_general(up_grad, w_down[...], nt, preferred_element_type=f32)
            column = (me if j == 0 else me ^ 1) % extra
            gate = jnp.sum(
                jnp.where(lane_iota(rows, extra) == column, gates, 0.0), axis=1, keepdims=True
            )
            sig = jax.nn.sigmoid(a)
            silu = a * sig
            h = silu * b
            dots = jnp.sum(h.astype(bf16).astype(f32) * back, axis=1, keepdims=True)
            scaled = gate * back
            da = (scaled * b * sig * (1.0 + a * (1.0 - sig))).astype(bf16)
            db = (scaled * silu).astype(bf16)
            first = j * 3 * hidden
            act[here, first : first + hidden] = da
            act[here, first + hidden : first + 2 * hidden] = db
            act[here, first + 2 * hidden : first + 3 * hidden] = (gate * h).astype(bf16)
            dx += lax.dot_general(da, w_gate[...], nt, preferred_element_type=f32)
            dx += lax.dot_general(db, w_up[...], nt, preferred_element_type=f32)
            gg += jnp.where(lane == column, dots, 0.0)
        for k, i in enumerate(group):
            part = slice(k * tokens, (k + 1) * tokens)
            dxg[i][:tokens] = dx[part].astype(bf16)
            packed = gg[part].T[:extra]
            for c in range(width // tokens):
                dxg[i][tokens:, c * tokens : (c + 1) * tokens] = jnp.where(
                    me // extra == c, packed, 0.0
                ).astype(bf16)


def rows_grads(xgs, dys, weights):
    slots = len(dys)
    tokens, width = dys[0].shape
    full = xgs[0].shape[0]
    hidden = weights[2].shape[0]
    rows = slots * tokens
    flops = 1 * rows * 2 * 5 * width * hidden
    moved = 12 * rows * width + 12 * width * hidden + 12 * rows * hidden
    return pl.pallas_call(
        functools.partial(rows_kernel, slots),
        out_shape=tuple(jax.ShapeDtypeStruct((full, width), bf16) for _ in dys)
        + (jax.ShapeDtypeStruct((rows, 6 * hidden), bf16),),
        in_specs=[VMEM] * (2 * slots + 6),
        out_specs=(VMEM,) * (slots + 1),
        compiler_params=params(20),
        cost_estimate=pl.CostEstimate(
            flops=flops, bytes_accessed=moved, transcendentals=2 * rows * hidden
        ),
        name="rows_grads",
    )(*xgs, *dys, *weights)


def weights_kernel(j, slots, steps, extra, *refs):
    xg_in, dy_in, act_in = refs[:slots], refs[slots : 2 * slots], refs[2 * slots : 2 * slots + steps]
    refs = refs[2 * slots + steps :]
    more, refs = refs[:extra], refs[extra:]
    gate_out, up_out, down_out = refs[:3]
    x, dy, act, sem = refs[3:]
    tokens, width = dy_in[0].shape
    hidden = act.shape[1] // 3
    step_rows = act_in[0].shape[0]
    copies = []

    def fetch(src, dst):
        copies.append(pltpu.make_async_copy(src, dst, sem.at[len(copies)]))
        copies[-1].start()

    for i in range(steps):
        fetch(
            act_in[i].at[:, pl.ds(j * 3 * hidden, 3 * hidden)],
            act.at[pl.ds(i * step_rows, step_rows)],
        )
    for i in range(slots):
        fetch(xg_in[i].at[pl.ds(0, tokens)], x.at[pl.ds(i * tokens, tokens)])
    for i in range(slots):
        fetch(dy_in[i], dy.at[pl.ds(i * tokens, tokens)])
    for c in copies[: steps + slots]:
        c.wait()

    def put(out, here, value, k):
        if extra:
            value = value + more[k][here].astype(f32)
        if len(out.shape) == 3:
            out[0, here[0], here[1]] = value.astype(out.dtype)
        else:
            out[here[0], here[1]] = value.astype(out.dtype)

    part = math.gcd(width, 256)
    everything = slice(None)
    for m in range(0, width, part):
        here = (slice(m, m + part), everything)
        both = lax.dot_general(
            x[:, m : m + part], act[:, : 2 * hidden], tn, preferred_element_type=f32
        )
        put(gate_out, here, both[:, :hidden], 0)
        put(up_out, here, both[:, hidden:], 1)
    for c in copies[steps + slots :]:
        c.wait()
    part = math.gcd(hidden, 128)
    for m in range(0, hidden, part):
        here = (slice(m, m + part), everything)
        value = lax.dot_general(
            act[:, 2 * hidden + m : 2 * hidden + m + part], dy[...], tn, preferred_element_type=f32
        )
        put(down_out, here, value, 2)


def weights_grads(j, xgs, dys, acts, dtype, more=()):
    slots, steps = len(dys), len(acts)
    tokens, width = dys[0].shape
    hidden = acts[0].shape[1] // 6
    rows = slots * tokens
    lead = (1,) if more else ()
    return pl.pallas_call(
        functools.partial(weights_kernel, j, slots, steps, len(more)),
        out_shape=(
            jax.ShapeDtypeStruct(lead + (width, hidden), dtype),
            jax.ShapeDtypeStruct(lead + (width, hidden), dtype),
            jax.ShapeDtypeStruct(lead + (hidden, width), dtype),
        ),
        in_specs=[ANY] * (2 * slots + steps) + [VMEM] * len(more),
        out_specs=(VMEM,) * 3,
        scratch_shapes=[
            pltpu.VMEM((rows, width), bf16),
            pltpu.VMEM((rows, width), bf16),
            pltpu.VMEM((rows, 3 * hidden), bf16),
            pltpu.SemaphoreType.DMA((2 * slots + steps,)),
        ],
        compiler_params=params(20),
        cost_estimate=pl.CostEstimate(
            flops=1000,
            bytes_accessed=1000,
            transcendentals=0,
        ),
        name="weights_grads",
    )(*xgs, *dys, *acts, *more)


def finish_kernel(parts, ids, kept, *refs):
    pieces, (_, tokens_out, gates_out) = refs[:parts], refs[parts:]
    tokens, width = tokens_out.shape
    total = pieces[0][...].astype(f32)
    for p in pieces[1:]:
        total = total + p[...].astype(f32)
    tokens_out[...] = total[:tokens].astype(bf16)
    devices = kept.shape[0]
    extra = pieces[0].shape[0] - tokens
    gg = [total[tokens:, k * tokens : (k + 1) * tokens] for k in range(devices // extra)]
    gg = jnp.concatenate(gg, axis=0) * kept[...]
    expert = row_iota(devices, tokens)
    place = row_iota(TOP, tokens)
    out = jnp.zeros((TOP, tokens), f32)
    for k in range(TOP):
        value = jnp.sum(jnp.where(expert == ids[k : k + 1], gg, 0.0), axis=0, keepdims=True)
        out = jnp.where(place == k, value, out)
    gates_out[...] = out.astype(bf16)


def finish(ids, kept, pieces, mark, width):
    tokens = ids.shape[1]
    return pl.pallas_call(
        functools.partial(finish_kernel, len(pieces)),
        out_shape=(
            jax.ShapeDtypeStruct((tokens, width), bf16),
            jax.ShapeDtypeStruct((TOP, tokens), bf16),
        ),
        in_specs=[VMEM] * (2 + len(pieces)) + [ANY],
        out_specs=(VMEM, VMEM),
        compiler_params=params(16),
        name="finish",
    )(ids, kept, *pieces, mark)


def add(*terms):
    total = terms[0].astype(f32)
    for t in terms[1:]:
        total = total + t.astype(f32)
    return total.astype(bf16)


def on_device(tokens_in, grad_out, gates, expert_ids, replica_table, w_gate, w_up, w_down):
    devices = lax.axis_size("expert")
    tokens, width = tokens_in.shape
    extra = 8 * -(-devices * tokens // (8 * width))
    chips = devices // CORES
    inner = 2 ** (int(math.log2(chips)) // 2)
    outer = chips // inner

    def moved(i, dz, dy):
        core, chip = i % CORES, i // CORES
        z, y = chip // inner, chip % inner
        return (((z + dz) % outer) * inner + (y + dy) % inner) * CORES + core

    def send_z(v):
        return lax.ppermute(v, "expert", [(i, moved(i, 1, 0)) for i in range(devices)])

    def send_down(v):
        return lax.ppermute(v, "expert", [(i, moved(i, -1, 0)) for i in range(devices)])

    def send_y(v):
        return lax.ppermute(v, "expert", [(i, moved(i, 0, 1)) for i in range(devices)])

    def send_core(v):
        return lax.ppermute(v, "expert", [(i, i ^ 1) for i in range(devices)])

    def together(*values):
        return lax.optimization_barrier(values)

    ids = expert_ids.T
    xg, kept = plan(replica_table[None], ids, gates.T, tokens_in, devices, extra)
    own = (w_gate[0], w_up[0], w_down[0])
    weights = own + tuple(send_core(w) for w in own)

    per = max(1, W_ROWS // (inner * tokens))
    groups = [range(z, min(outer, z + per)) for z in range(0, outer, per)]
    sums = [None, None]

    def partial(j, group, dtype, more=()):
        return weights_grads(
            j,
            [x for z in group for x in xgs[z]],
            [d for z in group for d in dys[z]],
            [acts[z] for z in group],
            dtype,
            more,
        )

    xgs, dys, mark = [[xg]], [[grad_out]], kept
    dxs, acts, across = [], [], []

    def send_across(z):
        if inner == 1:
            return []
        total = dxs[z][1]
        for y in range(2, inner):
            total = add(send_y(total), dxs[z][y])
        return [send_y(total)]

    for z in range(1, outer + 1):
        for k, stream in enumerate((xgs, dys)):
            last = stream[z - 1]
            ahead = None
            if z < outer:
                ahead = send_z(last[0])
            for y in range(1, inner):
                if k and z == outer > 1 and y == inner - 1:
                    last.append(send_z(stream[z - 2][y]))
                else:
                    last.append(send_y(last[y - 1]))
            done = [last[-1]] if inner > 1 else []
            if ahead is not None:
                done.append(ahead)
            if k == 0 and z == 1:
                done, mark, held = together(done, hold(HOLD), weights[3:5])
                weights = own + held + weights[5:]
            elif z == 1:
                done, held = together(done, weights[5:])
                weights = weights[:5] + held
            elif k == 0:
                done, acts[z - 2] = together(done, acts[z - 2])
            else:
                (done,) = together(done)
            if ahead is not None:
                stream.append([done.pop()])
            if inner > 1:
                last[-1] = done.pop()
        if z == outer > 2:
            first = send_z(dxs[1][0])
        *dx, act = rows_grads(xgs[z - 1], dys[z - 1], weights)
        dxs.append(dx)
        acts.append(act)
        if z > 2:
            across.append(send_across(z - 1))
        if len(groups) > 1 and z - 1 == groups[(z - 1) // per][-1]:
            for j in range(2):
                value = partial(j, groups[(z - 1) // per], f32)
                sums[j] = value if z <= per else [t + v for t, v in zip(sums[j], value)]
            if z < outer:
                sums, xgs[z] = together(sums, xgs[z])

    if outer > 1:
        down = [send_down(v) for v in dxs[1][1:]]
    single = len(groups) == 1
    if single:
        other = [send_core(v) for v in partial(1, groups[0], bf16)]
    else:
        other = [send_core(v.astype(bf16)) for v in sums[1]]

    pieces = []
    if outer > 1:
        if outer == 2:
            pieces.append(send_z(dxs[1][0]))
        dxs[0] = [dxs[0][0]] + [add(v, o) for v, o in zip(dxs[0][1:], down)]
    pieces += [dxs[0][0], *send_across(0)]
    if outer > 2:
        total = add(dxs[2][0], first, *across[0])
        for z in range(3, outer):
            total = add(send_z(total), dxs[z][0], *across[z - 2])
        _, other = together(total, other)
        pieces.append(send_z(total))
    if single:
        grad_w = partial(0, groups[0], bf16, other)
    else:
        grad_w = [(v + o.astype(f32)).astype(bf16)[None] for v, o in zip(sums[0], other)]
    pieces, grad_w = together(pieces, grad_w)
    grad_tokens, grad_gates = finish(ids, kept, pieces, mark, width)
    grad_gates = grad_gates.T
    return (grad_tokens, grad_gates, *grad_w)


def solution(mesh):
    both = ("groups", "expert")
    return jax.shard_map(
        on_device,
        mesh=mesh,
        in_specs=(
            P(both, None),
            P(both, None),
            P(both, None),
            P(both, None),
            P("groups"),
            P("expert", None, None),
            P("expert", None, None),
            P("expert", None, None),
        ),
        out_specs=(
            P(both, None),
            P(both, None),
            P(both, None, None),
            P(both, None, None),
            P(both, None, None),
        ),
        check_vma=False,
    )
```

```python
import functools
import math

import jax
import jax.numpy as jnp
from jax import lax
from jax.experimental import pallas as pl
from jax.experimental.pallas import tpu as pltpu
from jax.sharding import PartitionSpec as P

TOP = 8
CORES = 2
LANES = 128
ROW_BLOCK = 256
W_ROWS = 1024
HOLD = 10**10
PLAN_MIB = 60

f32 = jnp.float32
bf16 = jnp.bfloat16
nt = (((1,), (1,)), ((), ()))
tn = (((0,), (0,)), ((), ()))
VMEM = pl.BlockSpec(memory_space=pltpu.VMEM)
ANY = pl.BlockSpec(memory_space=pl.ANY)
HBM = pl.BlockSpec(memory_space=pltpu.HBM)


def params(mib):
    return pltpu.CompilerParams(vmem_limit_bytes=mib * 1024 * 1024)


def row_iota(rows, lanes):
    return lax.broadcasted_iota(jnp.int32, (rows, lanes), 0)


def lane_iota(rows, lanes):
    return lax.broadcasted_iota(jnp.int32, (rows, lanes), 1)


def plan_kernel(home_cap, rep_cap, table_in, ids_in, gates_in, x_in, xg, kept_out, *scratch):
    table, ids, gates, sem = scratch
    tokens, width = x_in.shape
    extra = xg.shape[0] - tokens
    pairs = (
        (table_in, table),
        (ids_in, ids),
        (gates_in, gates),
        (x_in, xg.at[pl.ds(0, tokens)]),
    )
    copies = [pltpu.make_async_copy(src, dst, sem.at[i]) for i, (src, dst) in enumerate(pairs)]
    for c in copies:
        c.start()
    devices = table.shape[1]
    earlier = row_iota(tokens, tokens) < lane_iota(tokens, tokens)
    earlier = jnp.where(earlier, 1.0, 0.0).astype(bf16)
    expert = row_iota(devices, tokens)
    for c in copies[:3]:
        c.wait()
    hosts = jnp.where(table[...] == row_iota(devices, devices), 1.0, 0.0)
    copied = 1.0 + jnp.sum(hosts, axis=1, keepdims=True)
    named = jnp.zeros((devices, tokens), f32)
    weight = jnp.zeros((devices, tokens), f32)
    for k in range(TOP):
        hit = expert == ids[k : k + 1]
        named = jnp.where(hit, 1.0, named)
        weight = jnp.where(hit, gates[k : k + 1].astype(f32), weight)
    rank = jnp.dot(named.astype(bf16), earlier, preferred_element_type=f32)
    turn = rank + lax.axis_index("expert").astype(f32)
    at_home = turn == copied * jnp.floor(turn / copied + 0.5)
    cap = jnp.where(at_home, float(home_cap), float(rep_cap))
    kept = jnp.where((named > 0.0) & (rank < cap * copied), 1.0, 0.0)
    kept_out[...] = kept
    dense = weight * kept
    for k in range(width // tokens):
        part = jnp.zeros((extra, tokens), f32)
        if k * extra < devices:
            part = dense[k * extra : (k + 1) * extra]
        xg[tokens:, k * tokens : (k + 1) * tokens] = part.astype(bf16)
    copies[3].wait()


def plan(table, ids, gates, x, devices, extra):
    tokens, width = x.shape
    home_cap = max(2, 5 * tokens * TOP // (4 * devices))
    rep_cap = max(2, tokens * TOP // (2 * devices))
    return pl.pallas_call(
        functools.partial(plan_kernel, home_cap, rep_cap),
        out_shape=(
            jax.ShapeDtypeStruct((tokens + extra, width), bf16),
            jax.ShapeDtypeStruct((devices, tokens), f32),
        ),
        in_specs=[HBM] * 4,
        out_specs=(VMEM, VMEM),
        scratch_shapes=[
            pltpu.VMEM(table.shape, jnp.int32),
            pltpu.VMEM(ids.shape, jnp.int32),
            pltpu.VMEM(gates.shape, bf16),
            pltpu.SemaphoreType.DMA((4,)),
        ],
        compiler_params=params(PLAN_MIB),
        name="plan",
    )(table, ids, gates, x)


def hold_kernel(out):
    out[...] = jnp.zeros_like(out)


def hold(flops):
    return pl.pallas_call(
        hold_kernel,
        out_shape=jax.ShapeDtypeStruct((8, LANES), f32),
        out_specs=VMEM,
        compiler_params=params(1),
        cost_estimate=pl.CostEstimate(flops=flops, bytes_accessed=1000, transcendentals=0),
        name="hold",
    )()


def rows_kernel(slots, *refs):
    xg, dy = refs[:slots], refs[slots : 2 * slots]
    weights = refs[2 * slots : 2 * slots + 6]
    dxg, act = refs[2 * slots + 6 : 3 * slots + 6], refs[3 * slots + 6]
    tokens, width = dy[0].shape
    hidden = weights[2].shape[0]
    extra = xg[0].shape[0] - tokens
    per = max(1, ROW_BLOCK // tokens)
    me = lax.axis_index("expert")

    def stack(parts):
        return parts[0] if len(parts) == 1 else jnp.concatenate(parts, axis=0)

    def unpack(ref):
        total = jnp.zeros((extra, tokens), f32)
        for c in range(width // tokens):
            part = ref[tokens:, c * tokens : (c + 1) * tokens].astype(f32)
            total = jnp.where(me // extra == c, part, total)
        return total.T

    for at in range(0, slots, per):
        group = range(at, min(slots, at + per))
        x = stack([xg[i][:tokens] for i in group])
        up_grad = stack([dy[i][...] for i in group])
        rows = len(group) * tokens
        here = pl.ds(at * tokens, rows)
        gates = stack([unpack(xg[i]) for i in group])
        lane = lane_iota(rows, LANES)
        dx, gg = 0.0, 0.0
        for j in range(2):
            w_gate, w_up, w_down = weights[3 * j : 3 * j + 3]
            a = jnp.dot(x, w_gate[...], preferred_element_type=f32)
            b = jnp.dot(x, w_up[...], preferred_element_type=f32)
            back = lax.dot_general(up_grad, w_down[...], nt, preferred_element_type=f32)
            column = (me if j == 0 else me ^ 1) % extra
            gate = jnp.sum(
                jnp.where(lane_iota(rows, extra) == column, gates, 0.0), axis=1, keepdims=True
            )
            sig = jax.nn.sigmoid(a)
            silu = a * sig
            h = silu * b
            dots = jnp.sum(h.astype(bf16).astype(f32) * back, axis=1, keepdims=True)
            scaled = gate * back
            da = (scaled * b * sig * (1.0 + a * (1.0 - sig))).astype(bf16)
            db = (scaled * silu).astype(bf16)
            first = j * 3 * hidden
            act[here, first : first + hidden] = da
            act[here, first + hidden : first + 2 * hidden] = db
            act[here, first + 2 * hidden : first + 3 * hidden] = (gate * h).astype(bf16)
            dx += lax.dot_general(da, w_gate[...], nt, preferred_element_type=f32)
            dx += lax.dot_general(db, w_up[...], nt, preferred_element_type=f32)
            gg += jnp.where(lane == column, dots, 0.0)
        for k, i in enumerate(group):
            part = slice(k * tokens, (k + 1) * tokens)
            dxg[i][:tokens] = dx[part].astype(bf16)
            packed = gg[part].T[:extra]
            for c in range(width // tokens):
                dxg[i][tokens:, c * tokens : (c + 1) * tokens] = jnp.where(
                    me // extra == c, packed, 0.0
                ).astype(bf16)


def rows_grads(xgs, dys, weights):
    slots = len(dys)
    tokens, width = dys[0].shape
    full = xgs[0].shape[0]
    hidden = weights[2].shape[0]
    rows = slots * tokens
    flops = 1 * rows * 2 * 5 * width * hidden
    moved = 12 * rows * width + 12 * width * hidden + 12 * rows * hidden
    return pl.pallas_call(
        functools.partial(rows_kernel, slots),
        out_shape=tuple(jax.ShapeDtypeStruct((full, width), bf16) for _ in dys)
        + (jax.ShapeDtypeStruct((rows, 6 * hidden), bf16),),
        in_specs=[VMEM] * (2 * slots + 6),
        out_specs=(VMEM,) * (slots + 1),
        compiler_params=params(20),
        cost_estimate=pl.CostEstimate(
            flops=flops, bytes_accessed=moved, transcendentals=2 * rows * hidden
        ),
        name="rows_grads",
    )(*xgs, *dys, *weights)


def weights_kernel(j, slots, steps, extra, *refs):
    xg_in, dy_in, act_in = refs[:slots], refs[slots : 2 * slots], refs[2 * slots : 2 * slots + steps]
    refs = refs[2 * slots + steps :]
    more, refs = refs[:extra], refs[extra:]
    gate_out, up_out, down_out = refs[:3]
    x, dy, act, sem = refs[3:]
    tokens, width = dy_in[0].shape
    hidden = act.shape[1] // 3
    step_rows = act_in[0].shape[0]
    copies = []

    def fetch(src, dst):
        copies.append(pltpu.make_async_copy(src, dst, sem.at[len(copies)]))
        copies[-1].start()

    for i in range(steps):
        fetch(
            act_in[i].at[:, pl.ds(j * 3 * hidden, 3 * hidden)],
            act.at[pl.ds(i * step_rows, step_rows)],
        )
    for i in range(slots):
        fetch(xg_in[i].at[pl.ds(0, tokens)], x.at[pl.ds(i * tokens, tokens)])
    for i in range(slots):
        fetch(dy_in[i], dy.at[pl.ds(i * tokens, tokens)])
    for c in copies[: steps + slots]:
        c.wait()

    def put(out, here, value, k):
        if extra:
            value = value + more[k][here].astype(f32)
        if len(out.shape) == 3:
            out[0, here[0], here[1]] = value.astype(out.dtype)
        else:
            out[here[0], here[1]] = value.astype(out.dtype)

    part = math.gcd(width, 256)
    everything = slice(None)
    for m in range(0, width, part):
        here = (slice(m, m + part), everything)
        both = lax.dot_general(
            x[:, m : m + part], act[:, : 2 * hidden], tn, preferred_element_type=f32
        )
        put(gate_out, here, both[:, :hidden], 0)
        put(up_out, here, both[:, hidden:], 1)
    for c in copies[steps + slots :]:
        c.wait()
    part = math.gcd(hidden, 128)
    for m in range(0, hidden, part):
        here = (slice(m, m + part), everything)
        value = lax.dot_general(
            act[:, 2 * hidden + m : 2 * hidden + m + part], dy[...], tn, preferred_element_type=f32
        )
        put(down_out, here, value, 2)


def weights_grads(j, xgs, dys, acts, dtype, more=()):
    slots, steps = len(dys), len(acts)
    tokens, width = dys[0].shape
    hidden = acts[0].shape[1] // 6
    rows = slots * tokens
    lead = (1,) if more else ()
    return pl.pallas_call(
        functools.partial(weights_kernel, j, slots, steps, len(more)),
        out_shape=(
            jax.ShapeDtypeStruct(lead + (width, hidden), dtype),
            jax.ShapeDtypeStruct(lead + (width, hidden), dtype),
            jax.ShapeDtypeStruct(lead + (hidden, width), dtype),
        ),
        in_specs=[ANY] * (2 * slots + steps) + [VMEM] * len(more),
        out_specs=(VMEM,) * 3,
        scratch_shapes=[
            pltpu.VMEM((rows, width), bf16),
            pltpu.VMEM((rows, width), bf16),
            pltpu.VMEM((rows, 3 * hidden), bf16),
            pltpu.SemaphoreType.DMA((2 * slots + steps,)),
        ],
        compiler_params=params(20),
        cost_estimate=pl.CostEstimate(
            flops=1000,
            bytes_accessed=1000,
            transcendentals=0,
        ),
        name="weights_grads",
    )(*xgs, *dys, *acts, *more)


def finish_kernel(parts, ids, kept, *refs):
    pieces, (_, tokens_out, gates_out) = refs[:parts], refs[parts:]
    tokens, width = tokens_out.shape
    total = pieces[0][...].astype(f32)
    for p in pieces[1:]:
        total = total + p[...].astype(f32)
    tokens_out[...] = total[:tokens].astype(bf16)
    devices = kept.shape[0]
    extra = pieces[0].shape[0] - tokens
    gg = [total[tokens:, k * tokens : (k + 1) * tokens] for k in range(devices // extra)]
    gg = jnp.concatenate(gg, axis=0) * kept[...]
    expert = row_iota(devices, tokens)
    place = row_iota(TOP, tokens)
    out = jnp.zeros((TOP, tokens), f32)
    for k in range(TOP):
        value = jnp.sum(jnp.where(expert == ids[k : k + 1], gg, 0.0), axis=0, keepdims=True)
        out = jnp.where(place == k, value, out)
    gates_out[...] = out.astype(bf16)


def finish(ids, kept, pieces, mark, width):
    tokens = ids.shape[1]
    return pl.pallas_call(
        functools.partial(finish_kernel, len(pieces)),
        out_shape=(
            jax.ShapeDtypeStruct((tokens, width), bf16),
            jax.ShapeDtypeStruct((TOP, tokens), bf16),
        ),
        in_specs=[VMEM] * (2 + len(pieces)) + [ANY],
        out_specs=(VMEM, VMEM),
        compiler_params=params(16),
        name="finish",
    )(ids, kept, *pieces, mark)


def add(*terms):
    total = terms[0].astype(f32)
    for t in terms[1:]:
        total = total + t.astype(f32)
    return total.astype(bf16)


def on_device(tokens_in, grad_out, gates, expert_ids, replica_table, w_gate, w_up, w_down):
    devices = lax.axis_size("expert")
    tokens, width = tokens_in.shape
    extra = 8 * -(-devices * tokens // (8 * width))
    chips = devices // CORES
    inner = 2 ** (int(math.log2(chips)) // 2)
    outer = chips // inner

    def moved(i, dz, dy):
        core, chip = i % CORES, i // CORES
        z, y = chip // inner, chip % inner
        return (((z + dz) % outer) * inner + (y + dy) % inner) * CORES + core

    def send_z(v):
        return lax.ppermute(v, "expert", [(i, moved(i, 1, 0)) for i in range(devices)])

    def send_down(v):
        return lax.ppermute(v, "expert", [(i, moved(i, -1, 0)) for i in range(devices)])

    def send_y(v):
        return lax.ppermute(v, "expert", [(i, moved(i, 0, 1)) for i in range(devices)])

    def send_core(v):
        return lax.ppermute(v, "expert", [(i, i ^ 1) for i in range(devices)])

    def together(*values):
        return lax.optimization_barrier(values)

    ids = expert_ids.T
    xg, kept = plan(replica_table[None], ids, gates.T, tokens_in, devices, extra)
    own = (w_gate[0], w_up[0], w_down[0])
    weights = own + tuple(send_core(w) for w in own)

    per = max(1, W_ROWS // (inner * tokens))
    groups = [range(z, min(outer, z + per)) for z in range(0, outer, per)]
    sums = [None, None]

    def partial(j, group, dtype, more=()):
        return weights_grads(
            j,
            [x for z in group for x in xgs[z]],
            [d for z in group for d in dys[z]],
            [acts[z] for z in group],
            dtype,
            more,
        )

    xgs, dys, mark = [[xg]], [[grad_out]], kept
    dxs, acts, across = [], [], []

    def send_across(z):
        if inner == 1:
            return []
        total = dxs[z][1]
        for y in range(2, inner):
            total = add(send_y(total), dxs[z][y])
        return [send_y(total)]

    for z in range(1, outer + 1):
        for k, stream in enumerate((xgs, dys)):
            last = stream[z - 1]
            ahead = None
            if z < outer:
                ahead = send_z(last[0])
            for y in range(1, inner):
                if k == 0 and z == outer > 1 and y == inner - 1:
                    last.append(send_z(stream[z - 2][y]))
                else:
                    last.append(send_y(last[y - 1]))
            done = [last[-1]] if inner > 1 else []
            if ahead is not None:
                done.append(ahead)
            if k == 0 and z == 1:
                done, mark, held = together(done, hold(HOLD), weights[3:5])
                weights = own + held + weights[5:]
            elif z == 1:
                done, held = together(done, weights[5:])
                weights = weights[:5] + held
            elif k == 0:
                done, acts[z - 2] = together(done, acts[z - 2])
            else:
                (done,) = together(done)
            if ahead is not None:
                stream.append([done.pop()])
            if inner > 1:
                last[-1] = done.pop()
        if z == outer > 2:
            first, xgs[z - 1] = together(send_z(dxs[1][0]), xgs[z - 1])
        *dx, act = rows_grads(xgs[z - 1], dys[z - 1], weights)
        dxs.append(dx)
        acts.append(act)
        if z > 2:
            across.append(send_across(z - 1))
        if len(groups) > 1 and z - 1 == groups[(z - 1) // per][-1]:
            for j in range(2):
                value = partial(j, groups[(z - 1) // per], f32)
                sums[j] = value if z <= per else [t + v for t, v in zip(sums[j], value)]
            if z < outer:
                sums, xgs[z] = together(sums, xgs[z])

    if outer > 1:
        down = [send_down(v) for v in dxs[1][1:]]
    single = len(groups) == 1
    if single:
        other = [send_core(v) for v in partial(1, groups[0], bf16)]
    else:
        other = [send_core(v.astype(bf16)) for v in sums[1]]

    pieces = []
    if outer > 1:
        if outer == 2:
            pieces.append(send_z(dxs[1][0]))
        dxs[0] = [dxs[0][0]] + [add(v, o) for v, o in zip(dxs[0][1:], down)]
    pieces += [dxs[0][0], *send_across(0)]
    if outer > 2:
        total = add(dxs[2][0], first, *across[0])
        for z in range(3, outer):
            total = add(send_z(total), dxs[z][0], *across[z - 2])
        _, other = together(total, other)
        pieces.append(send_z(total))
    if single:
        grad_w = partial(0, groups[0], bf16, other)
    else:
        grad_w = [(v + o.astype(f32)).astype(bf16)[None] for v, o in zip(sums[0], other)]
    pieces, grad_w = together(pieces, grad_w)
    grad_tokens, grad_gates = finish(ids, kept, pieces, mark, width)
    grad_gates = grad_gates.T
    return (grad_tokens, grad_gates, *grad_w)


def solution(mesh):
    both = ("groups", "expert")
    return jax.shard_map(
        on_device,
        mesh=mesh,
        in_specs=(
            P(both, None),
            P(both, None),
            P(both, None),
            P(both, None),
            P("groups"),
            P("expert", None, None),
            P("expert", None, None),
            P("expert", None, None),
        ),
        out_specs=(
            P(both, None),
            P(both, None),
            P(both, None, None),
            P(both, None, None),
            P(both, None, None),
        ),
        check_vma=False,
    )
```
